128 devices in a mesh: seg: 32 (over z, x_lo, y), sp: 4 (over x_hi, core).
Axes of the slice: x: 4 (x_hi: 2, x_lo: 2; x = x_hi * 2 + x_lo), y: 4, z: 4, core: 2. Of those that a mesh axis runs over, the one named last changes fastest.
Arguments:
- normed: bfloat16 [1024, 131072], P('sp', 'seg'), may hold values from -128 to 128, as said below
- w_qkv: bfloat16 [3, 2048, 2048], P(None, None, 'sp'), may hold values from -0.125 to 0.125
- w_out: bfloat16 [2048, 2048], P('sp'), may hold values from -0.125 to 0.125
Outputs:
- attention_out: bfloat16 [1024, 131072], P('sp', 'seg')
The draws below stay inside these ranges and needn't reach their ends.
Inputs may be any that keep to these rules, and one draw needn't show every extreme that they name: `normed`: activations of the layer after its normalization.
All inputs are finite; a program needn't handle non-finite values.
Results may differ from the reference program's by a relative error of at most 0.025.
The reference program's roundings to bfloat16 on the way count: a program that leaves them out, or rounds other values in their place, can miss the bound.
Values may be sent and summed in bfloat16 or wider, within the bound.
No kernel may reach another device: no remote copies, remote signals or barrier semaphores. Data moves between devices by JAX's collectives and lax.ppermute only.
A program may use at most 128 MiB of HBM per device.

```python
import math
import jax
import jax.numpy as jnp
from jax import lax

D = 2048
HEADS = 16
HEAD_DIM = 128
OFFSETS = 1024
SEGMENTS = 64


def draw_normed(key, part):
    key = jax.random.fold_in(key, 7)
    key_base, key_row = jax.random.split(key, 2)
    base = jnp.clip(jax.random.normal(key_base, (OFFSETS, SEGMENTS, D), jnp.float32), -6.0, 6.0)
    row_scale = jnp.exp(jax.random.uniform(key_row, (OFFSETS, SEGMENTS, 1), jnp.float32, math.log(0.4), math.log(1.6)))
    values = row_scale * base
    return values.reshape(OFFSETS, SEGMENTS * D).astype(jnp.bfloat16)


def level_of(own_key, extent, pieces, low, top_value):
    def one(dim, parts):
        steps = jax.random.uniform(jax.random.fold_in(jax.random.fold_in(own_key, 6), dim), (parts,), jnp.float32, low / len(pieces), top_value / len(pieces))
        return jnp.repeat(jnp.exp(steps), extent[dim] // parts).reshape((-1,) + (1,) * (len(extent) - dim - 1))

    loudness = one(*pieces[0])
    for cut in pieces[1:]:
        loudness = loudness * one(*cut)
    return loudness


def normal_values(key, shape, spread, bound, shards=(), kind=jnp.bfloat16):
    entries = spread * jax.random.normal(key, shape, jnp.float32)
    if shards:
        entries = entries * level_of(key, shape, shards, -0.22, 0.18)
    return jnp.clip(entries, -bound, bound).astype(kind)


def setup_inputs(seed: int = 0) -> dict:
    key_of = jax.random.split(jax.random.key(seed), 4)
    normed = draw_normed(jax.random.fold_in(key_of[3], 71), 0)
    w_qkv = normal_values(key_of[1], (3, D, D), D ** -0.5, 0.125, ((2, 4),))
    w_out = normal_values(key_of[2], (D, D), D ** -0.5, 0.125, ((0, 4),))
    return {"normed": normed, "w_qkv": w_qkv, "w_out": w_out}


def head_attention(trio):
    query_one = trio[0].astype(jnp.float32)
    key_one = trio[1].astype(jnp.float32)
    value_one = trio[2].astype(jnp.float32)
    offset_count = query_one.shape[0]
    segment_count = query_one.shape[1]
    score_scale = HEAD_DIM ** -0.5
    row_scores = jnp.einsum('tsd,usd->stu', query_one, key_one) * score_scale
    column_scores = jnp.einsum('tsd,trd->tsr', query_one, key_one) * score_scale
    row_allowed = (lax.broadcasted_iota(jnp.int32, (offset_count, offset_count), 1)
                   <= lax.broadcasted_iota(jnp.int32, (offset_count, offset_count), 0))[None]
    column_allowed = (lax.broadcasted_iota(jnp.int32, (segment_count, segment_count), 1)
                      < lax.broadcasted_iota(jnp.int32, (segment_count, segment_count), 0))[None]
    row_max = jnp.max(jnp.where(row_allowed, row_scores, -1e30), axis=-1)
    column_max = jnp.max(jnp.where(column_allowed, column_scores, -1e30), axis=-1)
    joint_max = jnp.maximum(row_max.T, column_max)
    row_weights = jnp.where(row_allowed, jnp.exp(jnp.minimum(row_scores - joint_max.T[:, :, None], 0.0)), 0.0)
    column_weights = jnp.where(column_allowed, jnp.exp(jnp.minimum(column_scores - joint_max[:, :, None], 0.0)), 0.0)
    denominator = jnp.sum(row_weights, axis=-1).T + jnp.sum(column_weights, axis=-1)
    row_rounded = lax.optimization_barrier(row_weights.astype(jnp.bfloat16)).astype(jnp.float32)
    column_rounded = lax.optimization_barrier(column_weights.astype(jnp.bfloat16)).astype(jnp.float32)
    numerator = jnp.einsum('stu,usd->tsd', row_rounded, value_one) + jnp.einsum('tsr,trd->tsd', column_rounded, value_one)
    return (numerator / denominator[:, :, None]).astype(jnp.bfloat16)


def reference(normed, w_qkv, w_out):
    tokens = normed.reshape(OFFSETS * SEGMENTS, D)
    stacked = []
    for member in range(3):
        projected = jnp.dot(tokens, w_qkv[member], preferred_element_type=jnp.float32).astype(jnp.bfloat16)
        stacked.append(jnp.moveaxis(projected.reshape(OFFSETS, SEGMENTS, HEADS, HEAD_DIM), 2, 0))
    attended = lax.map(head_attention, (stacked[0], stacked[1], stacked[2]))
    attended = jnp.moveaxis(attended, 0, 2).reshape(OFFSETS * SEGMENTS, D)
    mixed_out = jnp.dot(attended, w_out, preferred_element_type=jnp.float32).astype(jnp.bfloat16)
    return mixed_out.reshape(OFFSETS, SEGMENTS * D)
```

```python
import functools

import jax
import jax.numpy as jnp
from jax import lax
from jax.experimental import pallas as pl
from jax.experimental.pallas import tpu as pltpu
from jax.sharding import PartitionSpec as P

HEAD_DIM = 128
EXP_SCALE = HEAD_DIM ** (-0.5) * 1.4426950408889634
MASKED = -1e30
NZ, NXL, NY = 4, 2, 4
BF16, F32 = jnp.bfloat16, jnp.float32
VMEM_LIMIT = 52 * 1024 * 1024

CORE_PAIRS = [(0, 1), (1, 0), (2, 3), (3, 2)]
LOWER_TO_UPPER = [(0, 2), (1, 3)]


def seg_index(z, xl, y):
    return (z * NXL + xl) * NY + y


NEIGHBOUR_PAIRS = [
    (seg_index(z, xl, y) * 4 + xh * 2 + c, seg_index(z, 1 - xl, y) * 4 + (1 - xh) * 2 + c)
    for z in range(NZ)
    for xl in range(NXL)
    for y in range(NY)
    for xh in range(2)
    for c in range(2)
]
PLANES = [[seg_index(z, xl, y) for z in range(NZ) for y in range(NY)] for xl in range(NXL)]


def dot(a, b):
    return jnp.dot(a, b, preferred_element_type=F32)


def dot_t(a, b):
    return lax.dot_general(a, b, (((1,), (1,)), ((), ())), preferred_element_type=F32)


def split3(v):
    hi = v.astype(BF16).astype(F32)
    rest = v - hi
    mid = rest.astype(BF16).astype(F32)
    return hi, mid, (rest - mid).astype(BF16).astype(F32)


def col_kernel(x0, x1, w, out, xs, ws, qkv, bias, sem):
    copies_x = [pltpu.make_async_copy(r, xs.at[pl.ds(b * 512, 512)], sem.at[b]) for b, r in enumerate((x0, x1))]
    copies_w = [pltpu.make_async_copy(w.at[j], ws.at[j], sem.at[2 + j]) for j in range(3)]
    copies_x[0].start()
    copies_w[0].start()
    copies_x[1].start()
    copies_w[1].start()
    copies_w[2].start()
    rows = lax.broadcasted_iota(jnp.int32, (512, 512), 0)
    cols = lax.broadcasted_iota(jnp.int32, (512, 512), 1)
    allowed = ((rows & 7) == (cols & 7)) & ((cols >> 3) < (rows >> 3))
    bias[...] = jnp.where(allowed, 0.0, MASKED)
    for j in range(3):
        copies_w[j].wait()
        for b in range(2):
            if j == 0:
                copies_x[b].wait()
            qkv[j, b * 512:(b + 1) * 512, :] = dot(xs[b * 512:(b + 1) * 512, :], ws[j]).astype(BF16)
    lane = lax.broadcasted_iota(jnp.int32, (128, 128), 1)
    for b in range(2):
        for blk in range(4):
            n = (blk + 1) * 128
            q_rows = slice(b * 512 + blk * 128, b * 512 + (blk + 1) * 128)
            k_rows = slice(b * 512, b * 512 + n)
            stats = jnp.zeros((128, 128), F32)
            for h in range(4):
                f = slice(h * 128, (h + 1) * 128)
                s = dot_t(qkv[0, q_rows, f], qkv[1, k_rows, f]) + bias[blk * 128:(blk + 1) * 128, :n]
                top = jnp.max(s, axis=-1, keepdims=True)
                p = jnp.exp2((s - top) * EXP_SCALE)
                total = jnp.sum(p, axis=-1, keepdims=True)
                num = dot(p.astype(BF16), qkv[2, k_rows, f])
                out[blk * 8:(blk + 1) * 8, b, :, f] = num.astype(BF16).reshape(8, 16, 128)
                for i, v in enumerate(split3(top) + split3(total)):
                    stats = jnp.where(lane == h * 8 + i, v, stats)
            out[blk * 8:(blk + 1) * 8, b, :, 512:640] = stats.astype(BF16).reshape(8, 16, 128)


def column_part(x_own, x_oth, w):
    any_spec = pl.BlockSpec(memory_space=pl.ANY)
    return pl.pallas_call(
        col_kernel,
        out_shape=jax.ShapeDtypeStruct((32, 2, 16, 640), BF16),
        in_specs=[any_spec] * 3,
        out_specs=pl.BlockSpec(memory_space=pltpu.VMEM),
        scratch_shapes=[
            pltpu.VMEM((1024, 2048), BF16),
            pltpu.VMEM((3, 2048, 512), BF16),
            pltpu.VMEM((3, 1024, 512), BF16),
            pltpu.VMEM((512, 512), F32),
            pltpu.SemaphoreType.DMA((5,)),
        ],
        compiler_params=pltpu.CompilerParams(vmem_limit_bytes=VMEM_LIMIT),
        name="column_part",
    )(x_own, x_oth, w)


def row_kernel(where, own, oth, low_own, low_oth, w, num, stats, xs, ws, qs, ks, vs, sem):
    upper, core = where[0], where[1]
    own_row = pl.multiple_of(core * 256, 256)
    oth_row = pl.multiple_of((1 - core) * 256, 256)

    def piece(src, s, row, i):
        return pltpu.make_async_copy(
            src.at[:, pl.ds(s * 2048, 2048)], xs.at[s, pl.ds(row, 256), :], sem.at[i]
        )

    near = [[piece(own, s, 512 + own_row, 2 * s), piece(oth, s, 512 + oth_row, 2 * s + 1)] for s in range(2)]
    far = [[piece(low_own, s, own_row, 4 + 2 * s), piece(low_oth, s, oth_row, 5 + 2 * s)] for s in range(2)]
    weights = [pltpu.make_async_copy(w.at[j], ws.at[j], sem.at[8 + j]) for j in range(3)]
    for c in near[0]:
        c.start()
    weights[0].start()
    for c in near[1]:
        c.start()
    weights[1].start()
    weights[2].start()

    @pl.when(upper == 1)
    def _():
        for s in range(2):
            for c in far[s]:
                c.start()

    def project(j, s, row, dst, dst_row):
        res = dot(xs[s, row:row + 512, :], ws[j]).astype(BF16)
        for h in range(4):
            dst[s * 4 + h, dst_row:dst_row + 512, :] = res[:, h * 128:(h + 1) * 128]

    for j, (dst, dst_row) in enumerate(((qs, 0), (ks, 512), (vs, 512))):
        weights[j].wait()
        for s in range(2):
            if j == 0:
                for c in near[s]:
                    c.wait()
            project(j, s, 512, dst, dst_row)

    @pl.when(upper == 1)
    def _():
        for s in range(2):
            for c in far[s]:
                c.wait()
            project(1, s, 0, ks, 0)
            project(2, s, 0, vs, 0)

    later = lax.broadcasted_iota(jnp.int32, (256, 256), 1) > lax.broadcasted_iota(jnp.int32, (256, 256), 0)
    lane = lax.broadcasted_iota(jnp.int32, (256, 128), 1)

    def attend(first):
        for s in range(2):
            for blk in range(2):
                tile = core if blk == 0 else 1 - core
                st = jnp.zeros((256, 128), F32)
                for h in range(4):
                    i = s * 4 + h
                    q = qs[i, blk * 256:(blk + 1) * 256, :]
                    diag = 512 + blk * 256
                    sd = jnp.where(later, MASKED, dot_t(q, ks[i, diag:diag + 256, :]))
                    top = jnp.max(sd, axis=-1, keepdims=True)
                    if diag > first:
                        se = dot_t(q, ks[i, first:diag, :])
                        top = jnp.maximum(top, jnp.max(se, axis=-1, keepdims=True))
                    pd = jnp.exp2((sd - top) * EXP_SCALE)
                    total = jnp.sum(pd, axis=-1, keepdims=True)
                    acc = dot(pd.astype(BF16), vs[i, diag:diag + 256, :])
                    if diag > first:
                        pe = jnp.exp2((se - top) * EXP_SCALE)
                        total += jnp.sum(pe, axis=-1, keepdims=True)
                        acc += dot(pe.astype(BF16), vs[i, first:diag, :])
                    num[tile, s, :, h * 128:(h + 1) * 128] = acc
                    st = jnp.where(lane == 2 * h, top, st)
                    st = jnp.where(lane == 2 * h + 1, total, st)
                stats[tile, s, :, :] = st

    @pl.when(upper == 0)
    def _():
        attend(512)

    @pl.when(upper == 1)
    def _():
        attend(0)


def row_part(where, own, oth, low_own, low_oth, w):
    any_spec = pl.BlockSpec(memory_space=pl.ANY)
    vmem = pl.BlockSpec(memory_space=pltpu.VMEM)
    return pl.pallas_call(
        row_kernel,
        out_shape=(
            jax.ShapeDtypeStruct((2, 2, 256, 512), F32),
            jax.ShapeDtypeStruct((2, 2, 256, 128), F32),
        ),
        in_specs=[pl.BlockSpec(memory_space=pltpu.SMEM)] + [any_spec] * 5,
        out_specs=(vmem, vmem),
        scratch_shapes=[
            pltpu.VMEM((2, 1024, 2048), BF16),
            pltpu.VMEM((3, 2048, 512), BF16),
            pltpu.VMEM((8, 512, 128), BF16),
            pltpu.VMEM((8, 1024, 128), BF16),
            pltpu.VMEM((8, 1024, 128), BF16),
            pltpu.SemaphoreType.DMA((11,)),
        ],
        compiler_params=pltpu.CompilerParams(vmem_limit_bytes=VMEM_LIMIT),
        name="row_part",
    )(where, own, oth, low_own, low_oth, w)


def merge_kernel(num, stats, col, own, oth):
    for tile, out in enumerate((own, oth)):
        both = col[:, tile, :, 512:640].astype(F32)
        for s in range(2):
            st = stats[tile, s, :, :]
            cst = both[:, s * 8:(s + 1) * 8, :].reshape(256, 128)
            for h in range(4):
                f = slice(h * 128, (h + 1) * 128)
                row_top, row_total = st[:, 2 * h:2 * h + 1], st[:, 2 * h + 1:2 * h + 2]
                v = [cst[:, h * 8 + i:h * 8 + i + 1] for i in range(6)]
                col_top = (v[0] + v[1]) + v[2]
                col_total = (v[3] + v[4]) + v[5]
                top = jnp.maximum(row_top, col_top)
                row_factor = jnp.exp2((row_top - top) * EXP_SCALE)
                col_factor = jnp.exp2((col_top - top) * EXP_SCALE)
                total = row_total * row_factor + col_total * col_factor
                cnum = col[:, tile, :, f].astype(F32)[:, s * 8:(s + 1) * 8, :].reshape(256, 128)
                value = (num[tile, s, :, f] * row_factor + cnum * col_factor) / total
                out[s, :, f] = value.astype(BF16)


def merge(num, stats, col):
    vmem = pl.BlockSpec(memory_space=pltpu.VMEM)
    shape = jax.ShapeDtypeStruct((2, 256, 512), BF16)
    return pl.pallas_call(
        merge_kernel,
        out_shape=(shape, shape),
        in_specs=[vmem] * 3,
        out_specs=(vmem, vmem),
        compiler_params=pltpu.CompilerParams(vmem_limit_bytes=VMEM_LIMIT),
        name="merge",
    )(num, stats, col)


def out_kernel(a0, a1, a2, a3, w0, w1, w2, w3, out, ws, sem):
    copies = [pltpu.make_async_copy(w, ws.at[i], sem.at[i]) for i, w in enumerate((w0, w1, w2, w3))]
    for c in copies:
        c.start()
    for c in copies:
        c.wait()
    for s in range(2):
        acc = dot(a0[s], ws[0])
        for i, a in ((1, a1), (2, a2), (3, a3)):
            acc += dot(a[s], ws[i])
        out[:, s * 2048:(s + 1) * 2048] = acc.astype(BF16)


def output_part(attended, weights):
    any_spec = pl.BlockSpec(memory_space=pl.ANY)
    vmem = pl.BlockSpec(memory_space=pltpu.VMEM)
    return pl.pallas_call(
        out_kernel,
        out_shape=jax.ShapeDtypeStruct((256, 4096), BF16),
        in_specs=[vmem] * 4 + [any_spec] * 4,
        out_specs=vmem,
        scratch_shapes=[pltpu.VMEM((4, 512, 2048), BF16), pltpu.SemaphoreType.DMA((4,))],
        compiler_params=pltpu.CompilerParams(vmem_limit_bytes=VMEM_LIMIT),
        name="output_part",
    )(*attended, *weights)


def core_swap(a):
    return lax.ppermute(a, "sp", CORE_PAIRS)


def to_segments(a):
    return lax.all_to_all(a, "seg", split_axis=0, concat_axis=0, tiled=True)


def other_weights(w_qkv, w_out, seg):
    chip = (seg // (NXL * NY)) * NY + seg % NY
    qkv_chunk = lax.dynamic_slice(w_qkv, (0, chip * 128, 0), (3, 128, 512))
    out_chunk = lax.dynamic_slice(w_out, (chip * 32, 0), (32, 2048))
    qkv_chunk = lax.ppermute(qkv_chunk, ("seg", "sp"), NEIGHBOUR_PAIRS)
    out_chunk = lax.ppermute(out_chunk, ("seg", "sp"), NEIGHBOUR_PAIRS)
    qkv_other = lax.all_gather(qkv_chunk, "seg", axis=1, tiled=True, axis_index_groups=PLANES)
    out_other = lax.all_gather(out_chunk, "seg", axis=0, tiled=True, axis_index_groups=PLANES)
    return qkv_other, out_other


def shards(normed, w_qkv, w_out):
    seg, sp = lax.axis_index("seg"), lax.axis_index("sp")
    where = jnp.stack([sp // 2, sp % 2]).astype(jnp.int32)
    qkv_other, out_other = other_weights(w_qkv, w_out, seg)
    by_offset = normed.reshape(32, 8, 2, 2048).transpose(0, 2, 1, 3).reshape(32, 16, 2048)
    col_own = to_segments(by_offset).reshape(512, 2048)
    col_oth = core_swap(col_own)
    row_oth = core_swap(normed)
    low_own = lax.ppermute(normed, "sp", LOWER_TO_UPPER)
    low_oth = core_swap(low_own)
    out_weights = (w_out, out_other, core_swap(w_out), core_swap(out_other))
    own_parts, sent_parts = [], []
    for w in (w_qkv, qkv_other):
        col = to_segments(column_part(col_own, col_oth, w).reshape(32, 32, 640)).reshape(32, 2, 16, 640)
        num, stats = row_part(where, normed, row_oth, low_own, low_oth, w)
        own, oth = merge(num, stats, col)
        own_parts.append(own)
        sent_parts.append(core_swap(oth))
    return output_part(own_parts + sent_parts, out_weights)


def solution(mesh):
    in_specs = (P("sp", "seg"), P(None, None, "sp"), P("sp", None))
    return jax.shard_map(shards, mesh=mesh, in_specs=in_specs, out_specs=P("sp", "seg"), check_vma=False)
```

```python
import functools

import jax
import jax.numpy as jnp
from jax import lax
from jax.experimental import pallas as pl
from jax.experimental.pallas import tpu as pltpu
from jax.sharding import PartitionSpec as P

HEAD_DIM = 128
EXP_SCALE = HEAD_DIM ** (-0.5) * 1.4426950408889634
MASKED = -1e30
NZ, NXL, NY = 4, 2, 4
BF16, F32 = jnp.bfloat16, jnp.float32
VMEM_LIMIT = 58 * 1024 * 1024

CORE_PAIRS = [(0, 1), (1, 0), (2, 3), (3, 2)]
LOWER_TO_UPPER = [(0, 2), (1, 3)]


def seg_index(z, xl, y):
    return (z * NXL + xl) * NY + y


NEIGHBOUR_PAIRS = [
    (seg_index(z, xl, y) * 4 + xh * 2 + c, seg_index(z, 1 - xl, y) * 4 + (1 - xh) * 2 + c)
    for z in range(NZ)
    for xl in range(NXL)
    for y in range(NY)
    for xh in range(2)
    for c in range(2)
]
PLANES = [[seg_index(z, xl, y) for z in range(NZ) for y in range(NY)] for xl in range(NXL)]


ANY_SPEC = pl.BlockSpec(memory_space=pl.ANY)
HBM_SPEC = pl.BlockSpec(memory_space=pltpu.HBM)
SMEM_SPEC = pl.BlockSpec(memory_space=pltpu.SMEM)
VMEM_SPEC = pl.BlockSpec(memory_space=pltpu.VMEM)


def cost(us):
    return pl.CostEstimate(flops=int(us * 1e9), transcendentals=0, bytes_accessed=int(us * 1e6))


def dot(a, b):
    return jnp.dot(a, b, preferred_element_type=F32)


def dot_t(a, b):
    return lax.dot_general(a, b, (((1,), (1,)), ((), ())), preferred_element_type=F32)


def split3(v):
    hi = v.astype(BF16).astype(F32)
    rest = v - hi
    mid = rest.astype(BF16).astype(F32)
    return hi, mid, (rest - mid).astype(BF16).astype(F32)


def weight_copies(w, ws, sem):
    return [[pltpu.make_async_copy(w[0].at[j], ws.at[j], sem.at[j])] for j in range(3)]


def wait_all(copies):
    for c in copies:
        c.wait()


def col_kernel(nw, where, x0, *refs):
    x1, w, refs = refs[:4], refs[4:4 + nw], refs[4 + nw:]
    side, (out, side_out, xs, ws, wide, qs, ks, vs, res, pack, held, sem) = refs[0], refs[-12:]
    back = []
    copies_x = [
        [[pltpu.make_async_copy(x0.at[pl.ds(m, 256)], xs.at[pl.ds(m, 256)], sem.at[3 + m // 256])] for m in (0, 256)],
        [[pltpu.make_async_copy(x1[i], xs.at[pl.ds(512 + i * 128, 128)], sem.at[5 + i // 2]) for i in (m, m + 1)]
         for m in (0, 2)],
    ]
    copies_w = weight_copies(w, ws, sem)
    for c in copies_x[0][0] + copies_w[0] + copies_x[0][1] + copies_w[1] + copies_w[2]:
        c.start()
    for c in copies_x[1][0] + copies_x[1][1]:
        c.start()
    side_in = pltpu.make_async_copy(side, held, sem.at[7])
    side_back = pltpu.make_async_copy(held, side_out, sem.at[7])
    side_in.start()
    row_seg = lax.broadcasted_iota(jnp.int32, (64, 64), 0)
    col_seg = lax.broadcasted_iota(jnp.int32, (64, 64), 1)
    bias = jnp.where(col_seg < row_seg, 0.0, MASKED)
    lane = lax.broadcasted_iota(jnp.int32, (512, 128), 1)
    for b in range(2):
        for j, dst in enumerate((qs, ks, vs)):
            if b == 0:
                wait_all(copies_w[j])
            for m in (0, 256):
                if j == 0:
                    wait_all(copies_x[b][m // 256])
                part = dot(xs[b * 512 + m:b * 512 + m + 256, :], ws[j])
                for h in range(4):
                    wide[j * 4 + h, m:m + 256, :] = part[:, h * 128:(h + 1) * 128]
        if b == 0:
            side_in.wait()
            side_back.start()
        for j, dst in enumerate((qs, ks, vs)):
            for h in range(4):
                for t in range(8):
                    dst[h, t * 64:(t + 1) * 64, :] = wide[j * 4 + h, pl.ds(t, 64, stride=8), :].astype(BF16)
        stats = jnp.zeros((512, 128), F32)
        for h in range(4):
            s = jnp.concatenate(
                [dot_t(qs[h, t * 64:(t + 1) * 64, :], ks[h, t * 64:(t + 1) * 64, :]) + bias for t in range(8)], axis=0
            )
            top = jnp.max(s, axis=-1, keepdims=True)
            p = jnp.exp2((s - top) * EXP_SCALE)
            total = jnp.sum(p, axis=-1, keepdims=True)
            p = p.astype(BF16)
            for t in range(8):
                res[h, pl.ds(t, 64, stride=8), :] = dot(p[t * 64:(t + 1) * 64, :], vs[h, t * 64:(t + 1) * 64, :])
            for i, v in enumerate(split3(top) + split3(total)):
                stats = jnp.where(lane == i * 4 + h, v, stats)
        for t in range(8):
            res[4, pl.ds(t, 64, stride=8), :] = stats[t * 64:(t + 1) * 64, :]
        for h in range(5):
            pack[b, :, :, h * 128:(h + 1) * 128] = res[h].astype(BF16).reshape(32, 16, 128)
        back.append(pltpu.make_async_copy(pack.at[b], out.at[:, pl.ds(b * 16, 16), :], sem.at[8 + b]))
        back[b].start()
    wait_all(back)
    side_back.wait()


def column_part(where, x_own, x_oth, w, side, *after):
    return pl.pallas_call(
        functools.partial(col_kernel, len(w)),
        out_shape=(
            jax.ShapeDtypeStruct((32, 32, 640), BF16),
            jax.ShapeDtypeStruct(side.shape, side.dtype),
        ),
        in_specs=[SMEM_SPEC] + [HBM_SPEC] * (6 + len(w) + len(after)),
        out_specs=(ANY_SPEC, ANY_SPEC),
        scratch_shapes=[
            pltpu.VMEM((1024, 2048), BF16),
            pltpu.VMEM((3, 2048, 512), BF16),
            pltpu.VMEM((12, 512, 128), F32),
            pltpu.VMEM((4, 512, 128), BF16),
            pltpu.VMEM((4, 512, 128), BF16),
            pltpu.VMEM((4, 512, 128), BF16),
            pltpu.VMEM((5, 512, 128), F32),
            pltpu.VMEM((2, 32, 16, 640), BF16),
            pltpu.VMEM(side.shape, side.dtype),
            pltpu.SemaphoreType.DMA((10,)),
        ],
        cost_estimate=cost(4),
        compiler_params=pltpu.CompilerParams(vmem_limit_bytes=VMEM_LIMIT),
        name="column_part",
    )(where, x_own, *x_oth, *w, side, *after)


def load_piece(src, s, xs, row, sem):
    return pltpu.make_async_copy(src.at[:, pl.ds(s * 2048, 2048)], xs.at[s, pl.ds(row, 256), :], sem)


def load_parts(parts, s, xs, row, sem):
    n = parts[0].shape[0]
    return [
        pltpu.make_async_copy(src.at[:, pl.ds(s * 2048, 2048)], xs.at[s, pl.ds(row + i * n, n), :], sem)
        for i, src in enumerate(parts)
    ]


def project(x, w, s, dst, dst_row):
    res = dot(x, w).astype(BF16)
    for h in range(4):
        dst[s * 4 + h, dst_row:dst_row + 512, :] = res[:, h * 128:(h + 1) * 128]


def row_kernel(nw, where, own, oth, *refs):
    w, refs = refs[:nw], refs[nw:]
    num, stats, q_out, xs, ws, qs, ks, vs, acc, st_all, sem = refs[-11:]
    upper, core = where[0], where[1]
    with_low = ks.shape[1] == 1024
    base = 512 if with_low else 0
    own_row = pl.multiple_of(core * 256, 256)
    oth_row = pl.multiple_of((1 - core) * 256, 256)
    near = [
        [load_piece(own, s, xs, base + own_row, sem.at[3 + 2 * s]),
         load_piece(oth, s, xs, base + oth_row, sem.at[4 + 2 * s])]
        for s in range(2)
    ]
    weights = weight_copies(w, ws, sem)
    for c in near[0] + weights[0] + near[1] + weights[1] + weights[2]:
        c.start()
    if with_low:
        far = [
            [load_piece(refs[0], s, xs, own_row, sem.at[7 + 2 * s])]
            + load_parts(refs[1:5], s, xs, oth_row, sem.at[8 + 2 * s])
            for s in range(2)
        ]

        @pl.when(upper == 1)
        def _():
            for c in far[0] + far[1]:
                c.start()

    for j, (dst, dst_row) in enumerate(((qs, 0), (ks, base), (vs, base))):
        wait_all(weights[j])
        for s in range(2):
            if j == 0:
                wait_all(near[s])
            project(xs[s, base:base + 512, :], ws[j], s, dst, dst_row)
    if not with_low:
        q_copy = pltpu.make_async_copy(qs, q_out, sem.at[8])
        q_copy.start()

    if with_low:
        @pl.when(upper == 1)
        def _():
            for s in range(2):
                wait_all(far[s])
                project(xs[s, 0:512, :], ws[1], s, ks, 0)
                project(xs[s, 0:512, :], ws[2], s, vs, 0)

    later = lax.broadcasted_iota(jnp.int32, (256, 256), 1) > lax.broadcasted_iota(jnp.int32, (256, 256), 0)
    lane = lax.broadcasted_iota(jnp.int32, (256, 128), 1)

    def attend(first):
        back = []
        for s in range(2):
            for blk in range(2):
                tile = core if blk == 0 else 1 - core
                st = jnp.zeros((256, 128), F32)
                for h in range(4):
                    i = s * 4 + h
                    q = qs[i, blk * 256:(blk + 1) * 256, :]
                    diag = base + blk * 256
                    sd = jnp.where(later, MASKED, dot_t(q, ks[i, diag:diag + 256, :]))
                    top = jnp.max(sd, axis=-1, keepdims=True)
                    if diag > first:
                        se = dot_t(q, ks[i, first:diag, :])
                        top = jnp.maximum(top, jnp.max(se, axis=-1, keepdims=True))
                    pd = jnp.exp2((sd - top) * EXP_SCALE)
                    total = jnp.sum(pd, axis=-1, keepdims=True)
                    part = dot(pd.astype(BF16), vs[i, diag:diag + 256, :])
                    if diag > first:
                        pe = jnp.exp2((se - top) * EXP_SCALE)
                        total += jnp.sum(pe, axis=-1, keepdims=True)
                        part += dot(pe.astype(BF16), vs[i, first:diag, :])
                    acc[blk, s, :, h * 128:(h + 1) * 128] = part
                    st = jnp.where(lane == h, top, st)
                    st = jnp.where(lane == 12 + h, total, st)
                st_all[blk, s, :, :] = st
                n = 4 * s + 2 * blk
                back.append(pltpu.make_async_copy(acc.at[blk, s], num.at[tile, s], sem.at[11 + n]))
                back.append(pltpu.make_async_copy(st_all.at[blk, s], stats.at[tile, s], sem.at[12 + n]))
                back[-2].start()
                back[-1].start()
        wait_all(back)

    if with_low:
        @pl.when(upper == 0)
        def _():
            attend(512)

        @pl.when(upper == 1)
        def _():
            attend(0)
    else:
        attend(0)
        q_copy.wait()


ROW_SHAPES = (
    jax.ShapeDtypeStruct((2, 2, 256, 512), F32),
    jax.ShapeDtypeStruct((2, 2, 256, 128), F32),
)


def near_kernel(nw, where, own, oth, *refs):
    num, stats, q_out = refs[-11:-8]
    row_kernel(nw, where, own, oth, *refs[:-11], num, stats, q_out, *refs[-8:])


def near_part(where, own, oth, w, *after):
    return pl.pallas_call(
        functools.partial(near_kernel, len(w)),
        out_shape=ROW_SHAPES
        + (jax.ShapeDtypeStruct((8, 512, 128), BF16),),
        in_specs=[SMEM_SPEC] + [HBM_SPEC] * (2 + len(w) + len(after)),
        out_specs=(ANY_SPEC,) * 3,
        scratch_shapes=[
            pltpu.VMEM((2, 512, 2048), BF16),
            pltpu.VMEM((3, 2048, 512), BF16),
            pltpu.VMEM((8, 512, 128), BF16),
            pltpu.VMEM((8, 512, 128), BF16),
            pltpu.VMEM((8, 512, 128), BF16),
            pltpu.VMEM((2, 2, 256, 512), F32),
            pltpu.VMEM((2, 2, 256, 128), F32),
            pltpu.SemaphoreType.DMA((19,)),
        ],
        cost_estimate=cost(6),
        compiler_params=pltpu.CompilerParams(vmem_limit_bytes=VMEM_LIMIT),
        name="near_part",
    )(where, own, oth, *w, *after)


def full_kernel(nw, where, own, oth, *refs):
    num, stats = refs[-10:-8]
    row_kernel(nw, where, own, oth, *refs[:-10], num, stats, None, *refs[-8:])


def row_part(where, own, oth, low_own, low_oth, w, *after):
    return pl.pallas_call(
        functools.partial(full_kernel, len(w)),
        out_shape=ROW_SHAPES,
        in_specs=[SMEM_SPEC] + [HBM_SPEC] * (7 + len(w) + len(after)),
        out_specs=(ANY_SPEC, ANY_SPEC),
        scratch_shapes=[
            pltpu.VMEM((2, 1024, 2048), BF16),
            pltpu.VMEM((3, 2048, 512), BF16),
            pltpu.VMEM((8, 512, 128), BF16),
            pltpu.VMEM((8, 1024, 128), BF16),
            pltpu.VMEM((8, 1024, 128), BF16),
            pltpu.VMEM((2, 2, 256, 512), F32),
            pltpu.VMEM((2, 2, 256, 128), F32),
            pltpu.SemaphoreType.DMA((19,)),
        ],
        cost_estimate=cost(12),
        compiler_params=pltpu.CompilerParams(vmem_limit_bytes=VMEM_LIMIT),
        name="row_part",
    )(where, own, oth, *w, low_own, *low_oth, *after)


def far_kernel(where, low_own, *refs):
    low_oth, (w, q, num_in, stats_in), refs = refs[:4], refs[4:8], refs[8:]
    num, stats, xs, ws, qs, ks, vs, acc, st_all, sem = refs[-10:]
    upper, core = where[0], where[1]
    own_row = pl.multiple_of(core * 256, 256)
    oth_row = pl.multiple_of((1 - core) * 256, 256)

    @pl.when(upper == 1)
    def _():
        far = [
            [load_piece(low_own, s, xs, own_row, sem.at[2 * s])]
            + load_parts(low_oth, s, xs, oth_row, sem.at[1 + 2 * s])
            for s in range(2)
        ]
        weights = [pltpu.make_async_copy(w.at[j], ws.at[j - 1], sem.at[3 + j]) for j in (1, 2)]
        rest = [
            pltpu.make_async_copy(q, qs, sem.at[6]),
            pltpu.make_async_copy(num_in, acc, sem.at[7]),
            pltpu.make_async_copy(stats_in, st_all, sem.at[8]),
        ]
        for c in far[0] + weights[:1] + far[1] + weights[1:] + rest:
            c.start()
        for j, dst in enumerate((ks, vs)):
            weights[j].wait()
            for s in range(2):
                if j == 0:
                    wait_all(far[s])
                project(xs[s], ws[j], s, dst, 0)
        wait_all(rest)
        lane = lax.broadcasted_iota(jnp.int32, (256, 128), 1)
        back = []
        for s in range(2):
            for blk in range(2):
                tile = core if blk == 0 else 1 - core
                st = st_all[tile, s, :, :]
                new = st
                for h in range(4):
                    i = s * 4 + h
                    f = slice(h * 128, (h + 1) * 128)
                    scores = dot_t(qs[i, blk * 256:(blk + 1) * 256, :], ks[i])
                    near_top = st[:, h:h + 1]
                    top = jnp.maximum(near_top, jnp.max(scores, axis=-1, keepdims=True))
                    p = jnp.exp2((scores - top) * EXP_SCALE)
                    factor = jnp.exp2((near_top - top) * EXP_SCALE)
                    total = jnp.sum(p, axis=-1, keepdims=True) + st[:, 12 + h:13 + h] * factor
                    acc[tile, s, :, f] = acc[tile, s, :, f] * factor + dot(p.astype(BF16), vs[i])
                    new = jnp.where(lane == h, top, new)
                    new = jnp.where(lane == 12 + h, total, new)
                st_all[tile, s, :, :] = new
                n = 4 * s + 2 * blk
                back.append(pltpu.make_async_copy(acc.at[tile, s], num.at[tile, s], sem.at[9 + n]))
                back.append(pltpu.make_async_copy(st_all.at[tile, s], stats.at[tile, s], sem.at[10 + n]))
                back[-2].start()
                back[-1].start()
        wait_all(back)


def far_part(where, low_own, low_oth, w, q, num, stats, *after):
    return pl.pallas_call(
        far_kernel,
        out_shape=ROW_SHAPES,
        in_specs=[SMEM_SPEC] + [HBM_SPEC] * (9 + len(after)),
        out_specs=(ANY_SPEC, ANY_SPEC),
        scratch_shapes=[
            pltpu.VMEM((2, 512, 2048), BF16),
            pltpu.VMEM((2, 2048, 512), BF16),
            pltpu.VMEM((8, 512, 128), BF16),
            pltpu.VMEM((8, 512, 128), BF16),
            pltpu.VMEM((8, 512, 128), BF16),
            pltpu.VMEM((2, 2, 256, 512), F32),
            pltpu.VMEM((2, 2, 256, 128), F32),
            pltpu.SemaphoreType.DMA((17,)),
        ],
        input_output_aliases={8: 0, 9: 1},
        cost_estimate=cost(4),
        compiler_params=pltpu.CompilerParams(vmem_limit_bytes=VMEM_LIMIT),
        name="far_part",
    )(where, low_own, *low_oth, w, q, num, stats, *after)


def merge_kernel(num, stats, col, own, oth):
    for tile, out in enumerate((own, oth)):
        rows = slice(tile * 16, (tile + 1) * 16)
        both = col[:, rows, 512:640].astype(F32)
        for s in range(2):
            st = stats[tile, s, :, :]
            parts = both[:, s * 8:(s + 1) * 8, :].reshape(256, 128)
            cst = (parts + pltpu.roll(parts, 124, 1)) + pltpu.roll(parts, 120, 1)
            top = jnp.maximum(st, cst)
            row_factor = pltpu.roll(jnp.exp2((st - top) * EXP_SCALE), 12, 1)
            col_factor = pltpu.roll(jnp.exp2((cst - top) * EXP_SCALE), 12, 1)
            inverse = 1.0 / (st * row_factor + cst * col_factor)
            row_factor = row_factor * inverse
            col_factor = col_factor * inverse
            for h in range(4):
                f = slice(h * 128, (h + 1) * 128)
                cnum = col[:, rows, f].astype(F32)[:, s * 8:(s + 1) * 8, :].reshape(256, 128)
                value = num[tile, s, :, f] * row_factor[:, 12 + h:13 + h] + cnum * col_factor[:, 12 + h:13 + h]
                out[s, :, f] = value.astype(BF16)


def merge(num, stats, col):
    vmem = pl.BlockSpec(memory_space=pltpu.VMEM)
    shape = jax.ShapeDtypeStruct((2, 256, 512), BF16)
    return pl.pallas_call(
        merge_kernel,
        out_shape=(shape, shape),
        in_specs=[vmem] * 3,
        out_specs=(vmem, vmem),
        cost_estimate=cost(2),
        compiler_params=pltpu.CompilerParams(vmem_limit_bytes=VMEM_LIMIT),
        name="merge",
    )(num, stats, col)


def out_kernel(*refs):
    srcs, (out, att, ws, acc, sent, sem) = refs[:11], refs[11:]
    copies = []
    for i in range(4):
        copies.append([pltpu.make_async_copy(srcs[i], att.at[i], sem.at[2 * i])])
        if i < 3:
            copies[i].append(pltpu.make_async_copy(srcs[4 + i], ws.at[i], sem.at[2 * i + 1]))
    for i, part in enumerate(srcs[7:]):
        copies[3].append(pltpu.make_async_copy(part, ws.at[3, pl.ds(i * 128, 128), :], sem.at[7]))
    for c in copies[0] + copies[1] + copies[2] + copies[3]:
        c.start()
    for i in range(3):
        wait_all(copies[i])
        part = dot(att[i].reshape(512, 512), ws[i])
        acc[...] = part if i == 0 else acc[...] + part
    wait_all(copies[3])
    back = []
    for s in range(2):
        f = pl.ds(s * 2048, 2048)
        sent[:, f] = (acc[s * 256:(s + 1) * 256, :] + dot(att[3, s], ws[3])).astype(BF16)
        back.append(pltpu.make_async_copy(sent.at[:, f], out.at[:, f], sem.at[8 + s]))
        back[s].start()
    wait_all(back)


def output_part(attended, weights):
    any_spec = pl.BlockSpec(memory_space=pl.ANY)
    return pl.pallas_call(
        out_kernel,
        out_shape=jax.ShapeDtypeStruct((256, 4096), BF16),
        in_specs=[any_spec] * 11,
        out_specs=any_spec,
        scratch_shapes=[
            pltpu.VMEM((4, 2, 256, 512), BF16),
            pltpu.VMEM((4, 512, 2048), BF16),
            pltpu.VMEM((512, 2048), F32),
            pltpu.VMEM((256, 4096), BF16),
            pltpu.SemaphoreType.DMA((10,)),
        ],
        cost_estimate=cost(4),
        compiler_params=pltpu.CompilerParams(vmem_limit_bytes=VMEM_LIMIT),
        name="output_part",
    )(*attended, *weights)


def gate_kernel(*refs):
    pass


def gate(a, *after):
    return pl.pallas_call(
        gate_kernel,
        out_shape=jax.ShapeDtypeStruct(a.shape, a.dtype),
        in_specs=[ANY_SPEC] * (1 + len(after)),
        out_specs=ANY_SPEC,
        input_output_aliases={0: 0},
        name="gate",
    )(a, *after)


def core_swap(a):
    return lax.ppermute(a, "sp", CORE_PAIRS)


def core_swap_parts(a, parts=4):
    return [core_swap(part) for part in jnp.split(a, parts, axis=0)]


def to_segments(a):
    return lax.all_to_all(a, "seg", split_axis=0, concat_axis=0, tiled=True)


def from_neighbour(a):
    return lax.ppermute(a, ("seg", "sp"), NEIGHBOUR_PAIRS)


def shards(normed, w_qkv, w_out):
    seg, sp = lax.axis_index("seg"), lax.axis_index("sp")
    z, y = seg // (NXL * NY), seg % NY
    where = jnp.stack([sp // 2, sp % 2, z, y]).astype(jnp.int32)
    chunk = from_neighbour(lax.dynamic_slice(w_qkv, (0, (z * NY + y) * 128, 0), (3, 128, 512)))
    qkv_other = [lax.all_gather(chunk, "seg", axis=1, tiled=True, axis_index_groups=PLANES)]
    row_oth = core_swap(normed)
    low_own = lax.ppermute(gate(normed, chunk), "sp", LOWER_TO_UPPER)
    num_own, stats_own, q_own = near_part(where, normed, row_oth, [w_qkv], chunk)
    by_offset = normed.reshape(32, 8, 2, 2048).transpose(0, 2, 1, 3).reshape(32, 16, 2048)
    col_own = gate(to_segments(by_offset).reshape(512, 2048), q_own)
    col_oth = core_swap_parts(col_own)
    col, out_copy = column_part(where, col_own, col_oth, [w_qkv], w_out)
    col_a = to_segments(col)
    out_other = from_neighbour(out_copy)
    low_own = gate(low_own, col)
    low_oth = core_swap_parts(low_own)
    num_own, stats_own = far_part(where, low_own, low_oth, w_qkv, q_own, num_own, stats_own)
    col, _ = column_part(where, col_own, col_oth, qkv_other, chunk[0], num_own, col_a)
    col_b = to_segments(col)
    own_a, oth_a = merge(num_own, stats_own, col_a)
    recv_a = core_swap(oth_a)
    num, stats = row_part(where, normed, row_oth, low_own, low_oth, qkv_other, col)
    own_b, oth_b = merge(num, stats, col_b)
    recv_b = core_swap(oth_b)
    out_other = gate(out_other, num)
    out_weights = (w_out, core_swap(w_out), out_other, *core_swap_parts(out_other))
    return output_part((own_a, recv_a, own_b, recv_b), out_weights)


def solution(mesh):
    in_specs = (P("sp", "seg"), P(None, None, "sp"), P("sp", None))
    return jax.shard_map(shards, mesh=mesh, in_specs=in_specs, out_specs=P("sp", "seg"), check_vma=False)
```

```python
import functools

import jax
import jax.numpy as jnp
from jax import lax
from jax.experimental import pallas as pl
from jax.experimental.pallas import tpu as pltpu
from jax.sharding import PartitionSpec as P

HEAD_DIM = 128
EXP_SCALE = HEAD_DIM ** (-0.5) * 1.4426950408889634
MASKED = -1e30
NZ, NXL, NY = 4, 2, 4
BF16, F32 = jnp.bfloat16, jnp.float32
VMEM_LIMIT = 58 * 1024 * 1024

CORE_PAIRS = [(0, 1), (1, 0), (2, 3), (3, 2)]
LOWER_TO_UPPER = [(0, 2), (1, 3)]


def seg_index(z, xl, y):
    return (z * NXL + xl) * NY + y


NEIGHBOUR_PAIRS = [
    (seg_index(z, xl, y) * 4 + xh * 2 + c, seg_index(z, 1 - xl, y) * 4 + (1 - xh) * 2 + c)
    for z in range(NZ)
    for xl in range(NXL)
    for y in range(NY)
    for xh in range(2)
    for c in range(2)
]
MOVES = {
    (axis, d): [
        (seg_index(z, xl, y), seg_index((z + d) % NZ, xl, y) if axis == "z" else seg_index(z, xl, (y + d) % NY))
        for z in range(NZ)
        for xl in range(NXL)
        for y in range(NY)
    ]
    for axis in "zy"
    for d in (1, -1)
}
PIECES = [(half, step, sub) for half in range(2) for step, sub in ((0, 0), (1, 0), (3, 0), (2, 0), (2, 1))]


ANY_SPEC = pl.BlockSpec(memory_space=pl.ANY)
HBM_SPEC = pl.BlockSpec(memory_space=pltpu.HBM)
SMEM_SPEC = pl.BlockSpec(memory_space=pltpu.SMEM)
VMEM_SPEC = pl.BlockSpec(memory_space=pltpu.VMEM)


def cost(us):
    return pl.CostEstimate(flops=int(us * 1e9), transcendentals=0, bytes_accessed=int(us * 1e6))


def dot(a, b):
    return jnp.dot(a, b, preferred_element_type=F32)


def dot_t(a, b):
    return lax.dot_general(a, b, (((1,), (1,)), ((), ())), preferred_element_type=F32)


def split3(v):
    hi = v.astype(BF16).astype(F32)
    rest = v - hi
    mid = rest.astype(BF16).astype(F32)
    return hi, mid, (rest - mid).astype(BF16).astype(F32)


def weight_copies(w, ws, sem, where):
    if len(w) == 1:
        return [[pltpu.make_async_copy(w[0].at[j], ws.at[j], sem.at[j])] for j in range(3)]
    copies = [[], [], []]
    for i, (piece, (half, step, sub)) in enumerate(zip(w, PIECES)):
        row = pl.multiple_of(half * 1024 + lax.rem(where[2 + half] + step, 4) * 256 + sub * 128, 128)
        for j in range(3):
            copies[j].append(
                pltpu.make_async_copy(
                    piece.at[j], ws.at[j, pl.ds(row, piece.shape[1]), :], sem.at[j]
                )
            )
    return copies


def wait_all(copies):
    for c in copies:
        c.wait()


def col_kernel(nw, parts, where, x0, *refs):
    x1, w, refs = refs[:4], refs[4:4 + nw], refs[4 + nw:]
    side, out, sides, (xs, ws, wide, qs, ks, vs, res, pack, held, sem) = (
        refs[0], refs[-11 - parts], refs[-10 - parts:-10], refs[-10:]
    )
    back = []
    copies_x = [
        [[pltpu.make_async_copy(x0.at[pl.ds(m, 256)], xs.at[pl.ds(m, 256)], sem.at[3 + m // 256])] for m in (0, 256)],
        [[pltpu.make_async_copy(x1[i], xs.at[pl.ds(512 + i * 128, 128)], sem.at[5 + i // 2]) for i in (m, m + 1)]
         for m in (0, 2)],
    ]
    copies_w = weight_copies(w, ws, sem, where)
    for c in copies_x[0][0] + copies_w[0] + copies_x[0][1] + copies_w[1] + copies_w[2]:
        c.start()
    for c in copies_x[1][0] + copies_x[1][1]:
        c.start()
    side_in = pltpu.make_async_copy(side, held, sem.at[7])
    rows = side.shape[0] // parts
    side_back = [
        pltpu.make_async_copy(held.at[pl.ds(i * rows, rows)], to, sem.at[7]) for i, to in enumerate(sides)
    ]
    side_in.start()
    row_seg = lax.broadcasted_iota(jnp.int32, (64, 64), 0)
    col_seg = lax.broadcasted_iota(jnp.int32, (64, 64), 1)
    bias = jnp.where(col_seg < row_seg, 0.0, MASKED)
    lane = lax.broadcasted_iota(jnp.int32, (512, 128), 1)
    vs[:, :, 128:256] = jnp.ones((4, 512, 128), BF16)
    for b in range(2):
        for j, dst in enumerate((qs, ks, vs)):
            if b == 0:
                wait_all(copies_w[j])
            for m in (0, 256):
                if j == 0:
                    wait_all(copies_x[b][m // 256])
                part = dot(xs[b * 512 + m:b * 512 + m + 256, :], ws[j])
                for h in range(4):
                    wide[j * 4 + h, m:m + 256, :] = part[:, h * 128:(h + 1) * 128]
        if b == 0:
            side_in.wait()
            for c in side_back:
                c.start()
        for j, dst in enumerate((qs, ks, vs)):
            for h in range(4):
                for t in range(8):
                    dst[h, t * 64:(t + 1) * 64, 0:128] = wide[j * 4 + h, pl.ds(t, 64, stride=8), :].astype(BF16)
        raw = jnp.zeros((512, 128), F32)
        for h in range(4):
            s = jnp.concatenate(
                [dot_t(qs[h, t * 64:(t + 1) * 64, :], ks[h, t * 64:(t + 1) * 64, :]) + bias for t in range(8)], axis=0
            )
            top = jnp.max(s, axis=-1, keepdims=True)
            p = jnp.exp2((s - top) * EXP_SCALE)
            p = p.astype(BF16)
            totals = []
            for t in range(8):
                part = dot(p[t * 64:(t + 1) * 64, :], vs[h, t * 64:(t + 1) * 64, :])
                res[h, pl.ds(t, 64, stride=8), :] = part[:, 0:128]
                totals.append(part[:, 128:256])
            raw = jnp.where(lane == h, top, raw)
            raw = jnp.where(lane == 12 + h, jnp.concatenate(totals, axis=0), raw)
        hi, mid, low = split3(raw)
        stats = hi + pltpu.roll(mid, 4, 1) + pltpu.roll(low, 8, 1)
        for t in range(8):
            res[4, pl.ds(t, 64, stride=8), :] = stats[t * 64:(t + 1) * 64, :]
        for h in range(5):
            pack[b, :, :, h * 128:(h + 1) * 128] = res[h].astype(BF16).reshape(32, 16, 128)
        back.append(pltpu.make_async_copy(pack.at[b], out.at[:, pl.ds(b * 16, 16), :], sem.at[8 + b]))
        back[b].start()
    wait_all(back)
    wait_all(side_back)


def column_part(where, x_own, x_oth, w, side, parts, *after):
    return pl.pallas_call(
        functools.partial(col_kernel, len(w), parts),
        out_shape=(
            jax.ShapeDtypeStruct((32, 32, 640), BF16),
        )
        + (jax.ShapeDtypeStruct((side.shape[0] // parts, side.shape[1]), side.dtype),) * parts,
        in_specs=[SMEM_SPEC] + [HBM_SPEC] * (6 + len(w) + len(after)),
        out_specs=(ANY_SPEC,) * (1 + parts),
        scratch_shapes=[
            pltpu.VMEM((1024, 2048), BF16),
            pltpu.VMEM((3, 2048, 512), BF16),
            pltpu.VMEM((12, 512, 128), F32),
            pltpu.VMEM((4, 512, 128), BF16),
            pltpu.VMEM((4, 512, 128), BF16),
            pltpu.VMEM((4, 512, 256), BF16),
            pltpu.VMEM((5, 512, 128), F32),
            pltpu.VMEM((2, 32, 16, 640), BF16),
            pltpu.VMEM(side.shape, side.dtype),
            pltpu.SemaphoreType.DMA((10,)),
        ],
        cost_estimate=cost(4),
        compiler_params=pltpu.CompilerParams(vmem_limit_bytes=VMEM_LIMIT),
        name="column_part",
    )(where, x_own, *x_oth, *w, side, *after)


def load_piece(src, s, xs, row, sem):
    return pltpu.make_async_copy(src.at[:, pl.ds(s * 2048, 2048)], xs.at[s, pl.ds(row, 256), :], sem)


def load_parts(parts, s, xs, row, sem):
    n = parts[0].shape[0]
    return [
        pltpu.make_async_copy(src.at[:, pl.ds(s * 2048, 2048)], xs.at[s, pl.ds(row + i * n, n), :], sem)
        for i, src in enumerate(parts)
    ]


def project(x, w, s, dst, dst_row):
    res = dot(x, w).astype(BF16)
    for h in range(4):
        dst[s * 4 + h, dst_row:dst_row + 512, 0:128] = res[:, h * 128:(h + 1) * 128]


def row_kernel(nw, where, own, oth, *refs):
    w, refs = refs[:nw], refs[nw:]
    num, stats, aux, xs, ws, qs, ks, vs, acc, st_all, sem = refs[-11:]
    upper, core = where[0], where[1]
    with_low = ks.shape[1] == 1024
    base = 512 if with_low else 0
    own_row = pl.multiple_of(core * 256, 256)
    oth_row = pl.multiple_of((1 - core) * 256, 256)
    near = [
        [load_piece(own, s, xs, base + own_row, sem.at[3 + 2 * s]),
         load_piece(oth, s, xs, base + oth_row, sem.at[4 + 2 * s])]
        for s in range(2)
    ]
    vs[:, :, 128:256] = jnp.ones(vs.shape[:2] + (128,), BF16)
    weights = weight_copies(w, ws, sem, where)
    for c in near[0] + weights[0] + near[1] + weights[1] + weights[2]:
        c.start()
    if with_low:
        far = [
            [load_piece(refs[0], s, xs, own_row, sem.at[7 + 2 * s])]
            + load_parts(refs[1:5], s, xs, oth_row, sem.at[8 + 2 * s])
            for s in range(2)
        ]

        @pl.when(upper == 1)
        def _():
            for c in far[0] + far[1]:
                c.start()

    for j, (dst, dst_row) in enumerate(((qs, 0), (ks, base), (vs, base))):
        wait_all(weights[j])
        for s in range(2):
            if j == 0:
                wait_all(near[s])
            project(xs[s, base:base + 512, :], ws[j], s, dst, dst_row)
    if not with_low:
        extra = [pltpu.make_async_copy(qs, aux[0], sem.at[8])] + [
            pltpu.make_async_copy(xs.at[s, pl.ds(own_row, 256), :], aux[1].at[:, pl.ds(s * 2048, 2048)], sem.at[9 + s])
            for s in range(2)
        ]
        for c in extra:
            c.start()

    if with_low:
        @pl.when(upper == 1)
        def _():
            for s in range(2):
                wait_all(far[s])
                project(xs[s, 0:512, :], ws[1], s, ks, 0)
                project(xs[s, 0:512, :], ws[2], s, vs, 0)

    later = lax.broadcasted_iota(jnp.int32, (256, 256), 1) > lax.broadcasted_iota(jnp.int32, (256, 256), 0)
    lane = lax.broadcasted_iota(jnp.int32, (256, 128), 1)

    def attend(first):
        back = []
        for s in range(2):
            for blk in range(2):
                tile = core if blk == 0 else 1 - core
                st = jnp.zeros((256, 128), F32)
                for h in range(4):
                    i = s * 4 + h
                    q = qs[i, blk * 256:(blk + 1) * 256, :]
                    diag = base + blk * 256
                    sd = jnp.where(later, MASKED, dot_t(q, ks[i, diag:diag + 256, :]))
                    top = jnp.max(sd, axis=-1, keepdims=True)
                    if diag > first:
                        se = dot_t(q, ks[i, first:diag, :])
                        top = jnp.maximum(top, jnp.max(se, axis=-1, keepdims=True))
                    pd = jnp.exp2((sd - top) * EXP_SCALE)
                    part = dot(pd.astype(BF16), vs[i, diag:diag + 256, :])
                    if diag > first:
                        pe = jnp.exp2((se - top) * EXP_SCALE)
                        part += dot(pe.astype(BF16), vs[i, first:diag, :])
                    acc[blk, s, :, h * 128:(h + 1) * 128] = part[:, 0:128]
                    st = jnp.where(lane == h, top, st)
                    st = jnp.where(lane == 12 + h, part[:, 128:256], st)
                st_all[blk, s, :, :] = st
                n = 4 * s + 2 * blk
                back.append(pltpu.make_async_copy(acc.at[blk, s], num.at[tile, s], sem.at[11 + n]))
                back.append(pltpu.make_async_copy(st_all.at[blk, s], stats.at[tile, s], sem.at[12 + n]))
                back[-2].start()
                back[-1].start()
        wait_all(back)

    if with_low:
        @pl.when(upper == 0)
        def _():
            attend(512)

        @pl.when(upper == 1)
        def _():
            attend(0)
    else:
        attend(0)
        wait_all(extra)


ROW_SHAPES = (
    jax.ShapeDtypeStruct((2, 2, 256, 512), F32),
    jax.ShapeDtypeStruct((2, 2, 256, 128), F32),
)


def near_kernel(nw, where, own, oth, *refs):
    num, stats, q_out, own_out = refs[-12:-8]
    row_kernel(nw, where, own, oth, *refs[:-12], num, stats, (q_out, own_out), *refs[-8:])


def near_part(where, own, oth, w, *after):
    return pl.pallas_call(
        functools.partial(near_kernel, len(w)),
        out_shape=ROW_SHAPES
        + (jax.ShapeDtypeStruct((8, 512, 128), BF16), jax.ShapeDtypeStruct((256, 4096), BF16)),
        in_specs=[SMEM_SPEC] + [HBM_SPEC] * (2 + len(w) + len(after)),
        out_specs=(ANY_SPEC,) * 4,
        scratch_shapes=[
            pltpu.VMEM((2, 512, 2048), BF16),
            pltpu.VMEM((3, 2048, 512), BF16),
            pltpu.VMEM((8, 512, 128), BF16),
            pltpu.VMEM((8, 512, 128), BF16),
            pltpu.VMEM((8, 512, 256), BF16),
            pltpu.VMEM((2, 2, 256, 512), F32),
            pltpu.VMEM((2, 2, 256, 128), F32),
            pltpu.SemaphoreType.DMA((19,)),
        ],
        cost_estimate=cost(6),
        compiler_params=pltpu.CompilerParams(vmem_limit_bytes=VMEM_LIMIT),
        name="near_part",
    )(where, own, oth, *w, *after)


def full_kernel(nw, where, own, oth, *refs):
    num, stats = refs[-10:-8]
    row_kernel(nw, where, own, oth, *refs[:-10], num, stats, None, *refs[-8:])


def row_part(where, own, oth, low_own, low_oth, w, *after):
    return pl.pallas_call(
        functools.partial(full_kernel, len(w)),
        out_shape=ROW_SHAPES,
        in_specs=[SMEM_SPEC] + [HBM_SPEC] * (7 + len(w) + len(after)),
        out_specs=(ANY_SPEC, ANY_SPEC),
        scratch_shapes=[
            pltpu.VMEM((2, 1024, 2048), BF16),
            pltpu.VMEM((3, 2048, 512), BF16),
            pltpu.VMEM((8, 512, 128), BF16),
            pltpu.VMEM((8, 1024, 128), BF16),
            pltpu.VMEM((8, 1024, 256), BF16),
            pltpu.VMEM((2, 2, 256, 512), F32),
            pltpu.VMEM((2, 2, 256, 128), F32),
            pltpu.SemaphoreType.DMA((19,)),
        ],
        cost_estimate=cost(12),
        compiler_params=pltpu.CompilerParams(vmem_limit_bytes=VMEM_LIMIT),
        name="row_part",
    )(where, own, oth, *w, low_own, *low_oth, *after)


def far_kernel(where, low_own, *refs):
    low_oth, (w, q, num_in, stats_in), refs = refs[:4], refs[4:8], refs[8:]
    num, stats, xs, ws, qs, ks, vs, acc, st_all, sem = refs[-10:]
    upper, core = where[0], where[1]
    own_row = pl.multiple_of(core * 256, 256)
    oth_row = pl.multiple_of((1 - core) * 256, 256)

    @pl.when(upper == 1)
    def _():
        far = [
            [load_piece(low_own, s, xs, own_row, sem.at[2 * s])]
            + load_parts(low_oth, s, xs, oth_row, sem.at[1 + 2 * s])
            for s in range(2)
        ]
        weights = [pltpu.make_async_copy(w.at[j], ws.at[j - 1], sem.at[3 + j]) for j in (1, 2)]
        rest = [
            pltpu.make_async_copy(q, qs, sem.at[6]),
            pltpu.make_async_copy(num_in, acc, sem.at[7]),
            pltpu.make_async_copy(stats_in, st_all, sem.at[8]),
        ]
        for c in far[0] + weights[:1] + far[1] + weights[1:] + rest:
            c.start()
        vs[:, :, 128:256] = jnp.ones((8, 512, 128), BF16)
        for j, dst in enumerate((ks, vs)):
            weights[j].wait()
            for s in range(2):
                if j == 0:
                    wait_all(far[s])
                project(xs[s], ws[j], s, dst, 0)
        wait_all(rest)
        lane = lax.broadcasted_iota(jnp.int32, (256, 128), 1)
        back = []
        for s in range(2):
            for blk in range(2):
                tile = core if blk == 0 else 1 - core
                st = st_all[tile, s, :, :]
                new = st
                for h in range(4):
                    i = s * 4 + h
                    f = slice(h * 128, (h + 1) * 128)
                    scores = dot_t(qs[i, blk * 256:(blk + 1) * 256, :], ks[i])
                    near_top = st[:, h:h + 1]
                    top = jnp.maximum(near_top, jnp.max(scores, axis=-1, keepdims=True))
                    p = jnp.exp2((scores - top) * EXP_SCALE)
                    factor = jnp.exp2((near_top - top) * EXP_SCALE)
                    part = dot(p.astype(BF16), vs[i])
                    acc[tile, s, :, f] = acc[tile, s, :, f] * factor + part[:, 0:128]
                    new = jnp.where(lane == h, top, new)
                    new = jnp.where(lane == 12 + h, st * factor + part[:, 128:256], new)
                st_all[tile, s, :, :] = new
                n = 4 * s + 2 * blk
                back.append(pltpu.make_async_copy(acc.at[tile, s], num.at[tile, s], sem.at[9 + n]))
                back.append(pltpu.make_async_copy(st_all.at[tile, s], stats.at[tile, s], sem.at[10 + n]))
                back[-2].start()
                back[-1].start()
        wait_all(back)


def far_part(where, low_own, low_oth, w, q, num, stats, *after):
    return pl.pallas_call(
        far_kernel,
        out_shape=ROW_SHAPES,
        in_specs=[SMEM_SPEC] + [HBM_SPEC] * (9 + len(after)),
        out_specs=(ANY_SPEC, ANY_SPEC),
        scratch_shapes=[
            pltpu.VMEM((2, 512, 2048), BF16),
            pltpu.VMEM((2, 2048, 512), BF16),
            pltpu.VMEM((8, 512, 128), BF16),
            pltpu.VMEM((8, 512, 128), BF16),
            pltpu.VMEM((8, 512, 256), BF16),
            pltpu.VMEM((2, 2, 256, 512), F32),
            pltpu.VMEM((2, 2, 256, 128), F32),
            pltpu.SemaphoreType.DMA((17,)),
        ],
        input_output_aliases={8: 0, 9: 1},
        cost_estimate=cost(4),
        compiler_params=pltpu.CompilerParams(vmem_limit_bytes=VMEM_LIMIT),
        name="far_part",
    )(where, low_own, *low_oth, w, q, num, stats, *after)


def merge_kernel(parts, num_in, stats_in, col_in, *refs):
    if parts:
        side, refs, held = refs[0], refs[1:-1], refs[-1]
    own, oth, sides, (num, stats, col, done, sem) = refs[0], refs[1], refs[2:2 + parts], refs[2 + parts:]
    def halves(tile):
        return pl.ds(tile * 16, 16)

    into = [
        [pltpu.make_async_copy(col_in.at[:, halves(tile), :], col.at[:, halves(tile), :], sem.at[tile])]
        + [pltpu.make_async_copy(num_in.at[tile, s], num.at[tile, s], sem.at[2 + 2 * tile + s]) for s in range(2)]
        + [pltpu.make_async_copy(stats_in.at[tile, s], stats.at[tile, s], sem.at[2 + 2 * tile + s]) for s in range(2)]
        for tile in range(2)
    ]
    for c in into[1] + into[0]:
        c.start()
    if parts:
        side_in = pltpu.make_async_copy(side, held, sem.at[8])
        side_in.start()
    back = []
    for tile, out in ((1, oth), (0, own)):
        wait_all(into[tile])
        both = col[:, tile * 16:(tile + 1) * 16, 512:640].astype(F32)
        for s in range(2):
            st = stats[tile, s, :, :]
            terms = both[:, s * 8:(s + 1) * 8, :].reshape(256, 128)
            cst = (terms + pltpu.roll(terms, 124, 1)) + pltpu.roll(terms, 120, 1)
            top = jnp.maximum(st, cst)
            row_factor = pltpu.roll(jnp.exp2((st - top) * EXP_SCALE), 12, 1)
            col_factor = pltpu.roll(jnp.exp2((cst - top) * EXP_SCALE), 12, 1)
            inverse = 1.0 / (st * row_factor + cst * col_factor)
            row_factor = row_factor * inverse
            col_factor = col_factor * inverse
            for h in range(4):
                f = slice(h * 128, (h + 1) * 128)
                cnum = col[:, tile * 16:(tile + 1) * 16, f].astype(F32)[:, s * 8:(s + 1) * 8, :].reshape(256, 128)
                value = num[tile, s, :, f] * row_factor[:, 12 + h:13 + h] + cnum * col_factor[:, 12 + h:13 + h]
                done[tile, s, :, f] = value.astype(BF16)
        back.append(pltpu.make_async_copy(done.at[tile], out, sem.at[6 + tile]))
        back[-1].start()
    if parts:
        side_in.wait()
        n = side.shape[0] // parts
        for i, to in enumerate(sides):
            back.append(pltpu.make_async_copy(held.at[pl.ds(i * n, n)], to, sem.at[9]))
            back[-1].start()
    wait_all(back)


def merge(num, stats, col, side=(), parts=0):
    shape = jax.ShapeDtypeStruct((2, 256, 512), BF16)
    side_shape = [jax.ShapeDtypeStruct((a.shape[0] // parts, a.shape[1]), a.dtype) for a in side] * parts
    return pl.pallas_call(
        functools.partial(merge_kernel, parts),
        out_shape=(shape, shape, *side_shape),
        in_specs=[HBM_SPEC] * (3 + len(side)),
        out_specs=(ANY_SPEC,) * (2 + parts),
        scratch_shapes=[
            pltpu.VMEM((2, 2, 256, 512), F32),
            pltpu.VMEM((2, 2, 256, 128), F32),
            pltpu.VMEM((32, 32, 640), BF16),
            pltpu.VMEM((2, 2, 256, 512), BF16),
            pltpu.SemaphoreType.DMA((10,)),
        ]
        + [pltpu.VMEM(a.shape, a.dtype) for a in side],
        cost_estimate=cost(2),
        compiler_params=pltpu.CompilerParams(vmem_limit_bytes=VMEM_LIMIT),
        name="merge",
    )(num, stats, col, *side)


def out_kernel(*refs):
    srcs, (out, att, ws, acc, sent, sem) = refs[:11], refs[11:]
    copies = []
    for i in range(4):
        copies.append([pltpu.make_async_copy(srcs[i], att.at[i], sem.at[2 * i])])
        if i < 3:
            copies[i].append(pltpu.make_async_copy(srcs[4 + i], ws.at[i], sem.at[2 * i + 1]))
    for i, part in enumerate(srcs[7:]):
        copies[3].append(pltpu.make_async_copy(part, ws.at[3, pl.ds(i * 128, 128), :], sem.at[7]))
    for c in copies[0] + copies[1] + copies[2] + copies[3]:
        c.start()
    for i in range(3):
        wait_all(copies[i])
        part = dot(att[i].reshape(512, 512), ws[i])
        acc[...] = part if i == 0 else acc[...] + part
    wait_all(copies[3])
    back = []
    for s in range(2):
        f = pl.ds(s * 2048, 2048)
        sent[:, f] = (acc[s * 256:(s + 1) * 256, :] + dot(att[3, s], ws[3])).astype(BF16)
        back.append(pltpu.make_async_copy(sent.at[:, f], out.at[:, f], sem.at[8 + s]))
        back[s].start()
    wait_all(back)


def output_part(attended, weights):
    any_spec = pl.BlockSpec(memory_space=pl.ANY)
    return pl.pallas_call(
        out_kernel,
        out_shape=jax.ShapeDtypeStruct((256, 4096), BF16),
        in_specs=[any_spec] * 11,
        out_specs=any_spec,
        scratch_shapes=[
            pltpu.VMEM((4, 2, 256, 512), BF16),
            pltpu.VMEM((4, 512, 2048), BF16),
            pltpu.VMEM((512, 2048), F32),
            pltpu.VMEM((256, 4096), BF16),
            pltpu.SemaphoreType.DMA((10,)),
        ],
        cost_estimate=cost(4),
        compiler_params=pltpu.CompilerParams(vmem_limit_bytes=VMEM_LIMIT),
        name="output_part",
    )(*attended, *weights)


def gate_kernel(*refs):
    pass


def gate(a, *after):
    return pl.pallas_call(
        gate_kernel,
        out_shape=jax.ShapeDtypeStruct(a.shape, a.dtype),
        in_specs=[ANY_SPEC] * (1 + len(after)),
        out_specs=ANY_SPEC,
        input_output_aliases={0: 0},
        name="gate",
    )(a, *after)


def core_swap(a):
    return lax.ppermute(a, "sp", CORE_PAIRS)


def core_swap_parts(a, parts=4):
    return [core_swap(part) for part in jnp.split(a, parts, axis=0)]


def to_segments(a):
    return lax.all_to_all(a, "seg", split_axis=0, concat_axis=0, tiled=True)


def from_neighbour(a):
    return lax.ppermute(a, ("seg", "sp"), NEIGHBOUR_PAIRS)


def ring_near(quarter, axis):
    return (
        lax.ppermute(quarter, "seg", MOVES[axis, -1]),
        lax.ppermute(quarter, "seg", MOVES[axis, 1]),
    )


def cut_kernel(*refs):
    n = (len(refs) - 3) // 2
    srcs, dsts, held, sem = refs[:n], refs[n + 1:2 * n + 1], refs[-2], refs[-1]
    load = [
        pltpu.make_async_copy(src.at[:, pl.ds(128 * (i % 2), 128), :], held.at[i], sem.at[i])
        for i, src in enumerate(srcs)
    ]
    store = [pltpu.make_async_copy(held.at[i], dst, sem.at[n + i]) for i, dst in enumerate(dsts)]
    for c in load:
        c.start()
    for i in range(n):
        load[i].wait()
        store[i].start()
    wait_all(store)


def cut(pieces, after):
    n = len(pieces)
    half = jax.ShapeDtypeStruct((3, 128, 512), BF16)
    return pl.pallas_call(
        cut_kernel,
        out_shape=(half,) * n,
        in_specs=[ANY_SPEC] * (n + 1),
        out_specs=(ANY_SPEC,) * n,
        scratch_shapes=[pltpu.VMEM((n, 3, 128, 512), BF16), pltpu.SemaphoreType.DMA((2 * n,))],
        cost_estimate=cost(0.5),
        compiler_params=pltpu.CompilerParams(vmem_limit_bytes=VMEM_LIMIT),
        name="cut",
    )(*pieces, after)


def ring_far(nxt, prev, axis):
    return (
        lax.ppermute(nxt, "seg", MOVES[axis, -1]),
        lax.ppermute(prev, "seg", MOVES[axis, 1]),
    )


def other_quarter(w_qkv, row):
    return from_neighbour(lax.dynamic_slice(w_qkv, (0, row, 0), (3, 256, 512)))


def shards(normed, w_qkv, w_out):
    seg, sp = lax.axis_index("seg"), lax.axis_index("sp")
    z, y = seg // (NXL * NY), seg % NY
    where = jnp.stack([sp // 2, sp % 2, z, y]).astype(jnp.int32)
    by_z, by_y = other_quarter(w_qkv, z * 256), other_quarter(w_qkv, 1024 + y * 256)
    row_oth = core_swap(normed)
    num_own, stats_own, q_own, own_copy = near_part(where, normed, row_oth, [w_qkv])
    by_z, by_y = gate(by_z, q_own), gate(by_y, q_own)
    low_own = lax.ppermute(gate(own_copy, by_z, by_y), "sp", LOWER_TO_UPPER)
    z_near, y_near = ring_near(by_z, "z"), ring_near(by_y, "y")
    by_offset = normed.reshape(32, 8, 2, 2048).transpose(0, 2, 1, 3).reshape(32, 16, 2048)
    col_own = gate(to_segments(by_offset).reshape(512, 2048), q_own)
    col_oth = core_swap_parts(col_own)
    col, out_copy = column_part(where, col_own, col_oth, [w_qkv], w_out, 1)
    halves = cut((*z_near, *y_near), col)
    z_far, y_far = ring_far(*halves[:2], "z"), ring_far(*halves[2:], "y")
    qkv_other = [by_z, *z_near, *z_far, by_y, *y_near, *y_far]
    col_a = to_segments(gate(col, *z_far, *y_far))
    col, *low_parts = column_part(where, col_own, col_oth, qkv_other, low_own, 4)
    col_b = to_segments(col)
    out_other = from_neighbour(gate(out_copy, col))
    low_oth = [core_swap(part) for part in low_parts]
    num_own, stats_own = far_part(where, low_own, low_oth, w_qkv, q_own, num_own, stats_own)
    own_a, oth_a = merge(num_own, stats_own, col_a)
    recv_a = core_swap(oth_a)
    num, stats = row_part(where, normed, row_oth, low_own, low_oth, qkv_other, own_a)
    own_b, oth_b, *out_parts = merge(num, stats, col_b, (out_other,), 4)
    recv_b = core_swap(oth_b)
    out_weights = (w_out, core_swap(w_out), out_other, *[core_swap(part) for part in out_parts])
    return output_part((own_a, recv_a, own_b, recv_b), out_weights)


def solution(mesh):
    in_specs = (P("sp", "seg"), P(None, None, "sp"), P("sp", None))
    return jax.shard_map(shards, mesh=mesh, in_specs=in_specs, out_specs=P("sp", "seg"), check_vma=False)
```

```python
import functools

import jax
import jax.numpy as jnp
from jax import lax
from jax.experimental import pallas as pl
from jax.experimental.pallas import tpu as pltpu
from jax.sharding import PartitionSpec as P

HEAD_DIM = 128
EXP_SCALE = HEAD_DIM ** (-0.5) * 1.4426950408889634
MASKED = -1e30
NZ, NXL, NY = 4, 2, 4
BF16, F32 = jnp.bfloat16, jnp.float32
VMEM_LIMIT = 58 * 1024 * 1024

CORE_PAIRS = [(0, 1), (1, 0), (2, 3), (3, 2)]
LOWER_TO_UPPER = [(0, 2), (1, 3)]


def seg_index(z, xl, y):
    return (z * NXL + xl) * NY + y


NEIGHBOUR_PAIRS = [
    (seg_index(z, xl, y) * 4 + xh * 2 + c, seg_index(z, 1 - xl, y) * 4 + (1 - xh) * 2 + c)
    for z in range(NZ)
    for xl in range(NXL)
    for y in range(NY)
    for xh in range(2)
    for c in range(2)
]
MOVES = {
    (axis, d): [
        (seg_index(z, xl, y), seg_index((z + d) % NZ, xl, y) if axis == "z" else seg_index(z, xl, (y + d) % NY))
        for z in range(NZ)
        for xl in range(NXL)
        for y in range(NY)
    ]
    for axis in "zy"
    for d in (1, -1)
}
PAIRS = {
    axis: [
        (seg_index(z, xl, y), seg_index(z ^ 1, xl, y) if axis == "z" else seg_index(z, xl, y ^ 1))
        for z in range(NZ)
        for xl in range(NXL)
        for y in range(NY)
    ]
    for axis in "zy"
}
PIECES = [(half, step, sub) for half in range(2) for step, sub in ((0, 0), (1, 0), (3, 0), (2, 0), (2, 1))]


ANY_SPEC = pl.BlockSpec(memory_space=pl.ANY)
HBM_SPEC = pl.BlockSpec(memory_space=pltpu.HBM)
SMEM_SPEC = pl.BlockSpec(memory_space=pltpu.SMEM)
VMEM_SPEC = pl.BlockSpec(memory_space=pltpu.VMEM)


def cost(us):
    return pl.CostEstimate(flops=int(us * 1e9), transcendentals=0, bytes_accessed=int(us * 1e6))


def dot(a, b):
    return jnp.dot(a, b, preferred_element_type=F32)


def dot_t(a, b):
    return lax.dot_general(a, b, (((1,), (1,)), ((), ())), preferred_element_type=F32)


def split3(v):
    hi = v.astype(BF16).astype(F32)
    rest = v - hi
    mid = rest.astype(BF16).astype(F32)
    return hi, mid, (rest - mid).astype(BF16).astype(F32)


def weight_copies(w, ws, sem, where):
    if len(w) == 1:
        return [[pltpu.make_async_copy(w[0].at[j], ws.at[j], sem.at[j])] for j in range(3)]
    copies = [[], [], []]
    for i, (piece, (half, step, sub)) in enumerate(zip(w, PIECES)):
        row = pl.multiple_of(half * 1024 + lax.rem(where[2 + half] + step, 4) * 256 + sub * 128, 128)
        for j in range(3):
            copies[j].append(
                pltpu.make_async_copy(
                    piece.at[j], ws.at[j, pl.ds(row, piece.shape[1]), :], sem.at[j]
                )
            )
    return copies


def wait_all(copies):
    for c in copies:
        c.wait()


def col_kernel(nw, parts, where, x0, *refs):
    x1, w, refs = refs[:4], refs[4:4 + nw], refs[4 + nw:]
    side, out, sides, (xs, ws, wide, qs, ks, vs, res, pack, held, sem) = (
        refs[0], refs[-11 - parts], refs[-10 - parts:-10], refs[-10:]
    )
    back = []
    copies_x = [
        [[pltpu.make_async_copy(x0.at[pl.ds(m, 256)], xs.at[pl.ds(m, 256)], sem.at[3 + m // 256])] for m in (0, 256)],
        [[pltpu.make_async_copy(x1[i], xs.at[pl.ds(512 + i * 128, 128)], sem.at[5 + i // 2]) for i in (m, m + 1)]
         for m in (0, 2)],
    ]
    copies_w = weight_copies(w, ws, sem, where)
    for c in copies_x[0][0] + copies_w[0] + copies_x[0][1] + copies_w[1] + copies_w[2]:
        c.start()
    for c in copies_x[1][0] + copies_x[1][1]:
        c.start()
    side_in = pltpu.make_async_copy(side, held, sem.at[7])
    rows = side.shape[0] // parts
    side_back = [
        pltpu.make_async_copy(held.at[pl.ds(i * rows, rows)], to, sem.at[7]) for i, to in enumerate(sides)
    ]
    side_in.start()
    row_seg = lax.broadcasted_iota(jnp.int32, (64, 64), 0)
    col_seg = lax.broadcasted_iota(jnp.int32, (64, 64), 1)
    bias = jnp.where(col_seg < row_seg, 0.0, MASKED)
    lane = lax.broadcasted_iota(jnp.int32, (512, 128), 1)
    vs[:, :, 128:256] = jnp.ones((4, 512, 128), BF16)
    for b in range(2):
        for j, dst in enumerate((qs, ks, vs)):
            if b == 0:
                wait_all(copies_w[j])
            for m in (0, 256):
                if j == 0:
                    wait_all(copies_x[b][m // 256])
                part = dot(xs[b * 512 + m:b * 512 + m + 256, :], ws[j])
                for h in range(4):
                    wide[j * 4 + h, m:m + 256, :] = part[:, h * 128:(h + 1) * 128]
        if b == 0:
            side_in.wait()
            for c in side_back:
                c.start()
        for j, dst in enumerate((qs, ks, vs)):
            for h in range(4):
                for t in range(8):
                    dst[h, t * 64:(t + 1) * 64, 0:128] = wide[j * 4 + h, pl.ds(t, 64, stride=8), :].astype(BF16)
        raw = jnp.zeros((512, 128), F32)
        for h in range(4):
            s = jnp.concatenate(
                [dot_t(qs[h, t * 64:(t + 1) * 64, :], ks[h, t * 64:(t + 1) * 64, :]) + bias for t in range(8)], axis=0
            )
            top = jnp.max(s, axis=-1, keepdims=True)
            p = jnp.exp2((s - top) * EXP_SCALE)
            p = p.astype(BF16)
            totals = []
            for t in range(8):
                part = dot(p[t * 64:(t + 1) * 64, :], vs[h, t * 64:(t + 1) * 64, :])
                res[h, pl.ds(t, 64, stride=8), :] = part[:, 0:128]
                totals.append(part[:, 128:256])
            raw = jnp.where(lane == h, top, raw)
            raw = jnp.where(lane == 12 + h, jnp.concatenate(totals, axis=0), raw)
        hi, mid, low = split3(raw)
        stats = hi + pltpu.roll(mid, 4, 1) + pltpu.roll(low, 8, 1)
        for t in range(8):
            res[4, pl.ds(t, 64, stride=8), :] = stats[t * 64:(t + 1) * 64, :]
        for h in range(5):
            pack[b, :, :, h * 128:(h + 1) * 128] = res[h].astype(BF16).reshape(32, 16, 128)
        back.append(pltpu.make_async_copy(pack.at[b], out.at[:, pl.ds(b * 16, 16), :], sem.at[8 + b]))
        back[b].start()
    wait_all(back)
    wait_all(side_back)


def column_part(where, x_own, x_oth, w, side, parts, *after):
    return pl.pallas_call(
        functools.partial(col_kernel, len(w), parts),
        out_shape=(
            jax.ShapeDtypeStruct((32, 32, 640), BF16),
        )
        + (jax.ShapeDtypeStruct((side.shape[0] // parts, side.shape[1]), side.dtype),) * parts,
        in_specs=[SMEM_SPEC] + [HBM_SPEC] * (6 + len(w) + len(after)),
        out_specs=(ANY_SPEC,) * (1 + parts),
        scratch_shapes=[
            pltpu.VMEM((1024, 2048), BF16),
            pltpu.VMEM((3, 2048, 512), BF16),
            pltpu.VMEM((12, 512, 128), F32),
            pltpu.VMEM((4, 512, 128), BF16),
            pltpu.VMEM((4, 512, 128), BF16),
            pltpu.VMEM((4, 512, 256), BF16),
            pltpu.VMEM((5, 512, 128), F32),
            pltpu.VMEM((2, 32, 16, 640), BF16),
            pltpu.VMEM(side.shape, side.dtype),
            pltpu.SemaphoreType.DMA((10,)),
        ],
        cost_estimate=cost(4),
        compiler_params=pltpu.CompilerParams(vmem_limit_bytes=VMEM_LIMIT),
        name="column_part",
    )(where, x_own, *x_oth, *w, side, *after)


def load_piece(src, s, xs, row, sem):
    return pltpu.make_async_copy(src.at[:, pl.ds(s * 2048, 2048)], xs.at[s, pl.ds(row, 256), :], sem)


def load_parts(parts, s, xs, row, sem):
    n = parts[0].shape[0]
    return [
        pltpu.make_async_copy(src.at[:, pl.ds(s * 2048, 2048)], xs.at[s, pl.ds(row + i * n, n), :], sem)
        for i, src in enumerate(parts)
    ]


def project(x, w, s, dst, dst_row):
    res = dot(x, w).astype(BF16)
    for h in range(4):
        dst[s * 4 + h, dst_row:dst_row + 512, 0:128] = res[:, h * 128:(h + 1) * 128]


def row_kernel(nw, where, own, oth, *refs):
    w, refs = refs[:nw], refs[nw:]
    num, stats, aux, xs, ws, qs, ks, vs, acc, st_all, sem = refs[-11:]
    upper, core = where[0], where[1]
    with_low = ks.shape[1] == 1024
    base = 512 if with_low else 0
    own_row = pl.multiple_of(core * 256, 256)
    oth_row = pl.multiple_of((1 - core) * 256, 256)
    near = [
        [load_piece(own, s, xs, base + own_row, sem.at[3 + 2 * s]),
         load_piece(oth, s, xs, base + oth_row, sem.at[4 + 2 * s])]
        for s in range(2)
    ]
    vs[:, :, 128:256] = jnp.ones(vs.shape[:2] + (128,), BF16)
    weights = weight_copies(w, ws, sem, where)
    for c in near[0] + weights[0] + near[1] + weights[1] + weights[2]:
        c.start()
    if with_low:
        far = [
            [load_piece(refs[0], s, xs, own_row, sem.at[7 + 2 * s])]
            + load_parts(refs[1:5], s, xs, oth_row, sem.at[8 + 2 * s])
            for s in range(2)
        ]

        @pl.when(upper == 1)
        def _():
            for c in far[0] + far[1]:
                c.start()

    for j, (dst, dst_row) in enumerate(((qs, 0), (ks, base), (vs, base))):
        wait_all(weights[j])
        for s in range(2):
            if j == 0:
                wait_all(near[s])
            project(xs[s, base:base + 512, :], ws[j], s, dst, dst_row)
    if not with_low:
        extra = [pltpu.make_async_copy(qs, aux[0], sem.at[8])] + [
            pltpu.make_async_copy(xs.at[s, pl.ds(own_row, 256), :], aux[1].at[:, pl.ds(s * 2048, 2048)], sem.at[9 + s])
            for s in range(2)
        ]
        for c in extra:
            c.start()

    if with_low:
        @pl.when(upper == 1)
        def _():
            for s in range(2):
                wait_all(far[s])
                project(xs[s, 0:512, :], ws[1], s, ks, 0)
                project(xs[s, 0:512, :], ws[2], s, vs, 0)

    later = lax.broadcasted_iota(jnp.int32, (256, 256), 1) > lax.broadcasted_iota(jnp.int32, (256, 256), 0)
    lane = lax.broadcasted_iota(jnp.int32, (256, 128), 1)

    def attend(first):
        back = []
        for s in range(2):
            for blk in range(2):
                tile = core if blk == 0 else 1 - core
                st = jnp.zeros((256, 128), F32)
                for h in range(4):
                    i = s * 4 + h
                    q = qs[i, blk * 256:(blk + 1) * 256, :]
                    diag = base + blk * 256
                    sd = jnp.where(later, MASKED, dot_t(q, ks[i, diag:diag + 256, :]))
                    top = jnp.max(sd, axis=-1, keepdims=True)
                    if diag > first:
                        se = dot_t(q, ks[i, first:diag, :])
                        top = jnp.maximum(top, jnp.max(se, axis=-1, keepdims=True))
                    pd = jnp.exp2((sd - top) * EXP_SCALE)
                    part = dot(pd.astype(BF16), vs[i, diag:diag + 256, :])
                    if diag > first:
                        pe = jnp.exp2((se - top) * EXP_SCALE)
                        part += dot(pe.astype(BF16), vs[i, first:diag, :])
                    acc[blk, s, :, h * 128:(h + 1) * 128] = part[:, 0:128]
                    st = jnp.where(lane == h, top, st)
                    st = jnp.where(lane == 12 + h, part[:, 128:256], st)
                st_all[blk, s, :, :] = st
                n = 4 * s + 2 * blk
                back.append(pltpu.make_async_copy(acc.at[blk, s], num.at[tile, s], sem.at[11 + n]))
                back.append(pltpu.make_async_copy(st_all.at[blk, s], stats.at[tile, s], sem.at[12 + n]))
                back[-2].start()
                back[-1].start()
        wait_all(back)

    if with_low:
        @pl.when(upper == 0)
        def _():
            attend(512)

        @pl.when(upper == 1)
        def _():
            attend(0)
    else:
        attend(0)
        wait_all(extra)


ROW_SHAPES = (
    jax.ShapeDtypeStruct((2, 2, 256, 512), F32),
    jax.ShapeDtypeStruct((2, 2, 256, 128), F32),
)


def near_kernel(nw, where, own, oth, *refs):
    num, stats, q_out, own_out = refs[-12:-8]
    row_kernel(nw, where, own, oth, *refs[:-12], num, stats, (q_out, own_out), *refs[-8:])


def near_part(where, own, oth, w, *after):
    return pl.pallas_call(
        functools.partial(near_kernel, len(w)),
        out_shape=ROW_SHAPES
        + (jax.ShapeDtypeStruct((8, 512, 128), BF16), jax.ShapeDtypeStruct((256, 4096), BF16)),
        in_specs=[SMEM_SPEC] + [HBM_SPEC] * (2 + len(w) + len(after)),
        out_specs=(ANY_SPEC,) * 4,
        scratch_shapes=[
            pltpu.VMEM((2, 512, 2048), BF16),
            pltpu.VMEM((3, 2048, 512), BF16),
            pltpu.VMEM((8, 512, 128), BF16),
            pltpu.VMEM((8, 512, 128), BF16),
            pltpu.VMEM((8, 512, 256), BF16),
            pltpu.VMEM((2, 2, 256, 512), F32),
            pltpu.VMEM((2, 2, 256, 128), F32),
            pltpu.SemaphoreType.DMA((19,)),
        ],
        cost_estimate=cost(6),
        compiler_params=pltpu.CompilerParams(vmem_limit_bytes=VMEM_LIMIT),
        name="near_part",
    )(where, own, oth, *w, *after)


def full_kernel(nw, where, own, oth, *refs):
    num, stats = refs[-10:-8]
    row_kernel(nw, where, own, oth, *refs[:-10], num, stats, None, *refs[-8:])


def row_part(where, own, oth, low_own, low_oth, w, *after):
    return pl.pallas_call(
        functools.partial(full_kernel, len(w)),
        out_shape=ROW_SHAPES,
        in_specs=[SMEM_SPEC] + [HBM_SPEC] * (7 + len(w) + len(after)),
        out_specs=(ANY_SPEC, ANY_SPEC),
        scratch_shapes=[
            pltpu.VMEM((2, 1024, 2048), BF16),
            pltpu.VMEM((3, 2048, 512), BF16),
            pltpu.VMEM((8, 512, 128), BF16),
            pltpu.VMEM((8, 1024, 128), BF16),
            pltpu.VMEM((8, 1024, 256), BF16),
            pltpu.VMEM((2, 2, 256, 512), F32),
            pltpu.VMEM((2, 2, 256, 128), F32),
            pltpu.SemaphoreType.DMA((19,)),
        ],
        cost_estimate=cost(12),
        compiler_params=pltpu.CompilerParams(vmem_limit_bytes=VMEM_LIMIT),
        name="row_part",
    )(where, own, oth, *w, low_own, *low_oth, *after)


def far_kernel(where, low_own, *refs):
    low_oth, (w, q, num_in, stats_in), refs = refs[:4], refs[4:8], refs[8:]
    num, stats, xs, ws, qs, ks, vs, acc, st_all, sem = refs[-10:]
    upper, core = where[0], where[1]
    own_row = pl.multiple_of(core * 256, 256)
    oth_row = pl.multiple_of((1 - core) * 256, 256)

    @pl.when(upper == 1)
    def _():
        far = [
            [load_piece(low_own, s, xs, own_row, sem.at[2 * s])]
            + load_parts(low_oth, s, xs, oth_row, sem.at[1 + 2 * s])
            for s in range(2)
        ]
        weights = [pltpu.make_async_copy(w.at[j], ws.at[j - 1], sem.at[3 + j]) for j in (1, 2)]
        rest = [
            pltpu.make_async_copy(q, qs, sem.at[6]),
            pltpu.make_async_copy(num_in, acc, sem.at[7]),
            pltpu.make_async_copy(stats_in, st_all, sem.at[8]),
        ]
        for c in far[0] + weights[:1] + far[1] + weights[1:] + rest:
            c.start()
        vs[:, :, 128:256] = jnp.ones((8, 512, 128), BF16)
        for j, dst in enumerate((ks, vs)):
            weights[j].wait()
            for s in range(2):
                if j == 0:
                    wait_all(far[s])
                project(xs[s], ws[j], s, dst, 0)
        wait_all(rest)
        lane = lax.broadcasted_iota(jnp.int32, (256, 128), 1)
        back = []
        for s in range(2):
            for blk in range(2):
                tile = core if blk == 0 else 1 - core
                st = st_all[tile, s, :, :]
                new = st
                for h in range(4):
                    i = s * 4 + h
                    f = slice(h * 128, (h + 1) * 128)
                    scores = dot_t(qs[i, blk * 256:(blk + 1) * 256, :], ks[i])
                    near_top = st[:, h:h + 1]
                    top = jnp.maximum(near_top, jnp.max(scores, axis=-1, keepdims=True))
                    p = jnp.exp2((scores - top) * EXP_SCALE)
                    factor = jnp.exp2((near_top - top) * EXP_SCALE)
                    part = dot(p.astype(BF16), vs[i])
                    acc[tile, s, :, f] = acc[tile, s, :, f] * factor + part[:, 0:128]
                    new = jnp.where(lane == h, top, new)
                    new = jnp.where(lane == 12 + h, st * factor + part[:, 128:256], new)
                st_all[tile, s, :, :] = new
                n = 4 * s + 2 * blk
                back.append(pltpu.make_async_copy(acc.at[tile, s], num.at[tile, s], sem.at[9 + n]))
                back.append(pltpu.make_async_copy(st_all.at[tile, s], stats.at[tile, s], sem.at[10 + n]))
                back[-2].start()
                back[-1].start()
        wait_all(back)


def far_part(where, low_own, low_oth, w, q, num, stats, *after):
    return pl.pallas_call(
        far_kernel,
        out_shape=ROW_SHAPES,
        in_specs=[SMEM_SPEC] + [HBM_SPEC] * (9 + len(after)),
        out_specs=(ANY_SPEC, ANY_SPEC),
        scratch_shapes=[
            pltpu.VMEM((2, 512, 2048), BF16),
            pltpu.VMEM((2, 2048, 512), BF16),
            pltpu.VMEM((8, 512, 128), BF16),
            pltpu.VMEM((8, 512, 128), BF16),
            pltpu.VMEM((8, 512, 256), BF16),
            pltpu.VMEM((2, 2, 256, 512), F32),
            pltpu.VMEM((2, 2, 256, 128), F32),
            pltpu.SemaphoreType.DMA((17,)),
        ],
        input_output_aliases={8: 0, 9: 1},
        cost_estimate=cost(4),
        compiler_params=pltpu.CompilerParams(vmem_limit_bytes=VMEM_LIMIT),
        name="far_part",
    )(where, low_own, *low_oth, w, q, num, stats, *after)


def merge_kernel(parts, tiles, num_in, stats_in, col_in, *refs):
    if parts:
        side, refs, held = refs[0], refs[1:-1], refs[-1]
    outs, sides, (num, stats, col, done, sem) = refs[:len(tiles)], refs[len(tiles):-5], refs[-5:]
    def halves(tile):
        return pl.ds(tile * 16, 16)

    into = {
        tile: [pltpu.make_async_copy(col_in.at[:, halves(tile), :], col.at[:, halves(tile), :], sem.at[tile])]
        + [pltpu.make_async_copy(num_in.at[tile, s], num.at[tile, s], sem.at[2 + 2 * tile + s]) for s in range(2)]
        + [pltpu.make_async_copy(stats_in.at[tile, s], stats.at[tile, s], sem.at[2 + 2 * tile + s]) for s in range(2)]
        for tile in tiles
    }
    for tile in tiles:
        for c in into[tile]:
            c.start()
    if parts:
        side_in = pltpu.make_async_copy(side, held, sem.at[8])
        side_in.start()
    back = []
    for tile, out in zip(tiles, outs):
        wait_all(into[tile])
        both = col[:, tile * 16:(tile + 1) * 16, 512:640].astype(F32)
        for s in range(2):
            st = stats[tile, s, :, :]
            terms = both[:, s * 8:(s + 1) * 8, :].reshape(256, 128)
            cst = (terms + pltpu.roll(terms, 124, 1)) + pltpu.roll(terms, 120, 1)
            top = jnp.maximum(st, cst)
            row_factor = pltpu.roll(jnp.exp2((st - top) * EXP_SCALE), 12, 1)
            col_factor = pltpu.roll(jnp.exp2((cst - top) * EXP_SCALE), 12, 1)
            inverse = 1.0 / (st * row_factor + cst * col_factor)
            row_factor = row_factor * inverse
            col_factor = col_factor * inverse
            for h in range(4):
                f = slice(h * 128, (h + 1) * 128)
                cnum = col[:, tile * 16:(tile + 1) * 16, f].astype(F32)[:, s * 8:(s + 1) * 8, :].reshape(256, 128)
                value = num[tile, s, :, f] * row_factor[:, 12 + h:13 + h] + cnum * col_factor[:, 12 + h:13 + h]
                done[tile, s, :, f] = value.astype(BF16)
        back.append(pltpu.make_async_copy(done.at[tile], out, sem.at[6 + tile]))
        back[-1].start()
    if parts:
        side_in.wait()
        n = side.shape[0] // parts
        for i, to in enumerate(sides):
            back.append(pltpu.make_async_copy(held.at[pl.ds(i * n, n)], to, sem.at[9]))
            back[-1].start()
    wait_all(back)


def merge(num, stats, col, tiles, side=(), parts=0):
    shape = jax.ShapeDtypeStruct((2, 256, 512), BF16)
    side_shape = [jax.ShapeDtypeStruct((a.shape[0] // parts, a.shape[1]), a.dtype) for a in side] * parts
    return pl.pallas_call(
        functools.partial(merge_kernel, parts, tiles),
        out_shape=(shape,) * len(tiles) + (*side_shape,),
        in_specs=[HBM_SPEC] * (3 + len(side)),
        out_specs=(ANY_SPEC,) * (len(tiles) + parts),
        scratch_shapes=[
            pltpu.VMEM((2, 2, 256, 512), F32),
            pltpu.VMEM((2, 2, 256, 128), F32),
            pltpu.VMEM((32, 32, 640), BF16),
            pltpu.VMEM((2, 2, 256, 512), BF16),
            pltpu.SemaphoreType.DMA((10,)),
        ]
        + [pltpu.VMEM(a.shape, a.dtype) for a in side],
        cost_estimate=cost(2),
        compiler_params=pltpu.CompilerParams(vmem_limit_bytes=VMEM_LIMIT),
        name="merge",
    )(num, stats, col, *side)


def out_kernel(*refs):
    srcs, (out, att, ws, acc, sent, sem) = refs[:11], refs[11:]
    copies = []
    for i in range(4):
        copies.append([pltpu.make_async_copy(srcs[i], att.at[i], sem.at[2 * i])])
        if i < 3:
            copies[i].append(pltpu.make_async_copy(srcs[4 + i], ws.at[i], sem.at[2 * i + 1]))
    for i, part in enumerate(srcs[7:]):
        copies[3].append(pltpu.make_async_copy(part, ws.at[3, pl.ds(i * 128, 128), :], sem.at[7]))
    for c in copies[0] + copies[1] + copies[2] + copies[3]:
        c.start()
    for i in range(3):
        wait_all(copies[i])
        part = dot(att[i].reshape(512, 512), ws[i])
        acc[...] = part if i == 0 else acc[...] + part
    wait_all(copies[3])
    back = []
    for s in range(2):
        f = pl.ds(s * 2048, 2048)
        sent[:, f] = (acc[s * 256:(s + 1) * 256, :] + dot(att[3, s], ws[3])).astype(BF16)
        back.append(pltpu.make_async_copy(sent.at[:, f], out.at[:, f], sem.at[8 + s]))
        back[s].start()
    wait_all(back)


def output_part(attended, weights):
    any_spec = pl.BlockSpec(memory_space=pl.ANY)
    return pl.pallas_call(
        out_kernel,
        out_shape=jax.ShapeDtypeStruct((256, 4096), BF16),
        in_specs=[any_spec] * 11,
        out_specs=any_spec,
        scratch_shapes=[
            pltpu.VMEM((4, 2, 256, 512), BF16),
            pltpu.VMEM((4, 512, 2048), BF16),
            pltpu.VMEM((512, 2048), F32),
            pltpu.VMEM((256, 4096), BF16),
            pltpu.SemaphoreType.DMA((10,)),
        ],
        cost_estimate=cost(4),
        compiler_params=pltpu.CompilerParams(vmem_limit_bytes=VMEM_LIMIT),
        name="output_part",
    )(*attended, *weights)


def gate_kernel(*refs):
    pass


def gate(a, *after):
    return pl.pallas_call(
        gate_kernel,
        out_shape=jax.ShapeDtypeStruct(a.shape, a.dtype),
        in_specs=[ANY_SPEC] * (1 + len(after)),
        out_specs=ANY_SPEC,
        input_output_aliases={0: 0},
        name="gate",
    )(a, *after)


def core_swap(a):
    return lax.ppermute(a, "sp", CORE_PAIRS)


def core_swap_parts(a, parts=4):
    return [core_swap(part) for part in jnp.split(a, parts, axis=0)]


def to_segments(a):
    return lax.all_to_all(a, "seg", split_axis=0, concat_axis=0, tiled=True)


def from_neighbour(a):
    return lax.ppermute(a, ("seg", "sp"), NEIGHBOUR_PAIRS)


def ring_near(quarter, axis):
    return (
        lax.ppermute(quarter, "seg", MOVES[axis, -1]),
        lax.ppermute(quarter, "seg", MOVES[axis, 1]),
    )


def cut_kernel(*refs):
    n = (len(refs) - 3) // 2
    srcs, dsts, held, sem = refs[:n], refs[n + 1:2 * n + 1], refs[-2], refs[-1]
    load = [
        pltpu.make_async_copy(src.at[:, pl.ds(128 * (i % 2), 128), :], held.at[i], sem.at[i])
        for i, src in enumerate(srcs)
    ]
    store = [pltpu.make_async_copy(held.at[i], dst, sem.at[n + i]) for i, dst in enumerate(dsts)]
    for c in load:
        c.start()
    for i in range(n):
        load[i].wait()
        store[i].start()
    wait_all(store)


def cut(pieces, after):
    n = len(pieces)
    half = jax.ShapeDtypeStruct((3, 128, 512), BF16)
    return pl.pallas_call(
        cut_kernel,
        out_shape=(half,) * n,
        in_specs=[ANY_SPEC] * (n + 1),
        out_specs=(ANY_SPEC,) * n,
        scratch_shapes=[pltpu.VMEM((n, 3, 128, 512), BF16), pltpu.SemaphoreType.DMA((2 * n,))],
        cost_estimate=cost(0.5),
        compiler_params=pltpu.CompilerParams(vmem_limit_bytes=VMEM_LIMIT),
        name="cut",
    )(*pieces, after)


def ring_far(nxt, prev, axis):
    return (
        lax.ppermute(nxt, "seg", MOVES[axis, -1]),
        lax.ppermute(prev, "seg", MOVES[axis, 1]),
    )


def join_kernel(where, z_mine, z_pair, y_mine, y_pair, after, by_z, by_y, held, sem):
    load, store = [], []
    for i, (src, dst, own) in enumerate(
        ((z_mine, by_z, where[3]), (z_pair, by_z, 1 - where[3]), (y_mine, by_y, where[2]), (y_pair, by_y, 1 - where[2]))
    ):
        row = pl.multiple_of(lax.rem(own + 2, 2) * 128, 128)
        load.append(pltpu.make_async_copy(src, held.at[i], sem.at[i]))
        store.append(pltpu.make_async_copy(held.at[i], dst.at[:, pl.ds(row, 128), :], sem.at[4 + i]))
    for c in load:
        c.start()
    for i in range(4):
        load[i].wait()
        store[i].start()
    wait_all(store)


def other_quarters(w_qkv, where, z, y, after):
    def eighth(row):
        return from_neighbour(lax.dynamic_slice(w_qkv, (0, row, 0), (3, 128, 512)))

    z_mine, y_mine = eighth(z * 256 + y % 2 * 128), eighth(1024 + y * 256 + z % 2 * 128)
    z_pair, y_pair = lax.ppermute(z_mine, "seg", PAIRS["y"]), lax.ppermute(y_mine, "seg", PAIRS["z"])
    return pl.pallas_call(
        join_kernel,
        out_shape=(jax.ShapeDtypeStruct((3, 256, 512), BF16),) * 2,
        in_specs=[SMEM_SPEC] + [ANY_SPEC] * 5,
        out_specs=(ANY_SPEC,) * 2,
        scratch_shapes=[pltpu.VMEM((4, 3, 128, 512), BF16), pltpu.SemaphoreType.DMA((8,))],
        cost_estimate=cost(0.5),
        compiler_params=pltpu.CompilerParams(vmem_limit_bytes=VMEM_LIMIT),
        name="join",
    )(where, z_mine, z_pair, y_mine, y_pair, after)


def split_kernel(src, *refs):
    parts, (held, sem) = refs[-6:-2], refs[-2:]
    n = held.shape[0] // 4
    load = [pltpu.make_async_copy(src.at[pl.ds(i * n, n)], held.at[pl.ds(i * n, n)], sem.at[i]) for i in range(4)]
    store = [pltpu.make_async_copy(held.at[pl.ds(i * n, n)], to, sem.at[4 + i]) for i, to in enumerate(parts)]
    for c in load:
        c.start()
    for i in range(4):
        load[i].wait()
        store[i].start()
    wait_all(store)


def split_rows(a, *after):
    return pl.pallas_call(
        split_kernel,
        out_shape=(jax.ShapeDtypeStruct((a.shape[0] // 4, a.shape[1]), a.dtype),) * 4,
        in_specs=[ANY_SPEC] * (1 + len(after)),
        out_specs=(ANY_SPEC,) * 4,
        scratch_shapes=[pltpu.VMEM(a.shape, a.dtype), pltpu.SemaphoreType.DMA((8,))],
        cost_estimate=cost(0.5),
        compiler_params=pltpu.CompilerParams(vmem_limit_bytes=VMEM_LIMIT),
        name="split_rows",
    )(a, *after)


def shards(normed, w_qkv, w_out):
    seg, sp = lax.axis_index("seg"), lax.axis_index("sp")
    z, y = seg // (NXL * NY), seg % NY
    where = jnp.stack([sp // 2, sp % 2, z, y]).astype(jnp.int32)
    row_oth = core_swap(normed)
    num_own, stats_own, q_own, own_copy = near_part(where, normed, row_oth, [w_qkv])
    by_z, by_y = other_quarters(w_qkv, where, z, y, q_own)
    low_own = lax.ppermute(own_copy, "sp", LOWER_TO_UPPER)
    z_near, y_near = ring_near(by_z, "z"), ring_near(by_y, "y")
    by_offset = normed.reshape(32, 8, 2, 2048).transpose(0, 2, 1, 3).reshape(32, 16, 2048)
    col_own = gate(to_segments(by_offset).reshape(512, 2048), q_own)
    col_oth = core_swap_parts(col_own)
    col, out_copy = column_part(where, col_own, col_oth, [w_qkv], w_out, 1)
    halves = cut((*z_near, *y_near), col)
    z_far, y_far = ring_far(*halves[:2], "z"), ring_far(*halves[2:], "y")
    qkv_other = [by_z, *z_near, *z_far, by_y, *y_near, *y_far]
    low_oth_parts = split_rows(low_own, halves[0])
    low_oth = [core_swap(part) for part in low_oth_parts]
    num_own, stats_own = far_part(where, low_own, low_oth, w_qkv, q_own, num_own, stats_own)
    out_other = from_neighbour(gate(out_copy, low_oth_parts[0]))
    col_a = to_segments(gate(col, *z_far, *y_far, num_own))
    col, _ = column_part(where, col_own, col_oth, qkv_other, where.reshape(1, 4), 1, num_own)
    col_b = to_segments(col)
    oth_a, own_a, *out_parts = merge(num_own, stats_own, col_a, (1, 0), (out_other,), 4)
    recv_a = core_swap(oth_a)
    num, stats = row_part(where, normed, row_oth, low_own, low_oth, qkv_other, own_a)
    (oth_b,) = merge(num, stats, col_b, (1,))
    recv_b = core_swap(oth_b)
    (own_b,) = merge(num, stats, col_b, (0,))
    out_weights = (w_out, core_swap(w_out), out_other, *[core_swap(part) for part in out_parts])
    return output_part((own_a, recv_a, own_b, recv_b), out_weights)


def solution(mesh):
    in_specs = (P("sp", "seg"), P(None, None, "sp"), P("sp", None))
    return jax.shard_map(shards, mesh=mesh, in_specs=in_specs, out_specs=P("sp", "seg"), check_vma=False)
```

```python
import functools

import jax
import jax.numpy as jnp
from jax import lax
from jax.experimental import pallas as pl
from jax.experimental.pallas import tpu as pltpu
from jax.sharding import PartitionSpec as P

HEAD_DIM = 128
EXP_SCALE = HEAD_DIM ** (-0.5) * 1.4426950408889634
MASKED = -1e30
NZ, NXL, NY = 4, 2, 4
BF16, F32 = jnp.bfloat16, jnp.float32
VMEM_LIMIT = 58 * 1024 * 1024

CORE_PAIRS = [(0, 1), (1, 0), (2, 3), (3, 2)]
LOWER_TO_UPPER = [(0, 2), (1, 3)]


def seg_index(z, xl, y):
    return (z * NXL + xl) * NY + y


NEIGHBOUR_PAIRS = [
    (seg_index(z, xl, y) * 4 + xh * 2 + c, seg_index(z, 1 - xl, y) * 4 + (1 - xh) * 2 + c)
    for z in range(NZ)
    for xl in range(NXL)
    for y in range(NY)
    for xh in range(2)
    for c in range(2)
]
MOVES = {
    (axis, d): [
        (seg_index(z, xl, y), seg_index((z + d) % NZ, xl, y) if axis == "z" else seg_index(z, xl, (y + d) % NY))
        for z in range(NZ)
        for xl in range(NXL)
        for y in range(NY)
    ]
    for axis in "zy"
    for d in (1, -1)
}
PAIRS = {
    axis: [
        (seg_index(z, xl, y), seg_index(z ^ 1, xl, y) if axis == "z" else seg_index(z, xl, y ^ 1))
        for z in range(NZ)
        for xl in range(NXL)
        for y in range(NY)
    ]
    for axis in "zy"
}
PIECES = [(half, step, sub) for half in range(2) for step, sub in ((0, 0), (1, 0), (3, 0), (2, 0), (2, 1))]


ANY_SPEC = pl.BlockSpec(memory_space=pl.ANY)
HBM_SPEC = pl.BlockSpec(memory_space=pltpu.HBM)
SMEM_SPEC = pl.BlockSpec(memory_space=pltpu.SMEM)
VMEM_SPEC = pl.BlockSpec(memory_space=pltpu.VMEM)


def cost(us):
    return pl.CostEstimate(flops=int(us * 1e9), transcendentals=0, bytes_accessed=int(us * 1e6))


def dot(a, b):
    return jnp.dot(a, b, preferred_element_type=F32)


def dot_t(a, b):
    return lax.dot_general(a, b, (((1,), (1,)), ((), ())), preferred_element_type=F32)


def split3(v):
    hi = v.astype(BF16).astype(F32)
    rest = v - hi
    mid = rest.astype(BF16).astype(F32)
    return hi, mid, (rest - mid).astype(BF16).astype(F32)


def weight_copies(w, ws, sem, where):
    if len(w) == 1:
        return [[pltpu.make_async_copy(w[0].at[j], ws.at[j], sem.at[j])] for j in range(3)]
    copies = [[], [], []]
    for i, (piece, (half, step, sub)) in enumerate(zip(w, PIECES)):
        row = pl.multiple_of(half * 1024 + lax.rem(where[2 + half] + step, 4) * 256 + sub * 128, 128)
        for j in range(3):
            copies[j].append(
                pltpu.make_async_copy(
                    piece.at[j], ws.at[j, pl.ds(row, piece.shape[1]), :], sem.at[j]
                )
            )
    return copies


def wait_all(copies):
    for c in copies:
        c.wait()


def col_kernel(nw, parts, where, x0, *refs):
    x1, w, refs = refs[:4], refs[4:4 + nw], refs[4 + nw:]
    side, out, sides, (xs, ws, wide, qs, ks, vs, res, pack, held, sem) = (
        refs[0], refs[-11 - parts], refs[-10 - parts:-10], refs[-10:]
    )
    back = []
    copies_x = [
        [[pltpu.make_async_copy(x0.at[pl.ds(m, 256)], xs.at[pl.ds(m, 256)], sem.at[3 + m // 256])] for m in (0, 256)],
        [[pltpu.make_async_copy(x1[i], xs.at[pl.ds(512 + i * 128, 128)], sem.at[5 + i // 2]) for i in (m, m + 1)]
         for m in (0, 2)],
    ]
    copies_w = weight_copies(w, ws, sem, where)
    for c in copies_x[0][0] + copies_w[0] + copies_x[0][1] + copies_w[1] + copies_w[2]:
        c.start()
    for c in copies_x[1][0] + copies_x[1][1]:
        c.start()
    side_in = pltpu.make_async_copy(side, held, sem.at[7])
    rows = side.shape[0] // parts
    side_back = [
        pltpu.make_async_copy(held.at[pl.ds(i * rows, rows)], to, sem.at[7]) for i, to in enumerate(sides)
    ]
    side_in.start()
    row_seg = lax.broadcasted_iota(jnp.int32, (64, 64), 0)
    col_seg = lax.broadcasted_iota(jnp.int32, (64, 64), 1)
    bias = jnp.where(col_seg < row_seg, 0.0, MASKED)
    lane = lax.broadcasted_iota(jnp.int32, (512, 128), 1)
    vs[:, :, 128:256] = jnp.ones((4, 512, 128), BF16)
    for b in range(2):
        for j, dst in enumerate((qs, ks, vs)):
            if b == 0:
                wait_all(copies_w[j])
            for m in (0, 256):
                if j == 0:
                    wait_all(copies_x[b][m // 256])
                part = dot(xs[b * 512 + m:b * 512 + m + 256, :], ws[j])
                for h in range(4):
                    wide[j * 4 + h, m:m + 256, :] = part[:, h * 128:(h + 1) * 128]
        if b == 0:
            side_in.wait()
            for c in side_back:
                c.start()
        for j, dst in enumerate((qs, ks, vs)):
            for h in range(4):
                for t in range(8):
                    dst[h, t * 64:(t + 1) * 64, 0:128] = wide[j * 4 + h, pl.ds(t, 64, stride=8), :].astype(BF16)
        raw = jnp.zeros((512, 128), F32)
        for h in range(4):
            s = jnp.concatenate(
                [dot_t(qs[h, t * 64:(t + 1) * 64, :], ks[h, t * 64:(t + 1) * 64, :]) + bias for t in range(8)], axis=0
            )
            top = jnp.max(s, axis=-1, keepdims=True)
            p = jnp.exp2((s - top) * EXP_SCALE)
            p = p.astype(BF16)
            totals = []
            for t in range(8):
                part = dot(p[t * 64:(t + 1) * 64, :], vs[h, t * 64:(t + 1) * 64, :])
                res[h, pl.ds(t, 64, stride=8), :] = part[:, 0:128]
                totals.append(part[:, 128:256])
            raw = jnp.where(lane == h, top, raw)
            raw = jnp.where(lane == 12 + h, jnp.concatenate(totals, axis=0), raw)
        hi, mid, low = split3(raw)
        stats = hi + pltpu.roll(mid, 4, 1) + pltpu.roll(low, 8, 1)
        for t in range(8):
            res[4, pl.ds(t, 64, stride=8), :] = stats[t * 64:(t + 1) * 64, :]
        for h in range(5):
            pack[b, :, :, h * 128:(h + 1) * 128] = res[h].astype(BF16).reshape(32, 16, 128)
        back.append(pltpu.make_async_copy(pack.at[b], out.at[:, pl.ds(b * 16, 16), :], sem.at[8 + b]))
        back[b].start()
    wait_all(back)
    wait_all(side_back)


def column_part(where, x_own, x_oth, w, side, parts, *after):
    return pl.pallas_call(
        functools.partial(col_kernel, len(w), parts),
        out_shape=(
            jax.ShapeDtypeStruct((32, 32, 640), BF16),
        )
        + (jax.ShapeDtypeStruct((side.shape[0] // parts, side.shape[1]), side.dtype),) * parts,
        in_specs=[SMEM_SPEC] + [HBM_SPEC] * (6 + len(w) + len(after)),
        out_specs=(ANY_SPEC,) * (1 + parts),
        scratch_shapes=[
            pltpu.VMEM((1024, 2048), BF16),
            pltpu.VMEM((3, 2048, 512), BF16),
            pltpu.VMEM((12, 512, 128), F32),
            pltpu.VMEM((4, 512, 128), BF16),
            pltpu.VMEM((4, 512, 128), BF16),
            pltpu.VMEM((4, 512, 256), BF16),
            pltpu.VMEM((5, 512, 128), F32),
            pltpu.VMEM((2, 32, 16, 640), BF16),
            pltpu.VMEM(side.shape, side.dtype),
            pltpu.SemaphoreType.DMA((10,)),
        ],
        cost_estimate=cost(4),
        compiler_params=pltpu.CompilerParams(vmem_limit_bytes=VMEM_LIMIT),
        name="column_part",
    )(where, x_own, *x_oth, *w, side, *after)


def load_piece(src, s, xs, row, sem):
    return pltpu.make_async_copy(src.at[:, pl.ds(s * 2048, 2048)], xs.at[s, pl.ds(row, 256), :], sem)


def load_parts(parts, s, xs, row, sem):
    n = parts[0].shape[0]
    return [
        pltpu.make_async_copy(src.at[:, pl.ds(s * 2048, 2048)], xs.at[s, pl.ds(row + i * n, n), :], sem)
        for i, src in enumerate(parts)
    ]


def project(x, w, s, dst, dst_row):
    res = dot(x, w).astype(BF16)
    for h in range(4):
        dst[s * 4 + h, dst_row:dst_row + 512, 0:128] = res[:, h * 128:(h + 1) * 128]


def row_kernel(nw, where, own, oth, *refs):
    w, refs = refs[:nw], refs[nw:]
    num, stats, aux, xs, ws, qs, ks, vs, acc, st_all, sem = refs[-11:]
    upper, core = where[0], where[1]
    with_low = ks.shape[1] == 1024
    base = 512 if with_low else 0
    own_row = pl.multiple_of(core * 256, 256)
    oth_row = pl.multiple_of((1 - core) * 256, 256)
    near = [
        [load_piece(own, s, xs, base + own_row, sem.at[3 + 2 * s]),
         load_piece(oth, s, xs, base + oth_row, sem.at[4 + 2 * s])]
        for s in range(2)
    ]
    vs[:, :, 128:256] = jnp.ones(vs.shape[:2] + (128,), BF16)
    weights = weight_copies(w, ws, sem, where)
    for c in near[0] + weights[0] + near[1] + weights[1] + weights[2]:
        c.start()
    if with_low:
        far = [
            [load_piece(refs[0], s, xs, own_row, sem.at[7 + 2 * s])]
            + load_parts(refs[1:5], s, xs, oth_row, sem.at[8 + 2 * s])
            for s in range(2)
        ]

        @pl.when(upper == 1)
        def _():
            for c in far[0] + far[1]:
                c.start()

    for j, (dst, dst_row) in enumerate(((qs, 0), (ks, base), (vs, base))):
        wait_all(weights[j])
        for s in range(2):
            if j == 0:
                wait_all(near[s])
            project(xs[s, base:base + 512, :], ws[j], s, dst, dst_row)
    if not with_low:
        extra = [pltpu.make_async_copy(qs, aux[0], sem.at[8])] + [
            pltpu.make_async_copy(xs.at[s, pl.ds(own_row, 256), :], aux[1].at[:, pl.ds(s * 2048, 2048)], sem.at[9 + s])
            for s in range(2)
        ]
        for c in extra:
            c.start()

    if with_low:
        @pl.when(upper == 1)
        def _():
            for s in range(2):
                wait_all(far[s])
                project(xs[s, 0:512, :], ws[1], s, ks, 0)
                project(xs[s, 0:512, :], ws[2], s, vs, 0)

    later = lax.broadcasted_iota(jnp.int32, (256, 256), 1) > lax.broadcasted_iota(jnp.int32, (256, 256), 0)
    lane = lax.broadcasted_iota(jnp.int32, (256, 128), 1)

    def attend(first):
        back = []
        for s in range(2):
            for blk in range(2):
                tile = core if blk == 0 else 1 - core
                st = jnp.zeros((256, 128), F32)
                for h in range(4):
                    i = s * 4 + h
                    q = qs[i, blk * 256:(blk + 1) * 256, :]
                    diag = base + blk * 256
                    sd = jnp.where(later, MASKED, dot_t(q, ks[i, diag:diag + 256, :]))
                    top = jnp.max(sd, axis=-1, keepdims=True)
                    if diag > first:
                        se = dot_t(q, ks[i, first:diag, :])
                        top = jnp.maximum(top, jnp.max(se, axis=-1, keepdims=True))
                    pd = jnp.exp2((sd - top) * EXP_SCALE)
                    part = dot(pd.astype(BF16), vs[i, diag:diag + 256, :])
                    if diag > first:
                        pe = jnp.exp2((se - top) * EXP_SCALE)
                        part += dot(pe.astype(BF16), vs[i, first:diag, :])
                    acc[blk, s, :, h * 128:(h + 1) * 128] = part[:, 0:128]
                    st = jnp.where(lane == h, top, st)
                    st = jnp.where(lane == 12 + h, part[:, 128:256], st)
                st_all[blk, s, :, :] = st
                n = 4 * s + 2 * blk
                back.append(pltpu.make_async_copy(acc.at[blk, s], num.at[tile, s], sem.at[11 + n]))
                back.append(pltpu.make_async_copy(st_all.at[blk, s], stats.at[tile, s], sem.at[12 + n]))
                back[-2].start()
                back[-1].start()
        wait_all(back)

    if with_low:
        @pl.when(upper == 0)
        def _():
            attend(512)

        @pl.when(upper == 1)
        def _():
            attend(0)
    else:
        attend(0)
        wait_all(extra)


ROW_SHAPES = (
    jax.ShapeDtypeStruct((2, 2, 256, 512), F32),
    jax.ShapeDtypeStruct((2, 2, 256, 128), F32),
)


def near_kernel(nw, where, own, oth, *refs):
    num, stats, q_out, own_out = refs[-12:-8]
    row_kernel(nw, where, own, oth, *refs[:-12], num, stats, (q_out, own_out), *refs[-8:])


def near_part(where, own, oth, w, *after):
    return pl.pallas_call(
        functools.partial(near_kernel, len(w)),
        out_shape=ROW_SHAPES
        + (jax.ShapeDtypeStruct((8, 512, 128), BF16), jax.ShapeDtypeStruct((256, 4096), BF16)),
        in_specs=[SMEM_SPEC] + [HBM_SPEC] * (2 + len(w) + len(after)),
        out_specs=(ANY_SPEC,) * 4,
        scratch_shapes=[
            pltpu.VMEM((2, 512, 2048), BF16),
            pltpu.VMEM((3, 2048, 512), BF16),
            pltpu.VMEM((8, 512, 128), BF16),
            pltpu.VMEM((8, 512, 128), BF16),
            pltpu.VMEM((8, 512, 256), BF16),
            pltpu.VMEM((2, 2, 256, 512), F32),
            pltpu.VMEM((2, 2, 256, 128), F32),
            pltpu.SemaphoreType.DMA((19,)),
        ],
        cost_estimate=cost(6),
        compiler_params=pltpu.CompilerParams(vmem_limit_bytes=VMEM_LIMIT),
        name="near_part",
    )(where, own, oth, *w, *after)


def full_kernel(nw, where, own, oth, *refs):
    num, stats = refs[-10:-8]
    row_kernel(nw, where, own, oth, *refs[:-10], num, stats, None, *refs[-8:])


def row_part(where, own, oth, low_own, low_oth, w, *after):
    return pl.pallas_call(
        functools.partial(full_kernel, len(w)),
        out_shape=ROW_SHAPES,
        in_specs=[SMEM_SPEC] + [HBM_SPEC] * (7 + len(w) + len(after)),
        out_specs=(ANY_SPEC, ANY_SPEC),
        scratch_shapes=[
            pltpu.VMEM((2, 1024, 2048), BF16),
            pltpu.VMEM((3, 2048, 512), BF16),
            pltpu.VMEM((8, 512, 128), BF16),
            pltpu.VMEM((8, 1024, 128), BF16),
            pltpu.VMEM((8, 1024, 256), BF16),
            pltpu.VMEM((2, 2, 256, 512), F32),
            pltpu.VMEM((2, 2, 256, 128), F32),
            pltpu.SemaphoreType.DMA((19,)),
        ],
        cost_estimate=cost(12),
        compiler_params=pltpu.CompilerParams(vmem_limit_bytes=VMEM_LIMIT),
        name="row_part",
    )(where, own, oth, *w, low_own, *low_oth, *after)


def far_kernel(where, low_own, *refs):
    low_oth, (w, q, num_in, stats_in), refs = refs[:4], refs[4:8], refs[8:]
    num, stats, xs, ws, qs, ks, vs, acc, st_all, sem = refs[-10:]
    upper, core = where[0], where[1]
    own_row = pl.multiple_of(core * 256, 256)
    oth_row = pl.multiple_of((1 - core) * 256, 256)

    @pl.when(upper == 1)
    def _():
        far = [
            [load_piece(low_own, s, xs, own_row, sem.at[2 * s])]
            + load_parts(low_oth, s, xs, oth_row, sem.at[1 + 2 * s])
            for s in range(2)
        ]
        weights = [pltpu.make_async_copy(w.at[j], ws.at[j - 1], sem.at[3 + j]) for j in (1, 2)]
        rest = [
            pltpu.make_async_copy(q, qs, sem.at[6]),
            pltpu.make_async_copy(num_in, acc, sem.at[7]),
            pltpu.make_async_copy(stats_in, st_all, sem.at[8]),
        ]
        for c in far[0] + weights[:1] + far[1] + weights[1:] + rest:
            c.start()
        vs[:, :, 128:256] = jnp.ones((8, 512, 128), BF16)
        for j, dst in enumerate((ks, vs)):
            weights[j].wait()
            for s in range(2):
                if j == 0:
                    wait_all(far[s])
                project(xs[s], ws[j], s, dst, 0)
        wait_all(rest)
        lane = lax.broadcasted_iota(jnp.int32, (256, 128), 1)
        back = []
        for s in range(2):
            for blk in range(2):
                tile = core if blk == 0 else 1 - core
                st = st_all[tile, s, :, :]
                new = st
                for h in range(4):
                    i = s * 4 + h
                    f = slice(h * 128, (h + 1) * 128)
                    scores = dot_t(qs[i, blk * 256:(blk + 1) * 256, :], ks[i])
                    near_top = st[:, h:h + 1]
                    top = jnp.maximum(near_top, jnp.max(scores, axis=-1, keepdims=True))
                    p = jnp.exp2((scores - top) * EXP_SCALE)
                    factor = jnp.exp2((near_top - top) * EXP_SCALE)
                    part = dot(p.astype(BF16), vs[i])
                    acc[tile, s, :, f] = acc[tile, s, :, f] * factor + part[:, 0:128]
                    new = jnp.where(lane == h, top, new)
                    new = jnp.where(lane == 12 + h, st * factor + part[:, 128:256], new)
                st_all[tile, s, :, :] = new
                n = 4 * s + 2 * blk
                back.append(pltpu.make_async_copy(acc.at[tile, s], num.at[tile, s], sem.at[9 + n]))
                back.append(pltpu.make_async_copy(st_all.at[tile, s], stats.at[tile, s], sem.at[10 + n]))
                back[-2].start()
                back[-1].start()
        wait_all(back)


def far_part(where, low_own, low_oth, w, q, num, stats, *after):
    return pl.pallas_call(
        far_kernel,
        out_shape=ROW_SHAPES,
        in_specs=[SMEM_SPEC] + [HBM_SPEC] * (9 + len(after)),
        out_specs=(ANY_SPEC, ANY_SPEC),
        scratch_shapes=[
            pltpu.VMEM((2, 512, 2048), BF16),
            pltpu.VMEM((2, 2048, 512), BF16),
            pltpu.VMEM((8, 512, 128), BF16),
            pltpu.VMEM((8, 512, 128), BF16),
            pltpu.VMEM((8, 512, 256), BF16),
            pltpu.VMEM((2, 2, 256, 512), F32),
            pltpu.VMEM((2, 2, 256, 128), F32),
            pltpu.SemaphoreType.DMA((17,)),
        ],
        input_output_aliases={8: 0, 9: 1},
        cost_estimate=cost(4),
        compiler_params=pltpu.CompilerParams(vmem_limit_bytes=VMEM_LIMIT),
        name="far_part",
    )(where, low_own, *low_oth, w, q, num, stats, *after)


def merge_tile(num, stats, col, out):
    both = col[:, :, 512:640].astype(F32)
    for s in range(2):
        st = stats[s, :, :]
        terms = both[:, s * 8:(s + 1) * 8, :].reshape(256, 128)
        cst = (terms + pltpu.roll(terms, 124, 1)) + pltpu.roll(terms, 120, 1)
        top = jnp.maximum(st, cst)
        row_factor = pltpu.roll(jnp.exp2((st - top) * EXP_SCALE), 12, 1)
        col_factor = pltpu.roll(jnp.exp2((cst - top) * EXP_SCALE), 12, 1)
        inverse = 1.0 / (st * row_factor + cst * col_factor)
        row_factor = row_factor * inverse
        col_factor = col_factor * inverse
        for h in range(4):
            f = slice(h * 128, (h + 1) * 128)
            cnum = col[:, :, f].astype(F32)[:, s * 8:(s + 1) * 8, :].reshape(256, 128)
            value = num[s, :, f] * row_factor[:, 12 + h:13 + h] + cnum * col_factor[:, 12 + h:13 + h]
            out[s, :, f] = value.astype(BF16)


def merge_kernel(parts, tiles, n_after, num_in, stats_in, col_in, *refs):
    if parts:
        side, refs, held = refs[0], refs[1:-1], refs[-1]
    refs = refs[n_after:]
    outs, sides, (num, stats, col, done, sem) = refs[:len(tiles)], refs[len(tiles):-5], refs[-5:]
    def halves(tile):
        return pl.ds(tile * 16, 16)

    into = {
        tile: [pltpu.make_async_copy(col_in.at[:, halves(tile), :], col.at[:, halves(tile), :], sem.at[tile])]
        + [pltpu.make_async_copy(num_in.at[tile, s], num.at[tile, s], sem.at[2 + 2 * tile + s]) for s in range(2)]
        + [pltpu.make_async_copy(stats_in.at[tile, s], stats.at[tile, s], sem.at[2 + 2 * tile + s]) for s in range(2)]
        for tile in tiles
    }
    for tile in tiles:
        for c in into[tile]:
            c.start()
    if parts:
        side_in = pltpu.make_async_copy(side, held, sem.at[8])
        side_in.start()
    back = []
    for tile, out in zip(tiles, outs):
        wait_all(into[tile])
        merge_tile(num.at[tile], stats.at[tile], col.at[:, halves(tile), :], done.at[tile])
        back.append(pltpu.make_async_copy(done.at[tile], out, sem.at[6 + tile]))
        back[-1].start()
    if parts:
        side_in.wait()
        n = side.shape[0] // parts
        for i, to in enumerate(sides):
            back.append(pltpu.make_async_copy(held.at[pl.ds(i * n, n)], to, sem.at[9]))
            back[-1].start()
    wait_all(back)


def merge(num, stats, col, tiles, side=(), parts=0, after=()):
    shape = jax.ShapeDtypeStruct((2, 256, 512), BF16)
    side_shape = [jax.ShapeDtypeStruct((a.shape[0] // parts, a.shape[1]), a.dtype) for a in side] * parts
    return pl.pallas_call(
        functools.partial(merge_kernel, parts, tiles, len(after)),
        out_shape=(shape,) * len(tiles) + (*side_shape,),
        in_specs=[HBM_SPEC] * (3 + len(side) + len(after)),
        out_specs=(ANY_SPEC,) * (len(tiles) + parts),
        scratch_shapes=[
            pltpu.VMEM((2, 2, 256, 512), F32),
            pltpu.VMEM((2, 2, 256, 128), F32),
            pltpu.VMEM((32, 32, 640), BF16),
            pltpu.VMEM((2, 2, 256, 512), BF16),
            pltpu.SemaphoreType.DMA((10,)),
        ]
        + [pltpu.VMEM(a.shape, a.dtype) for a in side],
        cost_estimate=cost(2),
        compiler_params=pltpu.CompilerParams(vmem_limit_bytes=VMEM_LIMIT),
        name="merge",
    )(num, stats, col, *side, *after)


def out_kernel(own_a, recv_a, recv_b, num_in, stats_in, col_in, *refs):
    weights, (out, att, ws, acc, sent, num, stats, col, sem) = refs[:7], refs[7:]
    copies = [
        [pltpu.make_async_copy(own_a, att.at[0], sem.at[0])],
        [pltpu.make_async_copy(recv_a, att.at[1], sem.at[2])],
        [pltpu.make_async_copy(num_in.at[0], num, sem.at[4]),
         pltpu.make_async_copy(stats_in.at[0], stats, sem.at[10]),
         pltpu.make_async_copy(col_in.at[:, pl.ds(0, 16), :], col, sem.at[11])],
        [pltpu.make_async_copy(recv_b, att.at[3], sem.at[6])],
    ]
    for i in range(3):
        copies[i].append(pltpu.make_async_copy(weights[i], ws.at[i], sem.at[2 * i + 1]))
    for i, part in enumerate(weights[3:]):
        copies[3].append(pltpu.make_async_copy(part, ws.at[3, pl.ds(i * 128, 128), :], sem.at[7]))
    for c in copies[0] + copies[2][:3] + copies[1] + copies[2][3:] + copies[3]:
        c.start()
    for i in range(3):
        wait_all(copies[i])
        if i == 2:
            merge_tile(num, stats, col, att.at[2])
        part = dot(att[i].reshape(512, 512), ws[i])
        acc[...] = part if i == 0 else acc[...] + part
    wait_all(copies[3])
    back = []
    for s in range(2):
        f = pl.ds(s * 2048, 2048)
        sent[:, f] = (acc[s * 256:(s + 1) * 256, :] + dot(att[3, s], ws[3])).astype(BF16)
        back.append(pltpu.make_async_copy(sent.at[:, f], out.at[:, f], sem.at[8 + s]))
        back[s].start()
    wait_all(back)


def output_part(own_a, recv_a, recv_b, num, stats, col, weights):
    return pl.pallas_call(
        out_kernel,
        out_shape=jax.ShapeDtypeStruct((256, 4096), BF16),
        in_specs=[ANY_SPEC] * 13,
        out_specs=ANY_SPEC,
        scratch_shapes=[
            pltpu.VMEM((4, 2, 256, 512), BF16),
            pltpu.VMEM((4, 512, 2048), BF16),
            pltpu.VMEM((512, 2048), F32),
            pltpu.VMEM((256, 4096), BF16),
            pltpu.VMEM((2, 256, 512), F32),
            pltpu.VMEM((2, 256, 128), F32),
            pltpu.VMEM((32, 16, 640), BF16),
            pltpu.SemaphoreType.DMA((12,)),
        ],
        cost_estimate=cost(4),
        compiler_params=pltpu.CompilerParams(vmem_limit_bytes=VMEM_LIMIT),
        name="output_part",
    )(own_a, recv_a, recv_b, num, stats, col, *weights)


def gate_kernel(*refs):
    pass


def gate(a, *after):
    return pl.pallas_call(
        gate_kernel,
        out_shape=jax.ShapeDtypeStruct(a.shape, a.dtype),
        in_specs=[ANY_SPEC] * (1 + len(after)),
        out_specs=ANY_SPEC,
        input_output_aliases={0: 0},
        name="gate",
    )(a, *after)


def core_swap(a):
    return lax.ppermute(a, "sp", CORE_PAIRS)


def core_swap_parts(a, parts=4):
    return [core_swap(part) for part in jnp.split(a, parts, axis=0)]


def to_segments(a):
    return lax.all_to_all(a, "seg", split_axis=0, concat_axis=0, tiled=True)


def from_neighbour(a):
    return lax.ppermute(a, ("seg", "sp"), NEIGHBOUR_PAIRS)


def ring_near(quarter, axis):
    return (
        lax.ppermute(quarter, "seg", MOVES[axis, -1]),
        lax.ppermute(quarter, "seg", MOVES[axis, 1]),
    )


def cut_kernel(*refs):
    n = (len(refs) - 3) // 2
    srcs, dsts, held, sem = refs[:n], refs[n + 1:2 * n + 1], refs[-2], refs[-1]
    load = [
        pltpu.make_async_copy(src.at[:, pl.ds(128 * (i % 2), 128), :], held.at[i], sem.at[i])
        for i, src in enumerate(srcs)
    ]
    store = [pltpu.make_async_copy(held.at[i], dst, sem.at[n + i]) for i, dst in enumerate(dsts)]
    for c in load:
        c.start()
    for i in range(n):
        load[i].wait()
        store[i].start()
    wait_all(store)


def cut(pieces, after):
    n = len(pieces)
    half = jax.ShapeDtypeStruct((3, 128, 512), BF16)
    return pl.pallas_call(
        cut_kernel,
        out_shape=(half,) * n,
        in_specs=[ANY_SPEC] * (n + 1),
        out_specs=(ANY_SPEC,) * n,
        scratch_shapes=[pltpu.VMEM((n, 3, 128, 512), BF16), pltpu.SemaphoreType.DMA((2 * n,))],
        cost_estimate=cost(0.5),
        compiler_params=pltpu.CompilerParams(vmem_limit_bytes=VMEM_LIMIT),
        name="cut",
    )(*pieces, after)


def ring_far(nxt, prev, axis):
    return (
        lax.ppermute(nxt, "seg", MOVES[axis, -1]),
        lax.ppermute(prev, "seg", MOVES[axis, 1]),
    )


def join_kernel(where, z_mine, z_pair, y_mine, y_pair, after, by_z, by_y, held, sem):
    load, store = [], []
    for i, (src, dst, own) in enumerate(
        ((z_mine, by_z, where[3]), (z_pair, by_z, 1 - where[3]), (y_mine, by_y, where[2]), (y_pair, by_y, 1 - where[2]))
    ):
        row = pl.multiple_of(lax.rem(own + 2, 2) * 128, 128)
        load.append(pltpu.make_async_copy(src, held.at[i], sem.at[i]))
        store.append(pltpu.make_async_copy(held.at[i], dst.at[:, pl.ds(row, 128), :], sem.at[4 + i]))
    for c in load:
        c.start()
    for i in range(4):
        load[i].wait()
        store[i].start()
    wait_all(store)


def other_quarters(w_qkv, where, z, y, after):
    def eighth(row):
        return from_neighbour(lax.dynamic_slice(w_qkv, (0, row, 0), (3, 128, 512)))

    z_mine, y_mine = eighth(z * 256 + y % 2 * 128), eighth(1024 + y * 256 + z % 2 * 128)
    z_pair, y_pair = lax.ppermute(z_mine, "seg", PAIRS["y"]), lax.ppermute(y_mine, "seg", PAIRS["z"])
    return pl.pallas_call(
        join_kernel,
        out_shape=(jax.ShapeDtypeStruct((3, 256, 512), BF16),) * 2,
        in_specs=[SMEM_SPEC] + [ANY_SPEC] * 5,
        out_specs=(ANY_SPEC,) * 2,
        scratch_shapes=[pltpu.VMEM((4, 3, 128, 512), BF16), pltpu.SemaphoreType.DMA((8,))],
        cost_estimate=cost(0.5),
        compiler_params=pltpu.CompilerParams(vmem_limit_bytes=VMEM_LIMIT),
        name="join",
    )(where, z_mine, z_pair, y_mine, y_pair, after)


def split_kernel(src, *refs):
    parts, (held, sem) = refs[-6:-2], refs[-2:]
    n = held.shape[0] // 4
    load = [pltpu.make_async_copy(src.at[pl.ds(i * n, n)], held.at[pl.ds(i * n, n)], sem.at[i]) for i in range(4)]
    store = [pltpu.make_async_copy(held.at[pl.ds(i * n, n)], to, sem.at[4 + i]) for i, to in enumerate(parts)]
    for c in load:
        c.start()
    for i in range(4):
        load[i].wait()
        store[i].start()
    wait_all(store)


def split_rows(a, *after):
    return pl.pallas_call(
        split_kernel,
        out_shape=(jax.ShapeDtypeStruct((a.shape[0] // 4, a.shape[1]), a.dtype),) * 4,
        in_specs=[ANY_SPEC] * (1 + len(after)),
        out_specs=(ANY_SPEC,) * 4,
        scratch_shapes=[pltpu.VMEM(a.shape, a.dtype), pltpu.SemaphoreType.DMA((8,))],
        cost_estimate=cost(0.5),
        compiler_params=pltpu.CompilerParams(vmem_limit_bytes=VMEM_LIMIT),
        name="split_rows",
    )(a, *after)


def shards(normed, w_qkv, w_out):
    seg, sp = lax.axis_index("seg"), lax.axis_index("sp")
    z, y = seg // (NXL * NY), seg % NY
    where = jnp.stack([sp // 2, sp % 2, z, y]).astype(jnp.int32)
    row_oth = core_swap(normed)
    num_own, stats_own, q_own, own_copy = near_part(where, normed, row_oth, [w_qkv])
    by_z, by_y = other_quarters(w_qkv, where, z, y, q_own)
    low_own = lax.ppermute(own_copy, "sp", LOWER_TO_UPPER)
    z_near, y_near = ring_near(by_z, "z"), ring_near(by_y, "y")
    by_offset = normed.reshape(32, 8, 2, 2048).transpose(0, 2, 1, 3).reshape(32, 16, 2048)
    col_own = gate(to_segments(by_offset).reshape(512, 2048), q_own)
    col_oth = core_swap_parts(col_own)
    col, out_copy = column_part(where, col_own, col_oth, [w_qkv], w_out, 1)
    halves = cut((*z_near, *y_near), col)
    z_far, y_far = ring_far(*halves[:2], "z"), ring_far(*halves[2:], "y")
    qkv_other = [by_z, *z_near, *z_far, by_y, *y_near, *y_far]
    low_oth_parts = split_rows(low_own, halves[0])
    low_oth = [core_swap(part) for part in low_oth_parts]
    num_own, stats_own = far_part(where, low_own, low_oth, w_qkv, q_own, num_own, stats_own)
    out_other = from_neighbour(gate(out_copy, low_oth_parts[0]))
    col_a = to_segments(gate(col, *z_far, *y_far, num_own))
    col, _ = column_part(where, col_own, col_oth, qkv_other, where.reshape(1, 4), 1, num_own)
    col_b = to_segments(col)
    oth_a, own_a, *out_parts = merge(num_own, stats_own, col_a, (1, 0), (out_other,), 4, (col,))
    recv_a = core_swap(oth_a)
    swapped = [core_swap(part) for part in out_parts]
    num, stats = row_part(where, normed, row_oth, low_own, low_oth, qkv_other, own_a)
    (oth_b,) = merge(num, stats, col_b, (1,), after=(recv_a, *swapped))
    recv_b = core_swap(oth_b)
    out_weights = (w_out, core_swap(w_out), out_other, *swapped)
    return output_part(own_a, recv_a, recv_b, num, stats, col_b, out_weights)


def solution(mesh):
    in_specs = (P("sp", "seg"), P(None, None, "sp"), P("sp", None))
    return jax.shard_map(shards, mesh=mesh, in_specs=in_specs, out_specs=P("sp", "seg"), check_vma=False)
```

```python
import functools

import jax
import jax.numpy as jnp
from jax import lax
from jax.experimental import pallas as pl
from jax.experimental.pallas import tpu as pltpu
from jax.sharding import PartitionSpec as P

HEAD_DIM = 128
EXP_SCALE = HEAD_DIM ** (-0.5) * 1.4426950408889634
MASKED = -1e30
NZ, NXL, NY = 4, 2, 4
BF16, F32 = jnp.bfloat16, jnp.float32
VMEM_LIMIT = 58 * 1024 * 1024

CORE_PAIRS = [(0, 1), (1, 0), (2, 3), (3, 2)]
LOWER_TO_UPPER = [(0, 2), (1, 3)]


def seg_index(z, xl, y):
    return (z * NXL + xl) * NY + y


NEIGHBOUR_PAIRS = [
    (seg_index(z, xl, y) * 4 + xh * 2 + c, seg_index(z, 1 - xl, y) * 4 + (1 - xh) * 2 + c)
    for z in range(NZ)
    for xl in range(NXL)
    for y in range(NY)
    for xh in range(2)
    for c in range(2)
]
MOVES = {
    (axis, d): [
        (seg_index(z, xl, y), seg_index((z + d) % NZ, xl, y) if axis == "z" else seg_index(z, xl, (y + d) % NY))
        for z in range(NZ)
        for xl in range(NXL)
        for y in range(NY)
    ]
    for axis in "zy"
    for d in (1, -1)
}
PAIRS = {
    axis: [
        (seg_index(z, xl, y), seg_index(z ^ 1, xl, y) if axis == "z" else seg_index(z, xl, y ^ 1))
        for z in range(NZ)
        for xl in range(NXL)
        for y in range(NY)
    ]
    for axis in "zy"
}
PIECES = [(half, step, sub) for half in range(2) for step, sub in ((0, 0), (1, 0), (3, 0), (2, 0), (2, 1))]


ANY_SPEC = pl.BlockSpec(memory_space=pl.ANY)
HBM_SPEC = pl.BlockSpec(memory_space=pltpu.HBM)
SMEM_SPEC = pl.BlockSpec(memory_space=pltpu.SMEM)
VMEM_SPEC = pl.BlockSpec(memory_space=pltpu.VMEM)


def cost(us):
    return pl.CostEstimate(flops=int(us * 1e9), transcendentals=0, bytes_accessed=int(us * 1e6))


def dot(a, b):
    return jnp.dot(a, b, preferred_element_type=F32)


def dot_t(a, b):
    return lax.dot_general(a, b, (((1,), (1,)), ((), ())), preferred_element_type=F32)


def split3(v):
    hi = v.astype(BF16).astype(F32)
    rest = v - hi
    mid = rest.astype(BF16).astype(F32)
    return hi, mid, (rest - mid).astype(BF16).astype(F32)


def weight_copies(w, ws, sem, where):
    if len(w) == 1:
        return [[pltpu.make_async_copy(w[0].at[j], ws.at[j], sem.at[j])] for j in range(3)]
    copies = [[], [], []]
    for i, (piece, (half, step, sub)) in enumerate(zip(w, PIECES)):
        row = pl.multiple_of(half * 1024 + lax.rem(where[2 + half] + step, 4) * 256 + sub * 128, 128)
        for j in range(3):
            copies[j].append(
                pltpu.make_async_copy(
                    piece.at[j], ws.at[j, pl.ds(row, piece.shape[1]), :], sem.at[j]
                )
            )
    return copies


def wait_all(copies):
    for c in copies:
        c.wait()


def col_kernel(nw, parts, where, x0, *refs):
    x1, w, refs = refs[:4], refs[4:4 + nw], refs[4 + nw:]
    side, out, sides, (xs, ws, wide, qs, ks, vs, res, pack, held, sem) = (
        refs[0], refs[-11 - parts], refs[-10 - parts:-10], refs[-10:]
    )
    back = []
    copies_x = [
        [[pltpu.make_async_copy(x0.at[pl.ds(m, 256)], xs.at[pl.ds(m, 256)], sem.at[3 + m // 256])] for m in (0, 256)],
        [[pltpu.make_async_copy(x1[i], xs.at[pl.ds(512 + i * 128, 128)], sem.at[5 + i // 2]) for i in (m, m + 1)]
         for m in (0, 2)],
    ]
    copies_w = weight_copies(w, ws, sem, where)
    for c in copies_x[0][0] + copies_w[0] + copies_x[0][1] + copies_w[1] + copies_w[2]:
        c.start()
    for c in copies_x[1][0] + copies_x[1][1]:
        c.start()
    side_in = pltpu.make_async_copy(side, held, sem.at[7])
    rows = side.shape[0] // parts
    side_back = [
        pltpu.make_async_copy(held.at[pl.ds(i * rows, rows)], to, sem.at[7]) for i, to in enumerate(sides)
    ]
    side_in.start()
    row_seg = lax.broadcasted_iota(jnp.int32, (64, 64), 0)
    col_seg = lax.broadcasted_iota(jnp.int32, (64, 64), 1)
    bias = jnp.where(col_seg < row_seg, 0.0, MASKED)
    lane = lax.broadcasted_iota(jnp.int32, (512, 128), 1)
    vs[:, :, 128:256] = jnp.ones((4, 512, 128), BF16)
    for b in range(2):
        for j, dst in enumerate((qs, ks, vs)):
            if b == 0:
                wait_all(copies_w[j])
            for m in (0, 256):
                if j == 0:
                    wait_all(copies_x[b][m // 256])
                part = dot(xs[b * 512 + m:b * 512 + m + 256, :], ws[j])
                for h in range(4):
                    wide[j * 4 + h, m:m + 256, :] = part[:, h * 128:(h + 1) * 128]
        if b == 0:
            side_in.wait()
            for c in side_back:
                c.start()
        for j, dst in enumerate((qs, ks, vs)):
            for h in range(4):
                for t in range(8):
                    dst[h, t * 64:(t + 1) * 64, 0:128] = wide[j * 4 + h, pl.ds(t, 64, stride=8), :].astype(BF16)
        raw = jnp.zeros((512, 128), F32)
        for h in range(4):
            s = jnp.concatenate(
                [dot_t(qs[h, t * 64:(t + 1) * 64, :], ks[h, t * 64:(t + 1) * 64, :]) + bias for t in range(8)], axis=0
            )
            top = jnp.max(s, axis=-1, keepdims=True)
            p = jnp.exp2((s - top) * EXP_SCALE)
            p = p.astype(BF16)
            totals = []
            for t in range(8):
                part = dot(p[t * 64:(t + 1) * 64, :], vs[h, t * 64:(t + 1) * 64, :])
                res[h, pl.ds(t, 64, stride=8), :] = part[:, 0:128]
                totals.append(part[:, 128:256])
            raw = jnp.where(lane == h, top, raw)
            raw = jnp.where(lane == 12 + h, jnp.concatenate(totals, axis=0), raw)
        hi, mid, low = split3(raw)
        stats = hi + pltpu.roll(mid, 4, 1) + pltpu.roll(low, 8, 1)
        for t in range(8):
            res[4, pl.ds(t, 64, stride=8), :] = stats[t * 64:(t + 1) * 64, :]
        for h in range(5):
            pack[b, :, :, h * 128:(h + 1) * 128] = res[h].astype(BF16).reshape(32, 16, 128)
        back.append(pltpu.make_async_copy(pack.at[b], out.at[:, pl.ds(b * 16, 16), :], sem.at[8 + b]))
        back[b].start()
    wait_all(back)
    wait_all(side_back)


def column_part(where, x_own, x_oth, w, side, parts, *after):
    return pl.pallas_call(
        functools.partial(col_kernel, len(w), parts),
        out_shape=(
            jax.ShapeDtypeStruct((32, 32, 640), BF16),
        )
        + (jax.ShapeDtypeStruct((side.shape[0] // parts, side.shape[1]), side.dtype),) * parts,
        in_specs=[SMEM_SPEC] + [HBM_SPEC] * (6 + len(w) + len(after)),
        out_specs=(ANY_SPEC,) * (1 + parts),
        scratch_shapes=[
            pltpu.VMEM((1024, 2048), BF16),
            pltpu.VMEM((3, 2048, 512), BF16),
            pltpu.VMEM((12, 512, 128), F32),
            pltpu.VMEM((4, 512, 128), BF16),
            pltpu.VMEM((4, 512, 128), BF16),
            pltpu.VMEM((4, 512, 256), BF16),
            pltpu.VMEM((5, 512, 128), F32),
            pltpu.VMEM((2, 32, 16, 640), BF16),
            pltpu.VMEM(side.shape, side.dtype),
            pltpu.SemaphoreType.DMA((10,)),
        ],
        cost_estimate=cost(4),
        compiler_params=pltpu.CompilerParams(vmem_limit_bytes=VMEM_LIMIT),
        name="column_part",
    )(where, x_own, *x_oth, *w, side, *after)


def load_piece(src, s, xs, row, sem):
    return pltpu.make_async_copy(src.at[:, pl.ds(s * 2048, 2048)], xs.at[s, pl.ds(row, 256), :], sem)


def load_parts(parts, s, xs, row, sem):
    n = parts[0].shape[0]
    return [
        pltpu.make_async_copy(src.at[:, pl.ds(s * 2048, 2048)], xs.at[s, pl.ds(row + i * n, n), :], sem)
        for i, src in enumerate(parts)
    ]


def project(x, w, s, dst, dst_row):
    res = dot(x, w).astype(BF16)
    for h in range(4):
        dst[s * 4 + h, dst_row:dst_row + 512, 0:128] = res[:, h * 128:(h + 1) * 128]


def row_kernel(nw, where, own, oth, *refs):
    w, refs = refs[:nw], refs[nw:]
    num, stats, aux, xs, ws, qs, ks, vs, acc, st_all, sem = refs[-11:]
    upper, core = where[0], where[1]
    with_low = ks.shape[1] == 1024
    base = 512 if with_low else 0
    own_row = pl.multiple_of(core * 256, 256)
    oth_row = pl.multiple_of((1 - core) * 256, 256)
    near = [
        [load_piece(own, s, xs, base + own_row, sem.at[3 + 2 * s]),
         load_piece(oth, s, xs, base + oth_row, sem.at[4 + 2 * s])]
        for s in range(2)
    ]
    vs[:, :, 128:256] = jnp.ones(vs.shape[:2] + (128,), BF16)
    weights = weight_copies(w, ws, sem, where)
    for c in near[0] + weights[0] + near[1] + weights[1] + weights[2]:
        c.start()
    if with_low:
        far = [
            load_parts(refs[0:4], s, xs, own_row, sem.at[7 + 2 * s])
            + load_parts(refs[4:8], s, xs, oth_row, sem.at[8 + 2 * s])
            for s in range(2)
        ]

        @pl.when(upper == 1)
        def _():
            for c in far[0] + far[1]:
                c.start()

    for j, (dst, dst_row) in enumerate(((qs, 0), (ks, base), (vs, base))):
        wait_all(weights[j])
        for s in range(2):
            if j == 0:
                wait_all(near[s])
            project(xs[s, base:base + 512, :], ws[j], s, dst, dst_row)
    if not with_low:
        extra = [pltpu.make_async_copy(qs, aux[0], sem.at[8])] + [
            pltpu.make_async_copy(
                xs.at[s, pl.ds(own_row + i * 64, 64), :], aux[1 + i].at[:, pl.ds(s * 2048, 2048)], sem.at[9 + s]
            )
            for s in range(2)
            for i in range(4)
        ]
        for c in extra:
            c.start()

    if with_low:
        @pl.when(upper == 1)
        def _():
            for s in range(2):
                wait_all(far[s])
                project(xs[s, 0:512, :], ws[1], s, ks, 0)
                project(xs[s, 0:512, :], ws[2], s, vs, 0)

    later = lax.broadcasted_iota(jnp.int32, (256, 256), 1) > lax.broadcasted_iota(jnp.int32, (256, 256), 0)
    lane = lax.broadcasted_iota(jnp.int32, (256, 128), 1)

    def attend(first):
        back = []
        for s in range(2):
            for blk in range(2):
                tile = core if blk == 0 else 1 - core
                st = jnp.zeros((256, 128), F32)
                for h in range(4):
                    i = s * 4 + h
                    q = qs[i, blk * 256:(blk + 1) * 256, :]
                    diag = base + blk * 256
                    sd = jnp.where(later, MASKED, dot_t(q, ks[i, diag:diag + 256, :]))
                    top = jnp.max(sd, axis=-1, keepdims=True)
                    if diag > first:
                        se = dot_t(q, ks[i, first:diag, :])
                        top = jnp.maximum(top, jnp.max(se, axis=-1, keepdims=True))
                    pd = jnp.exp2((sd - top) * EXP_SCALE)
                    part = dot(pd.astype(BF16), vs[i, diag:diag + 256, :])
                    if diag > first:
                        pe = jnp.exp2((se - top) * EXP_SCALE)
                        part += dot(pe.astype(BF16), vs[i, first:diag, :])
                    acc[blk, s, :, h * 128:(h + 1) * 128] = part[:, 0:128]
                    st = jnp.where(lane == h, top, st)
                    st = jnp.where(lane == 12 + h, part[:, 128:256], st)
                st_all[blk, s, :, :] = st
                n = 4 * s + 2 * blk
                back.append(pltpu.make_async_copy(acc.at[blk, s], num.at[tile, s], sem.at[11 + n]))
                back.append(pltpu.make_async_copy(st_all.at[blk, s], stats.at[tile, s], sem.at[12 + n]))
                back[-2].start()
                back[-1].start()
        wait_all(back)

    if with_low:
        @pl.when(upper == 0)
        def _():
            attend(512)

        @pl.when(upper == 1)
        def _():
            attend(0)
    else:
        attend(0)
        wait_all(extra)


ROW_SHAPES = (
    jax.ShapeDtypeStruct((2, 2, 256, 512), F32),
    jax.ShapeDtypeStruct((2, 2, 256, 128), F32),
)


def near_kernel(nw, where, own, oth, *refs):
    num, stats, *aux = refs[-15:-8]
    row_kernel(nw, where, own, oth, *refs[:-15], num, stats, aux, *refs[-8:])


def near_part(where, own, oth, w, *after):
    return pl.pallas_call(
        functools.partial(near_kernel, len(w)),
        out_shape=ROW_SHAPES
        + (jax.ShapeDtypeStruct((8, 512, 128), BF16),)
        + (jax.ShapeDtypeStruct((64, 4096), BF16),) * 4,
        in_specs=[SMEM_SPEC] + [HBM_SPEC] * (2 + len(w) + len(after)),
        out_specs=(ANY_SPEC,) * 7,
        scratch_shapes=[
            pltpu.VMEM((2, 512, 2048), BF16),
            pltpu.VMEM((3, 2048, 512), BF16),
            pltpu.VMEM((8, 512, 128), BF16),
            pltpu.VMEM((8, 512, 128), BF16),
            pltpu.VMEM((8, 512, 256), BF16),
            pltpu.VMEM((2, 2, 256, 512), F32),
            pltpu.VMEM((2, 2, 256, 128), F32),
            pltpu.SemaphoreType.DMA((19,)),
        ],
        cost_estimate=cost(6),
        compiler_params=pltpu.CompilerParams(vmem_limit_bytes=VMEM_LIMIT),
        name="near_part",
    )(where, own, oth, *w, *after)


def full_kernel(nw, where, own, oth, *refs):
    num, stats = refs[-10:-8]
    row_kernel(nw, where, own, oth, *refs[:-10], num, stats, None, *refs[-8:])


def row_part(where, own, oth, low_own, low_oth, w, *after):
    return pl.pallas_call(
        functools.partial(full_kernel, len(w)),
        out_shape=ROW_SHAPES,
        in_specs=[SMEM_SPEC] + [HBM_SPEC] * (10 + len(w) + len(after)),
        out_specs=(ANY_SPEC, ANY_SPEC),
        scratch_shapes=[
            pltpu.VMEM((2, 1024, 2048), BF16),
            pltpu.VMEM((3, 2048, 512), BF16),
            pltpu.VMEM((8, 512, 128), BF16),
            pltpu.VMEM((8, 1024, 128), BF16),
            pltpu.VMEM((8, 1024, 256), BF16),
            pltpu.VMEM((2, 2, 256, 512), F32),
            pltpu.VMEM((2, 2, 256, 128), F32),
            pltpu.SemaphoreType.DMA((19,)),
        ],
        cost_estimate=cost(12),
        compiler_params=pltpu.CompilerParams(vmem_limit_bytes=VMEM_LIMIT),
        name="row_part",
    )(where, own, oth, *w, *low_own, *low_oth, *after)


def far_kernel(where, *refs):
    low_own, low_oth, (w, q, num_in, stats_in), refs = refs[:4], refs[4:8], refs[8:12], refs[12:]
    num, stats, xs, ws, qs, ks, vs, acc, st_all, sem = refs[-10:]
    upper, core = where[0], where[1]
    own_row = pl.multiple_of(core * 256, 256)
    oth_row = pl.multiple_of((1 - core) * 256, 256)

    @pl.when(upper == 1)
    def _():
        far = [
            load_parts(low_own, s, xs, own_row, sem.at[2 * s])
            + load_parts(low_oth, s, xs, oth_row, sem.at[1 + 2 * s])
            for s in range(2)
        ]
        weights = [pltpu.make_async_copy(w.at[j], ws.at[j - 1], sem.at[3 + j]) for j in (1, 2)]
        rest = [
            pltpu.make_async_copy(q, qs, sem.at[6]),
            pltpu.make_async_copy(num_in, acc, sem.at[7]),
            pltpu.make_async_copy(stats_in, st_all, sem.at[8]),
        ]
        for c in far[0] + weights[:1] + far[1] + weights[1:] + rest:
            c.start()
        vs[:, :, 128:256] = jnp.ones((8, 512, 128), BF16)
        for j, dst in enumerate((ks, vs)):
            weights[j].wait()
            for s in range(2):
                if j == 0:
                    wait_all(far[s])
                project(xs[s], ws[j], s, dst, 0)
        wait_all(rest)
        lane = lax.broadcasted_iota(jnp.int32, (256, 128), 1)
        back = []
        for s in range(2):
            for blk in range(2):
                tile = core if blk == 0 else 1 - core
                st = st_all[tile, s, :, :]
                new = st
                for h in range(4):
                    i = s * 4 + h
                    f = slice(h * 128, (h + 1) * 128)
                    scores = dot_t(qs[i, blk * 256:(blk + 1) * 256, :], ks[i])
                    near_top = st[:, h:h + 1]
                    top = jnp.maximum(near_top, jnp.max(scores, axis=-1, keepdims=True))
                    p = jnp.exp2((scores - top) * EXP_SCALE)
                    factor = jnp.exp2((near_top - top) * EXP_SCALE)
                    part = dot(p.astype(BF16), vs[i])
                    acc[tile, s, :, f] = acc[tile, s, :, f] * factor + part[:, 0:128]
                    new = jnp.where(lane == h, top, new)
                    new = jnp.where(lane == 12 + h, st * factor + part[:, 128:256], new)
                st_all[tile, s, :, :] = new
                n = 4 * s + 2 * blk
                back.append(pltpu.make_async_copy(acc.at[tile, s], num.at[tile, s], sem.at[9 + n]))
                back.append(pltpu.make_async_copy(st_all.at[tile, s], stats.at[tile, s], sem.at[10 + n]))
                back[-2].start()
                back[-1].start()
        wait_all(back)


def far_part(where, low_own, low_oth, w, q, num, stats, *after):
    return pl.pallas_call(
        far_kernel,
        out_shape=ROW_SHAPES,
        in_specs=[SMEM_SPEC] + [HBM_SPEC] * (12 + len(after)),
        out_specs=(ANY_SPEC, ANY_SPEC),
        scratch_shapes=[
            pltpu.VMEM((2, 512, 2048), BF16),
            pltpu.VMEM((2, 2048, 512), BF16),
            pltpu.VMEM((8, 512, 128), BF16),
            pltpu.VMEM((8, 512, 128), BF16),
            pltpu.VMEM((8, 512, 256), BF16),
            pltpu.VMEM((2, 2, 256, 512), F32),
            pltpu.VMEM((2, 2, 256, 128), F32),
            pltpu.SemaphoreType.DMA((17,)),
        ],
        input_output_aliases={11: 0, 12: 1},
        cost_estimate=cost(4),
        compiler_params=pltpu.CompilerParams(vmem_limit_bytes=VMEM_LIMIT),
        name="far_part",
    )(where, *low_own, *low_oth, w, q, num, stats, *after)


def merge_tile(num, stats, col, out):
    both = col[:, :, 512:640].astype(F32)
    for s in range(2):
        st = stats[s, :, :]
        terms = both[:, s * 8:(s + 1) * 8, :].reshape(256, 128)
        cst = (terms + pltpu.roll(terms, 124, 1)) + pltpu.roll(terms, 120, 1)
        top = jnp.maximum(st, cst)
        row_factor = pltpu.roll(jnp.exp2((st - top) * EXP_SCALE), 12, 1)
        col_factor = pltpu.roll(jnp.exp2((cst - top) * EXP_SCALE), 12, 1)
        inverse = 1.0 / (st * row_factor + cst * col_factor)
        row_factor = row_factor * inverse
        col_factor = col_factor * inverse
        for h in range(4):
            f = slice(h * 128, (h + 1) * 128)
            cnum = col[:, :, f].astype(F32)[:, s * 8:(s + 1) * 8, :].reshape(256, 128)
            value = num[s, :, f] * row_factor[:, 12 + h:13 + h] + cnum * col_factor[:, 12 + h:13 + h]
            out[s, :, f] = value.astype(BF16)


def merge_kernel(parts, tiles, n_after, num_in, stats_in, col_in, *refs):
    if parts:
        side, refs, held = refs[0], refs[1:-1], refs[-1]
    refs = refs[n_after:]
    outs, sides, (num, stats, col, done, sem) = refs[:len(tiles)], refs[len(tiles):-5], refs[-5:]
    def halves(tile):
        return pl.ds(tile * 16, 16)

    into = {
        tile: [pltpu.make_async_copy(col_in.at[:, halves(tile), :], col.at[:, halves(tile), :], sem.at[tile])]
        + [pltpu.make_async_copy(num_in.at[tile, s], num.at[tile, s], sem.at[2 + 2 * tile + s]) for s in range(2)]
        + [pltpu.make_async_copy(stats_in.at[tile, s], stats.at[tile, s], sem.at[2 + 2 * tile + s]) for s in range(2)]
        for tile in tiles
    }
    for tile in tiles:
        for c in into[tile]:
            c.start()
    if parts:
        side_in = pltpu.make_async_copy(side, held, sem.at[8])
        side_in.start()
    back = []
    for tile, out in zip(tiles, outs):
        wait_all(into[tile])
        merge_tile(num.at[tile], stats.at[tile], col.at[:, halves(tile), :], done.at[tile])
        back.append(pltpu.make_async_copy(done.at[tile], out, sem.at[6 + tile]))
        back[-1].start()
    if parts:
        side_in.wait()
        n = side.shape[0] // parts
        for i, to in enumerate(sides):
            back.append(pltpu.make_async_copy(held.at[pl.ds(i * n, n)], to, sem.at[9]))
            back[-1].start()
    wait_all(back)


def merge(num, stats, col, tiles, side=(), parts=0, after=()):
    shape = jax.ShapeDtypeStruct((2, 256, 512), BF16)
    side_shape = [jax.ShapeDtypeStruct((a.shape[0] // parts, a.shape[1]), a.dtype) for a in side] * parts
    return pl.pallas_call(
        functools.partial(merge_kernel, parts, tiles, len(after)),
        out_shape=(shape,) * len(tiles) + (*side_shape,),
        in_specs=[HBM_SPEC] * (3 + len(side) + len(after)),
        out_specs=(ANY_SPEC,) * (len(tiles) + parts),
        scratch_shapes=[
            pltpu.VMEM((2, 2, 256, 512), F32),
            pltpu.VMEM((2, 2, 256, 128), F32),
            pltpu.VMEM((32, 32, 640), BF16),
            pltpu.VMEM((2, 2, 256, 512), BF16),
            pltpu.SemaphoreType.DMA((10,)),
        ]
        + [pltpu.VMEM(a.shape, a.dtype) for a in side],
        cost_estimate=cost(2),
        compiler_params=pltpu.CompilerParams(vmem_limit_bytes=VMEM_LIMIT),
        name="merge",
    )(num, stats, col, *side, *after)


def out_kernel(own_a, recv_a, recv_b, num_in, stats_in, col_in, *refs):
    weights, (out, att, ws, acc, sent, num, stats, col, sem) = refs[:7], refs[7:]
    copies = [
        [pltpu.make_async_copy(own_a, att.at[0], sem.at[0])],
        [pltpu.make_async_copy(recv_a, att.at[1], sem.at[2])],
        [pltpu.make_async_copy(num_in.at[0], num, sem.at[4]),
         pltpu.make_async_copy(stats_in.at[0], stats, sem.at[10]),
         pltpu.make_async_copy(col_in.at[:, pl.ds(0, 16), :], col, sem.at[11])],
        [pltpu.make_async_copy(recv_b, att.at[3], sem.at[6])],
    ]
    for i in range(3):
        copies[i].append(pltpu.make_async_copy(weights[i], ws.at[i], sem.at[2 * i + 1]))
    for i, part in enumerate(weights[3:]):
        copies[3].append(pltpu.make_async_copy(part, ws.at[3, pl.ds(i * 128, 128), :], sem.at[7]))
    for c in copies[0] + copies[2][:3] + copies[1] + copies[2][3:] + copies[3]:
        c.start()
    for i in range(3):
        wait_all(copies[i])
        if i == 2:
            merge_tile(num, stats, col, att.at[2])
        part = dot(att[i].reshape(512, 512), ws[i])
        acc[...] = part if i == 0 else acc[...] + part
    wait_all(copies[3])
    back = []
    for s in range(2):
        f = pl.ds(s * 2048, 2048)
        sent[:, f] = (acc[s * 256:(s + 1) * 256, :] + dot(att[3, s], ws[3])).astype(BF16)
        back.append(pltpu.make_async_copy(sent.at[:, f], out.at[:, f], sem.at[8 + s]))
        back[s].start()
    wait_all(back)


def output_part(own_a, recv_a, recv_b, num, stats, col, weights):
    return pl.pallas_call(
        out_kernel,
        out_shape=jax.ShapeDtypeStruct((256, 4096), BF16),
        in_specs=[ANY_SPEC] * 13,
        out_specs=ANY_SPEC,
        scratch_shapes=[
            pltpu.VMEM((4, 2, 256, 512), BF16),
            pltpu.VMEM((4, 512, 2048), BF16),
            pltpu.VMEM((512, 2048), F32),
            pltpu.VMEM((256, 4096), BF16),
            pltpu.VMEM((2, 256, 512), F32),
            pltpu.VMEM((2, 256, 128), F32),
            pltpu.VMEM((32, 16, 640), BF16),
            pltpu.SemaphoreType.DMA((12,)),
        ],
        cost_estimate=cost(4),
        compiler_params=pltpu.CompilerParams(vmem_limit_bytes=VMEM_LIMIT),
        name="output_part",
    )(own_a, recv_a, recv_b, num, stats, col, *weights)


def gate_kernel(*refs):
    pass


def gate(a, *after):
    return pl.pallas_call(
        gate_kernel,
        out_shape=jax.ShapeDtypeStruct(a.shape, a.dtype),
        in_specs=[ANY_SPEC] * (1 + len(after)),
        out_specs=ANY_SPEC,
        input_output_aliases={0: 0},
        name="gate",
    )(a, *after)


def core_swap(a):
    return lax.ppermute(a, "sp", CORE_PAIRS)


def core_swap_parts(a, parts=4):
    return [core_swap(part) for part in jnp.split(a, parts, axis=0)]


def to_segments(a):
    return lax.all_to_all(a, "seg", split_axis=0, concat_axis=0, tiled=True)


def from_neighbour(a):
    return lax.ppermute(a, ("seg", "sp"), NEIGHBOUR_PAIRS)


def ring_near(quarter, axis):
    return (
        lax.ppermute(quarter, "seg", MOVES[axis, -1]),
        lax.ppermute(quarter, "seg", MOVES[axis, 1]),
    )


def cut_kernel(*refs):
    n = (len(refs) - 3) // 2
    srcs, dsts, held, sem = refs[:n], refs[n + 1:2 * n + 1], refs[-2], refs[-1]
    load = [
        pltpu.make_async_copy(src.at[:, pl.ds(128 * (i % 2), 128), :], held.at[i], sem.at[i])
        for i, src in enumerate(srcs)
    ]
    store = [pltpu.make_async_copy(held.at[i], dst, sem.at[n + i]) for i, dst in enumerate(dsts)]
    for c in load:
        c.start()
    for i in range(n):
        load[i].wait()
        store[i].start()
    wait_all(store)


def cut(pieces, after):
    n = len(pieces)
    half = jax.ShapeDtypeStruct((3, 128, 512), BF16)
    return pl.pallas_call(
        cut_kernel,
        out_shape=(half,) * n,
        in_specs=[ANY_SPEC] * (n + 1),
        out_specs=(ANY_SPEC,) * n,
        scratch_shapes=[pltpu.VMEM((n, 3, 128, 512), BF16), pltpu.SemaphoreType.DMA((2 * n,))],
        cost_estimate=cost(0.5),
        compiler_params=pltpu.CompilerParams(vmem_limit_bytes=VMEM_LIMIT),
        name="cut",
    )(*pieces, after)


def ring_far(nxt, prev, axis):
    return (
        lax.ppermute(nxt, "seg", MOVES[axis, -1]),
        lax.ppermute(prev, "seg", MOVES[axis, 1]),
    )


def join_kernel(where, z_mine, z_pair, y_mine, y_pair, after, by_z, by_y, held, sem):
    load, store = [], []
    for i, (src, dst, own) in enumerate(
        ((z_mine, by_z, where[3]), (z_pair, by_z, 1 - where[3]), (y_mine, by_y, where[2]), (y_pair, by_y, 1 - where[2]))
    ):
        row = pl.multiple_of(lax.rem(own + 2, 2) * 128, 128)
        load.append(pltpu.make_async_copy(src, held.at[i], sem.at[i]))
        store.append(pltpu.make_async_copy(held.at[i], dst.at[:, pl.ds(row, 128), :], sem.at[4 + i]))
    for c in load:
        c.start()
    for i in range(4):
        load[i].wait()
        store[i].start()
    wait_all(store)


def other_quarters(w_qkv, where, z, y, after):
    def eighth(row):
        return from_neighbour(lax.dynamic_slice(w_qkv, (0, row, 0), (3, 128, 512)))

    z_mine, y_mine = eighth(z * 256 + y % 2 * 128), eighth(1024 + y * 256 + z % 2 * 128)
    z_pair, y_pair = lax.ppermute(z_mine, "seg", PAIRS["y"]), lax.ppermute(y_mine, "seg", PAIRS["z"])
    return pl.pallas_call(
        join_kernel,
        out_shape=(jax.ShapeDtypeStruct((3, 256, 512), BF16),) * 2,
        in_specs=[SMEM_SPEC] + [ANY_SPEC] * 5,
        out_specs=(ANY_SPEC,) * 2,
        scratch_shapes=[pltpu.VMEM((4, 3, 128, 512), BF16), pltpu.SemaphoreType.DMA((8,))],
        cost_estimate=cost(0.5),
        compiler_params=pltpu.CompilerParams(vmem_limit_bytes=VMEM_LIMIT),
        name="join",
    )(where, z_mine, z_pair, y_mine, y_pair, after)


def shards(normed, w_qkv, w_out):
    seg, sp = lax.axis_index("seg"), lax.axis_index("sp")
    z, y = seg // (NXL * NY), seg % NY
    where = jnp.stack([sp // 2, sp % 2, z, y]).astype(jnp.int32)
    row_oth = core_swap(normed)
    num_own, stats_own, q_own, *own_parts = near_part(where, normed, row_oth, [w_qkv])
    by_z, by_y = other_quarters(w_qkv, where, z, y, q_own)
    low_own = [lax.ppermute(part, "sp", LOWER_TO_UPPER) for part in own_parts]
    z_near, y_near = ring_near(by_z, "z"), ring_near(by_y, "y")
    by_offset = normed.reshape(32, 8, 2, 2048).transpose(0, 2, 1, 3).reshape(32, 16, 2048)
    col_own = gate(to_segments(by_offset).reshape(512, 2048), q_own)
    col_oth = core_swap_parts(col_own)
    col, out_copy = column_part(where, col_own, col_oth, [w_qkv], w_out, 1)
    halves = cut((*z_near, *y_near), col)
    z_far, y_far = ring_far(*halves[:2], "z"), ring_far(*halves[2:], "y")
    qkv_other = [by_z, *z_near, *z_far, by_y, *y_near, *y_far]
    low_own = [gate(part, halves[0]) for part in low_own]
    low_oth = [core_swap(part) for part in low_own]
    num_own, stats_own = far_part(where, low_own, low_oth, w_qkv, q_own, num_own, stats_own)
    out_other = from_neighbour(gate(out_copy, low_own[3]))
    col_a = to_segments(gate(col, *z_far, *y_far, num_own))
    col, _ = column_part(where, col_own, col_oth, qkv_other, where.reshape(1, 4), 1, num_own)
    col_b = to_segments(col)
    oth_a, own_a, *out_parts = merge(num_own, stats_own, col_a, (1, 0), (out_other,), 4, (col,))
    recv_a = core_swap(oth_a)
    swapped = [core_swap(part) for part in out_parts]
    num, stats = row_part(where, normed, row_oth, low_own, low_oth, qkv_other, own_a)
    (oth_b,) = merge(num, stats, col_b, (1,), after=(recv_a, *swapped))
    recv_b = core_swap(oth_b)
    out_weights = (w_out, core_swap(w_out), out_other, *swapped)
    return output_part(own_a, recv_a, recv_b, num, stats, col_b, out_weights)


def solution(mesh):
    in_specs = (P("sp", "seg"), P(None, None, "sp"), P("sp", None))
    return jax.shard_map(shards, mesh=mesh, in_specs=in_specs, out_specs=P("sp", "seg"), check_vma=False)
```

```python
import functools

import jax
import jax.numpy as jnp
from jax import lax
from jax.experimental import pallas as pl
from jax.experimental.pallas import tpu as pltpu
from jax.sharding import PartitionSpec as P

HEAD_DIM = 128
EXP_SCALE = HEAD_DIM ** (-0.5) * 1.4426950408889634
MASKED = -1e30
NZ, NXL, NY = 4, 2, 4
BF16, F32 = jnp.bfloat16, jnp.float32
VMEM_LIMIT = 58 * 1024 * 1024

CORE_PAIRS = [(0, 1), (1, 0), (2, 3), (3, 2)]
LOWER_TO_UPPER = [(0, 2), (1, 3)]


def seg_index(z, xl, y):
    return (z * NXL + xl) * NY + y


NEIGHBOUR_PAIRS = [
    (seg_index(z, xl, y) * 4 + xh * 2 + c, seg_index(z, 1 - xl, y) * 4 + (1 - xh) * 2 + c)
    for z in range(NZ)
    for xl in range(NXL)
    for y in range(NY)
    for xh in range(2)
    for c in range(2)
]
MOVES = {
    (axis, d): [
        (seg_index(z, xl, y), seg_index((z + d) % NZ, xl, y) if axis == "z" else seg_index(z, xl, (y + d) % NY))
        for z in range(NZ)
        for xl in range(NXL)
        for y in range(NY)
    ]
    for axis in "zy"
    for d in (1, -1)
}
PAIRS = {
    axis: [
        (seg_index(z, xl, y), seg_index(z ^ 1, xl, y) if axis == "z" else seg_index(z, xl, y ^ 1))
        for z in range(NZ)
        for xl in range(NXL)
        for y in range(NY)
    ]
    for axis in "zy"
}
PIECES = [(half, step, sub) for half in range(2) for step, sub in ((0, 0), (1, 0), (3, 0), (2, 0), (2, 1))]


ANY_SPEC = pl.BlockSpec(memory_space=pl.ANY)
HBM_SPEC = pl.BlockSpec(memory_space=pltpu.HBM)
SMEM_SPEC = pl.BlockSpec(memory_space=pltpu.SMEM)
VMEM_SPEC = pl.BlockSpec(memory_space=pltpu.VMEM)


def cost(us):
    return pl.CostEstimate(flops=int(us * 1e9), transcendentals=0, bytes_accessed=int(us * 1e6))


def dot(a, b):
    return jnp.dot(a, b, preferred_element_type=F32)


def dot_t(a, b):
    return lax.dot_general(a, b, (((1,), (1,)), ((), ())), preferred_element_type=F32)


def split3(v):
    hi = v.astype(BF16).astype(F32)
    rest = v - hi
    mid = rest.astype(BF16).astype(F32)
    return hi, mid, (rest - mid).astype(BF16).astype(F32)


def weight_copies(w, ws, sem, where):
    if len(w) == 1:
        return [[pltpu.make_async_copy(w[0].at[j], ws.at[j], sem.at[j])] for j in range(3)]
    copies = [[], [], []]
    for i, (piece, (half, step, sub)) in enumerate(zip(w, PIECES)):
        row = pl.multiple_of(half * 1024 + lax.rem(where[2 + half] + step, 4) * 256 + sub * 128, 128)
        for j in range(3):
            copies[j].append(
                pltpu.make_async_copy(
                    piece.at[j], ws.at[j, pl.ds(row, piece.shape[1]), :], sem.at[j]
                )
            )
    return copies


def wait_all(copies):
    for c in copies:
        c.wait()


def col_kernel(nw, parts, where, x0, *refs):
    x1, w, refs = refs[:4], refs[4:4 + nw], refs[4 + nw:]
    side, out, sides, (xs, ws, wide, qs, ks, vs, res, pack, held, sem) = (
        refs[0], refs[-11 - parts], refs[-10 - parts:-10], refs[-10:]
    )
    back = []
    copies_x = [
        [[pltpu.make_async_copy(x0.at[pl.ds(m, 256)], xs.at[pl.ds(m, 256)], sem.at[3 + m // 256])] for m in (0, 256)],
        [[pltpu.make_async_copy(x1[i], xs.at[pl.ds(512 + i * 128, 128)], sem.at[5 + i // 2]) for i in (m, m + 1)]
         for m in (0, 2)],
    ]
    copies_w = weight_copies(w, ws, sem, where)
    for c in copies_x[0][0] + copies_w[0] + copies_x[0][1] + copies_w[1] + copies_w[2]:
        c.start()
    for c in copies_x[1][0] + copies_x[1][1]:
        c.start()
    side_in = pltpu.make_async_copy(side, held, sem.at[7])
    rows = side.shape[0] // parts
    side_back = [
        pltpu.make_async_copy(held.at[pl.ds(i * rows, rows)], to, sem.at[7]) for i, to in enumerate(sides)
    ]
    side_in.start()
    row_seg = lax.broadcasted_iota(jnp.int32, (64, 64), 0)
    col_seg = lax.broadcasted_iota(jnp.int32, (64, 64), 1)
    bias = jnp.where(col_seg < row_seg, 0.0, MASKED)
    lane = lax.broadcasted_iota(jnp.int32, (512, 128), 1)
    vs[:, :, 128:256] = jnp.ones((4, 512, 128), BF16)
    for b in range(2):
        for j, dst in enumerate((qs, ks, vs)):
            if b == 0:
                wait_all(copies_w[j])
            for m in (0, 256):
                if j == 0:
                    wait_all(copies_x[b][m // 256])
                part = dot(xs[b * 512 + m:b * 512 + m + 256, :], ws[j])
                for h in range(4):
                    wide[j * 4 + h, m:m + 256, :] = part[:, h * 128:(h + 1) * 128]
        if b == 0:
            side_in.wait()
            for c in side_back:
                c.start()
        for j, dst in enumerate((qs, ks, vs)):
            for h in range(4):
                for t in range(8):
                    dst[h, t * 64:(t + 1) * 64, 0:128] = wide[j * 4 + h, pl.ds(t, 64, stride=8), :].astype(BF16)
        raw = jnp.zeros((512, 128), F32)
        for h in range(4):
            s = jnp.concatenate(
                [dot_t(qs[h, t * 64:(t + 1) * 64, :], ks[h, t * 64:(t + 1) * 64, :]) + bias for t in range(8)], axis=0
            )
            top = jnp.max(s, axis=-1, keepdims=True)
            p = jnp.exp2((s - top) * EXP_SCALE)
            p = p.astype(BF16)
            totals = []
            for t in range(8):
                part = dot(p[t * 64:(t + 1) * 64, :], vs[h, t * 64:(t + 1) * 64, :])
                res[h, pl.ds(t, 64, stride=8), :] = part[:, 0:128]
                totals.append(part[:, 128:256])
            raw = jnp.where(lane == h, top, raw)
            raw = jnp.where(lane == 12 + h, jnp.concatenate(totals, axis=0), raw)
        hi, mid, low = split3(raw)
        stats = hi + pltpu.roll(mid, 4, 1) + pltpu.roll(low, 8, 1)
        for t in range(8):
            res[4, pl.ds(t, 64, stride=8), :] = stats[t * 64:(t + 1) * 64, :]
        for h in range(5):
            pack[b, :, :, h * 128:(h + 1) * 128] = res[h].astype(BF16).reshape(32, 16, 128)
        back.append(pltpu.make_async_copy(pack.at[b], out.at[:, pl.ds(b * 16, 16), :], sem.at[8 + b]))
        back[b].start()
    wait_all(back)
    wait_all(side_back)


def column_part(where, x_own, x_oth, w, side, parts, *after):
    return pl.pallas_call(
        functools.partial(col_kernel, len(w), parts),
        out_shape=(
            jax.ShapeDtypeStruct((32, 32, 640), BF16),
        )
        + (jax.ShapeDtypeStruct((side.shape[0] // parts, side.shape[1]), side.dtype),) * parts,
        in_specs=[SMEM_SPEC] + [HBM_SPEC] * (6 + len(w) + len(after)),
        out_specs=(ANY_SPEC,) * (1 + parts),
        scratch_shapes=[
            pltpu.VMEM((1024, 2048), BF16),
            pltpu.VMEM((3, 2048, 512), BF16),
            pltpu.VMEM((12, 512, 128), F32),
            pltpu.VMEM((4, 512, 128), BF16),
            pltpu.VMEM((4, 512, 128), BF16),
            pltpu.VMEM((4, 512, 256), BF16),
            pltpu.VMEM((5, 512, 128), F32),
            pltpu.VMEM((2, 32, 16, 640), BF16),
            pltpu.VMEM(side.shape, side.dtype),
            pltpu.SemaphoreType.DMA((10,)),
        ],
        cost_estimate=cost(4),
        compiler_params=pltpu.CompilerParams(vmem_limit_bytes=VMEM_LIMIT),
        name="column_part",
    )(where, x_own, *x_oth, *w, side, *after)


def load_piece(src, s, xs, row, sem):
    return pltpu.make_async_copy(src.at[:, pl.ds(s * 2048, 2048)], xs.at[s, pl.ds(row, 256), :], sem)


def load_parts(parts, s, xs, row, sem):
    n = parts[0].shape[0]
    return [
        pltpu.make_async_copy(src.at[:, pl.ds(s * 2048, 2048)], xs.at[s, pl.ds(row + i * n, n), :], sem)
        for i, src in enumerate(parts)
    ]


def project(x, w, s, dst, dst_row):
    res = dot(x, w).astype(BF16)
    for h in range(4):
        dst[s * 4 + h, dst_row:dst_row + 512, 0:128] = res[:, h * 128:(h + 1) * 128]


def row_kernel(nw, where, own, oth, *refs):
    w, refs = refs[:nw], refs[nw:]
    num, stats, aux, xs, ws, qs, ks, vs, acc, st_all, sem = refs[-11:]
    upper, core = where[0], where[1]
    with_low = ks.shape[1] == 1024
    base = 512 if with_low else 0
    own_row = pl.multiple_of(core * 256, 256)
    oth_row = pl.multiple_of((1 - core) * 256, 256)
    near = [
        [load_piece(own, s, xs, base + own_row, sem.at[3 + 2 * s]),
         load_piece(oth, s, xs, base + oth_row, sem.at[4 + 2 * s])]
        for s in range(2)
    ]
    vs[:, :, 128:256] = jnp.ones(vs.shape[:2] + (128,), BF16)
    weights = weight_copies(w, ws, sem, where)
    for c in near[0] + weights[0] + near[1] + weights[1] + weights[2]:
        c.start()
    if with_low:
        far = [
            [load_piece(refs[0], s, xs, own_row, sem.at[7 + 2 * s])]
            + load_parts(refs[1:5], s, xs, oth_row, sem.at[8 + 2 * s])
            for s in range(2)
        ]

        @pl.when(upper == 1)
        def _():
            for c in far[0] + far[1]:
                c.start()

    for j, (dst, dst_row) in enumerate(((qs, 0), (ks, base), (vs, base))):
        wait_all(weights[j])
        for s in range(2):
            if j == 0:
                wait_all(near[s])
            project(xs[s, base:base + 512, :], ws[j], s, dst, dst_row)
    if not with_low:
        extra = [pltpu.make_async_copy(qs, aux[0], sem.at[8])] + [
            pltpu.make_async_copy(xs.at[s, pl.ds(own_row, 256), :], aux[1].at[:, pl.ds(s * 2048, 2048)], sem.at[9 + s])
            for s in range(2)
        ]
        for c in extra:
            c.start()

    if with_low:
        @pl.when(upper == 1)
        def _():
            for s in range(2):
                wait_all(far[s])
                project(xs[s, 0:512, :], ws[1], s, ks, 0)
                project(xs[s, 0:512, :], ws[2], s, vs, 0)

    later = lax.broadcasted_iota(jnp.int32, (256, 256), 1) > lax.broadcasted_iota(jnp.int32, (256, 256), 0)
    lane = lax.broadcasted_iota(jnp.int32, (256, 128), 1)

    def attend(first):
        back = []
        for s in range(2):
            for blk in range(2):
                tile = core if blk == 0 else 1 - core
                st = jnp.zeros((256, 128), F32)
                for h in range(4):
                    i = s * 4 + h
                    q = qs[i, blk * 256:(blk + 1) * 256, :]
                    diag = base + blk * 256
                    sd = jnp.where(later, MASKED, dot_t(q, ks[i, diag:diag + 256, :]))
                    top = jnp.max(sd, axis=-1, keepdims=True)
                    if diag > first:
                        se = dot_t(q, ks[i, first:diag, :])
                        top = jnp.maximum(top, jnp.max(se, axis=-1, keepdims=True))
                    pd = jnp.exp2((sd - top) * EXP_SCALE)
                    part = dot(pd.astype(BF16), vs[i, diag:diag + 256, :])
                    if diag > first:
                        pe = jnp.exp2((se - top) * EXP_SCALE)
                        part += dot(pe.astype(BF16), vs[i, first:diag, :])
                    acc[blk, s, :, h * 128:(h + 1) * 128] = part[:, 0:128]
                    st = jnp.where(lane == h, top, st)
                    st = jnp.where(lane == 12 + h, part[:, 128:256], st)
                st_all[blk, s, :, :] = st
                n = 4 * s + 2 * blk
                back.append(pltpu.make_async_copy(acc.at[blk, s], num.at[tile, s], sem.at[11 + n]))
                back.append(pltpu.make_async_copy(st_all.at[blk, s], stats.at[tile, s], sem.at[12 + n]))
                back[-2].start()
                back[-1].start()
        wait_all(back)

    if with_low:
        @pl.when(upper == 0)
        def _():
            attend(512)

        @pl.when(upper == 1)
        def _():
            attend(0)
    else:
        attend(0)
        wait_all(extra)


ROW_SHAPES = (
    jax.ShapeDtypeStruct((2, 2, 256, 512), F32),
    jax.ShapeDtypeStruct((2, 2, 256, 128), F32),
)


def near_kernel(nw, where, own, oth, *refs):
    num, stats, q_out, own_out = refs[-12:-8]
    row_kernel(nw, where, own, oth, *refs[:-12], num, stats, (q_out, own_out), *refs[-8:])


def near_part(where, own, oth, w, *after):
    return pl.pallas_call(
        functools.partial(near_kernel, len(w)),
        out_shape=ROW_SHAPES
        + (jax.ShapeDtypeStruct((8, 512, 128), BF16), jax.ShapeDtypeStruct((256, 4096), BF16)),
        in_specs=[SMEM_SPEC] + [HBM_SPEC] * (2 + len(w) + len(after)),
        out_specs=(ANY_SPEC,) * 4,
        scratch_shapes=[
            pltpu.VMEM((2, 512, 2048), BF16),
            pltpu.VMEM((3, 2048, 512), BF16),
            pltpu.VMEM((8, 512, 128), BF16),
            pltpu.VMEM((8, 512, 128), BF16),
            pltpu.VMEM((8, 512, 256), BF16),
            pltpu.VMEM((2, 2, 256, 512), F32),
            pltpu.VMEM((2, 2, 256, 128), F32),
            pltpu.SemaphoreType.DMA((19,)),
        ],
        cost_estimate=cost(6),
        compiler_params=pltpu.CompilerParams(vmem_limit_bytes=VMEM_LIMIT),
        name="near_part",
    )(where, own, oth, *w, *after)


def full_kernel(nw, where, own, oth, *refs):
    num, stats = refs[-10:-8]
    row_kernel(nw, where, own, oth, *refs[:-10], num, stats, None, *refs[-8:])


def row_part(where, own, oth, low_own, low_oth, w, *after):
    return pl.pallas_call(
        functools.partial(full_kernel, len(w)),
        out_shape=ROW_SHAPES,
        in_specs=[SMEM_SPEC] + [HBM_SPEC] * (7 + len(w) + len(after)),
        out_specs=(ANY_SPEC, ANY_SPEC),
        scratch_shapes=[
            pltpu.VMEM((2, 1024, 2048), BF16),
            pltpu.VMEM((3, 2048, 512), BF16),
            pltpu.VMEM((8, 512, 128), BF16),
            pltpu.VMEM((8, 1024, 128), BF16),
            pltpu.VMEM((8, 1024, 256), BF16),
            pltpu.VMEM((2, 2, 256, 512), F32),
            pltpu.VMEM((2, 2, 256, 128), F32),
            pltpu.SemaphoreType.DMA((19,)),
        ],
        cost_estimate=cost(3),
        compiler_params=pltpu.CompilerParams(vmem_limit_bytes=VMEM_LIMIT),
        name="row_part",
    )(where, own, oth, *w, low_own, *low_oth, *after)


def far_kernel(where, low_own, *refs):
    low_oth, (w, q, num_in, stats_in), refs = refs[:4], refs[4:8], refs[8:]
    num, stats, xs, ws, qs, ks, vs, acc, st_all, sem = refs[-10:]
    upper, core = where[0], where[1]
    own_row = pl.multiple_of(core * 256, 256)
    oth_row = pl.multiple_of((1 - core) * 256, 256)

    @pl.when(upper == 1)
    def _():
        far = [
            [load_piece(low_own, s, xs, own_row, sem.at[2 * s])]
            + load_parts(low_oth, s, xs, oth_row, sem.at[1 + 2 * s])
            for s in range(2)
        ]
        weights = [pltpu.make_async_copy(w.at[j], ws.at[j - 1], sem.at[3 + j]) for j in (1, 2)]
        rest = [
            pltpu.make_async_copy(q, qs, sem.at[6]),
            pltpu.make_async_copy(num_in, acc, sem.at[7]),
            pltpu.make_async_copy(stats_in, st_all, sem.at[8]),
        ]
        for c in far[0] + weights[:1] + far[1] + weights[1:] + rest:
            c.start()
        vs[:, :, 128:256] = jnp.ones((8, 512, 128), BF16)
        for j, dst in enumerate((ks, vs)):
            weights[j].wait()
            for s in range(2):
                if j == 0:
                    wait_all(far[s])
                project(xs[s], ws[j], s, dst, 0)
        wait_all(rest)
        lane = lax.broadcasted_iota(jnp.int32, (256, 128), 1)
        back = []
        for s in range(2):
            for blk in range(2):
                tile = core if blk == 0 else 1 - core
                st = st_all[tile, s, :, :]
                new = st
                for h in range(4):
                    i = s * 4 + h
                    f = slice(h * 128, (h + 1) * 128)
                    scores = dot_t(qs[i, blk * 256:(blk + 1) * 256, :], ks[i])
                    near_top = st[:, h:h + 1]
                    top = jnp.maximum(near_top, jnp.max(scores, axis=-1, keepdims=True))
                    p = jnp.exp2((scores - top) * EXP_SCALE)
                    factor = jnp.exp2((near_top - top) * EXP_SCALE)
                    part = dot(p.astype(BF16), vs[i])
                    acc[tile, s, :, f] = acc[tile, s, :, f] * factor + part[:, 0:128]
                    new = jnp.where(lane == h, top, new)
                    new = jnp.where(lane == 12 + h, st * factor + part[:, 128:256], new)
                st_all[tile, s, :, :] = new
                n = 4 * s + 2 * blk
                back.append(pltpu.make_async_copy(acc.at[tile, s], num.at[tile, s], sem.at[9 + n]))
                back.append(pltpu.make_async_copy(st_all.at[tile, s], stats.at[tile, s], sem.at[10 + n]))
                back[-2].start()
                back[-1].start()
        wait_all(back)


def far_part(where, low_own, low_oth, w, q, num, stats, *after):
    return pl.pallas_call(
        far_kernel,
        out_shape=ROW_SHAPES,
        in_specs=[SMEM_SPEC] + [HBM_SPEC] * (9 + len(after)),
        out_specs=(ANY_SPEC, ANY_SPEC),
        scratch_shapes=[
            pltpu.VMEM((2, 512, 2048), BF16),
            pltpu.VMEM((2, 2048, 512), BF16),
            pltpu.VMEM((8, 512, 128), BF16),
            pltpu.VMEM((8, 512, 128), BF16),
            pltpu.VMEM((8, 512, 256), BF16),
            pltpu.VMEM((2, 2, 256, 512), F32),
            pltpu.VMEM((2, 2, 256, 128), F32),
            pltpu.SemaphoreType.DMA((17,)),
        ],
        input_output_aliases={8: 0, 9: 1},
        cost_estimate=cost(4),
        compiler_params=pltpu.CompilerParams(vmem_limit_bytes=VMEM_LIMIT),
        name="far_part",
    )(where, low_own, *low_oth, w, q, num, stats, *after)


def merge_tile(num, stats, col, out):
    both = col[:, :, 512:640].astype(F32)
    for s in range(2):
        st = stats[s, :, :]
        terms = both[:, s * 8:(s + 1) * 8, :].reshape(256, 128)
        cst = (terms + pltpu.roll(terms, 124, 1)) + pltpu.roll(terms, 120, 1)
        top = jnp.maximum(st, cst)
        row_factor = pltpu.roll(jnp.exp2((st - top) * EXP_SCALE), 12, 1)
        col_factor = pltpu.roll(jnp.exp2((cst - top) * EXP_SCALE), 12, 1)
        inverse = 1.0 / (st * row_factor + cst * col_factor)
        row_factor = row_factor * inverse
        col_factor = col_factor * inverse
        for h in range(4):
            f = slice(h * 128, (h + 1) * 128)
            cnum = col[:, :, f].astype(F32)[:, s * 8:(s + 1) * 8, :].reshape(256, 128)
            value = num[s, :, f] * row_factor[:, 12 + h:13 + h] + cnum * col_factor[:, 12 + h:13 + h]
            out[s, :, f] = value.astype(BF16)


def merge_kernel(parts, tiles, n_after, num_in, stats_in, col_in, *refs):
    if parts:
        side, refs, held = refs[0], refs[1:-1], refs[-1]
    refs = refs[n_after:]
    outs, sides, (num, stats, col, done, sem) = refs[:len(tiles)], refs[len(tiles):-5], refs[-5:]
    def halves(tile):
        return pl.ds(tile * 16, 16)

    into = {
        tile: [pltpu.make_async_copy(col_in.at[:, halves(tile), :], col.at[:, halves(tile), :], sem.at[tile])]
        + [pltpu.make_async_copy(num_in.at[tile, s], num.at[tile, s], sem.at[2 + 2 * tile + s]) for s in range(2)]
        + [pltpu.make_async_copy(stats_in.at[tile, s], stats.at[tile, s], sem.at[2 + 2 * tile + s]) for s in range(2)]
        for tile in tiles
    }
    for tile in tiles:
        for c in into[tile]:
            c.start()
    if parts:
        side_in = pltpu.make_async_copy(side, held, sem.at[8])
        side_in.start()
    back = []
    for tile, out in zip(tiles, outs):
        wait_all(into[tile])
        merge_tile(num.at[tile], stats.at[tile], col.at[:, halves(tile), :], done.at[tile])
        back.append(pltpu.make_async_copy(done.at[tile], out, sem.at[6 + tile]))
        back[-1].start()
    if parts:
        side_in.wait()
        n = side.shape[0] // parts
        for i, to in enumerate(sides):
            back.append(pltpu.make_async_copy(held.at[pl.ds(i * n, n)], to, sem.at[9]))
            back[-1].start()
    wait_all(back)


def merge(num, stats, col, tiles, side=(), parts=0, after=()):
    shape = jax.ShapeDtypeStruct((2, 256, 512), BF16)
    side_shape = [jax.ShapeDtypeStruct((a.shape[0] // parts, a.shape[1]), a.dtype) for a in side] * parts
    return pl.pallas_call(
        functools.partial(merge_kernel, parts, tiles, len(after)),
        out_shape=(shape,) * len(tiles) + (*side_shape,),
        in_specs=[HBM_SPEC] * (3 + len(side) + len(after)),
        out_specs=(ANY_SPEC,) * (len(tiles) + parts),
        scratch_shapes=[
            pltpu.VMEM((2, 2, 256, 512), F32),
            pltpu.VMEM((2, 2, 256, 128), F32),
            pltpu.VMEM((32, 32, 640), BF16),
            pltpu.VMEM((2, 2, 256, 512), BF16),
            pltpu.SemaphoreType.DMA((10,)),
        ]
        + [pltpu.VMEM(a.shape, a.dtype) for a in side],
        cost_estimate=cost(2),
        compiler_params=pltpu.CompilerParams(vmem_limit_bytes=VMEM_LIMIT),
        name="merge",
    )(num, stats, col, *side, *after)


def out_kernel(own_a, recv_a, recv_b, num_in, stats_in, col_in, *refs):
    weights, (out, att, ws, acc, sent, num, stats, col, sem) = refs[:7], refs[7:]
    copies = [
        [pltpu.make_async_copy(own_a, att.at[0], sem.at[0])],
        [pltpu.make_async_copy(recv_a, att.at[1], sem.at[2])],
        [pltpu.make_async_copy(num_in.at[0], num, sem.at[4]),
         pltpu.make_async_copy(stats_in.at[0], stats, sem.at[10]),
         pltpu.make_async_copy(col_in.at[:, pl.ds(0, 16), :], col, sem.at[11])],
        [pltpu.make_async_copy(recv_b, att.at[3], sem.at[6])],
    ]
    for i in range(3):
        copies[i].append(pltpu.make_async_copy(weights[i], ws.at[i], sem.at[2 * i + 1]))
    for i, part in enumerate(weights[3:]):
        copies[3].append(pltpu.make_async_copy(part, ws.at[3, pl.ds(i * 128, 128), :], sem.at[7]))
    for c in copies[0] + copies[2][:3] + copies[1] + copies[2][3:] + copies[3]:
        c.start()
    for i in range(3):
        wait_all(copies[i])
        if i == 2:
            merge_tile(num, stats, col, att.at[2])
        part = dot(att[i].reshape(512, 512), ws[i])
        acc[...] = part if i == 0 else acc[...] + part
    wait_all(copies[3])
    back = []
    for s in range(2):
        f = pl.ds(s * 2048, 2048)
        sent[:, f] = (acc[s * 256:(s + 1) * 256, :] + dot(att[3, s], ws[3])).astype(BF16)
        back.append(pltpu.make_async_copy(sent.at[:, f], out.at[:, f], sem.at[8 + s]))
        back[s].start()
    wait_all(back)


def output_part(own_a, recv_a, recv_b, num, stats, col, weights):
    return pl.pallas_call(
        out_kernel,
        out_shape=jax.ShapeDtypeStruct((256, 4096), BF16),
        in_specs=[ANY_SPEC] * 13,
        out_specs=ANY_SPEC,
        scratch_shapes=[
            pltpu.VMEM((4, 2, 256, 512), BF16),
            pltpu.VMEM((4, 512, 2048), BF16),
            pltpu.VMEM((512, 2048), F32),
            pltpu.VMEM((256, 4096), BF16),
            pltpu.VMEM((2, 256, 512), F32),
            pltpu.VMEM((2, 256, 128), F32),
            pltpu.VMEM((32, 16, 640), BF16),
            pltpu.SemaphoreType.DMA((12,)),
        ],
        cost_estimate=cost(4),
        compiler_params=pltpu.CompilerParams(vmem_limit_bytes=VMEM_LIMIT),
        name="output_part",
    )(own_a, recv_a, recv_b, num, stats, col, *weights)


def gate_kernel(*refs):
    pass


def gate(a, *after):
    return pl.pallas_call(
        gate_kernel,
        out_shape=jax.ShapeDtypeStruct(a.shape, a.dtype),
        in_specs=[ANY_SPEC] * (1 + len(after)),
        out_specs=ANY_SPEC,
        input_output_aliases={0: 0},
        name="gate",
    )(a, *after)


def core_swap(a):
    return lax.ppermute(a, "sp", CORE_PAIRS)


def core_swap_parts(a, parts=4):
    return [core_swap(part) for part in jnp.split(a, parts, axis=0)]


def to_segments(a):
    return lax.all_to_all(a, "seg", split_axis=0, concat_axis=0, tiled=True)


def from_neighbour(a):
    return lax.ppermute(a, ("seg", "sp"), NEIGHBOUR_PAIRS)


def ring_near(quarter, axis):
    return (
        lax.ppermute(quarter, "seg", MOVES[axis, -1]),
        lax.ppermute(quarter, "seg", MOVES[axis, 1]),
    )


def cut_kernel(*refs):
    n = (len(refs) - 3) // 2
    srcs, dsts, held, sem = refs[:n], refs[n + 1:2 * n + 1], refs[-2], refs[-1]
    load = [
        pltpu.make_async_copy(src.at[:, pl.ds(128 * (i % 2), 128), :], held.at[i], sem.at[i])
        for i, src in enumerate(srcs)
    ]
    store = [pltpu.make_async_copy(held.at[i], dst, sem.at[n + i]) for i, dst in enumerate(dsts)]
    for c in load:
        c.start()
    for i in range(n):
        load[i].wait()
        store[i].start()
    wait_all(store)


def cut(pieces, after):
    n = len(pieces)
    half = jax.ShapeDtypeStruct((3, 128, 512), BF16)
    return pl.pallas_call(
        cut_kernel,
        out_shape=(half,) * n,
        in_specs=[ANY_SPEC] * (n + 1),
        out_specs=(ANY_SPEC,) * n,
        scratch_shapes=[pltpu.VMEM((n, 3, 128, 512), BF16), pltpu.SemaphoreType.DMA((2 * n,))],
        cost_estimate=cost(0.5),
        compiler_params=pltpu.CompilerParams(vmem_limit_bytes=VMEM_LIMIT),
        name="cut",
    )(*pieces, after)


def ring_far(nxt, prev, axis):
    return (
        lax.ppermute(nxt, "seg", MOVES[axis, -1]),
        lax.ppermute(prev, "seg", MOVES[axis, 1]),
    )


def join_kernel(where, z_mine, z_pair, y_mine, y_pair, after, by_z, by_y, held, sem):
    load, store = [], []
    for i, (src, dst, own) in enumerate(
        ((z_mine, by_z, where[3]), (z_pair, by_z, 1 - where[3]), (y_mine, by_y, where[2]), (y_pair, by_y, 1 - where[2]))
    ):
        row = pl.multiple_of(lax.rem(own + 2, 2) * 128, 128)
        load.append(pltpu.make_async_copy(src, held.at[i], sem.at[i]))
        store.append(pltpu.make_async_copy(held.at[i], dst.at[:, pl.ds(row, 128), :], sem.at[4 + i]))
    for c in load:
        c.start()
    for i in range(4):
        load[i].wait()
        store[i].start()
    wait_all(store)


def other_quarters(w_qkv, where, z, y, after):
    def eighth(row):
        return from_neighbour(lax.dynamic_slice(w_qkv, (0, row, 0), (3, 128, 512)))

    z_mine, y_mine = eighth(z * 256 + y % 2 * 128), eighth(1024 + y * 256 + z % 2 * 128)
    z_pair, y_pair = lax.ppermute(z_mine, "seg", PAIRS["y"]), lax.ppermute(y_mine, "seg", PAIRS["z"])
    return pl.pallas_call(
        join_kernel,
        out_shape=(jax.ShapeDtypeStruct((3, 256, 512), BF16),) * 2,
        in_specs=[SMEM_SPEC] + [ANY_SPEC] * 5,
        out_specs=(ANY_SPEC,) * 2,
        scratch_shapes=[pltpu.VMEM((4, 3, 128, 512), BF16), pltpu.SemaphoreType.DMA((8,))],
        cost_estimate=cost(0.5),
        compiler_params=pltpu.CompilerParams(vmem_limit_bytes=VMEM_LIMIT),
        name="join",
    )(where, z_mine, z_pair, y_mine, y_pair, after)


def split_kernel(src, *refs):
    parts, (held, sem) = refs[-6:-2], refs[-2:]
    n = held.shape[0] // 4
    load = [pltpu.make_async_copy(src.at[pl.ds(i * n, n)], held.at[pl.ds(i * n, n)], sem.at[i]) for i in range(4)]
    store = [pltpu.make_async_copy(held.at[pl.ds(i * n, n)], to, sem.at[4 + i]) for i, to in enumerate(parts)]
    for c in load:
        c.start()
    for i in range(4):
        load[i].wait()
        store[i].start()
    wait_all(store)


def split_rows(a, *after):
    return pl.pallas_call(
        split_kernel,
        out_shape=(jax.ShapeDtypeStruct((a.shape[0] // 4, a.shape[1]), a.dtype),) * 4,
        in_specs=[ANY_SPEC] * (1 + len(after)),
        out_specs=(ANY_SPEC,) * 4,
        scratch_shapes=[pltpu.VMEM(a.shape, a.dtype), pltpu.SemaphoreType.DMA((8,))],
        cost_estimate=cost(0.5),
        compiler_params=pltpu.CompilerParams(vmem_limit_bytes=VMEM_LIMIT),
        name="split_rows",
    )(a, *after)


def shards(normed, w_qkv, w_out):
    seg, sp = lax.axis_index("seg"), lax.axis_index("sp")
    z, y = seg // (NXL * NY), seg % NY
    where = jnp.stack([sp // 2, sp % 2, z, y]).astype(jnp.int32)
    row_oth = core_swap(normed)
    num_own, stats_own, q_own, own_copy = near_part(where, normed, row_oth, [w_qkv])
    by_z, by_y = other_quarters(w_qkv, where, z, y, q_own)
    low_own = lax.ppermute(own_copy, "sp", LOWER_TO_UPPER)
    z_near, y_near = ring_near(by_z, "z"), ring_near(by_y, "y")
    by_offset = normed.reshape(32, 8, 2, 2048).transpose(0, 2, 1, 3).reshape(32, 16, 2048)
    col_own = gate(to_segments(by_offset).reshape(512, 2048), q_own)
    col_oth = core_swap_parts(col_own)
    col, out_copy = column_part(where, col_own, col_oth, [w_qkv], w_out, 1)
    halves = cut((*z_near, *y_near), col)
    z_far, y_far = ring_far(*halves[:2], "z"), ring_far(*halves[2:], "y")
    qkv_other = [by_z, *z_near, *z_far, by_y, *y_near, *y_far]
    low_oth_parts = split_rows(low_own, halves[0])
    low_oth = [core_swap(part) for part in low_oth_parts]
    num_own, stats_own = far_part(where, low_own, low_oth, w_qkv, q_own, num_own, stats_own)
    out_other = from_neighbour(gate(out_copy, low_oth_parts[0]))
    col_a = to_segments(gate(col, *z_far, *y_far, num_own))
    col, _ = column_part(where, col_own, col_oth, qkv_other, where.reshape(1, 4), 1, num_own)
    col_b = to_segments(col)
    oth_a, own_a, *out_parts = merge(num_own, stats_own, col_a, (1, 0), (out_other,), 4, (col,))
    recv_a = core_swap(oth_a)
    swapped = [core_swap(part) for part in out_parts]
    num, stats = row_part(where, normed, row_oth, low_own, low_oth, qkv_other, own_a)
    (oth_b,) = merge(num, stats, col_b, (1,), after=(recv_a, *swapped))
    recv_b = core_swap(oth_b)
    out_weights = (w_out, core_swap(w_out), out_other, *swapped)
    return output_part(own_a, recv_a, recv_b, num, stats, col_b, out_weights)


def solution(mesh):
    in_specs = (P("sp", "seg"), P(None, None, "sp"), P("sp", None))
    return jax.shard_map(shards, mesh=mesh, in_specs=in_specs, out_specs=P("sp", "seg"), check_vma=False)
```
